32 devices in a mesh: dp: 16 (over z, y, x), section: 2 (over core).
Axes of the slice: x: 2, y: 2, z: 4, core: 2. Of those that a mesh axis runs over, the one named last changes fastest.
Arguments:
- tokens: bfloat16 [32, 1024, 1024], P('dp'), may hold values from -6 to 6
- seq_length: int32 [32], P('dp'), may hold values from 256 to 1024, as said below
- cotangent: bfloat16 [32, 1024, 1024], P('dp'), may hold values from -6 to 6
- ln_gain: bfloat16 [2, 2, 1024], P('section'), may hold values from 0.25 to 1.75
- ln_bias: bfloat16 [2, 2, 1024], P('section'), may hold values from -1.796875 to 1.796875
- w_qkv: bfloat16 [2, 1024, 3072], P('section', 'dp'), may hold values from -0.1875 to 0.1875
- w_out: bfloat16 [2, 1024, 1024], P('section', 'dp'), may hold values from -2 to 2
- w_fc: bfloat16 [2, 1024, 4096], P('section', 'dp'), may hold values from -0.1875 to 0.1875
- w_proj: bfloat16 [2, 4096, 1024], P('section', 'dp'), may hold values from -0.09375 to 0.09375
- prefix_table: bfloat16 [10, 1024], replicated, may hold values from -6 to 6
- reparam_w1: bfloat16 [1024, 512], replicated, may hold values from -0.1875 to 0.1875
- reparam_b1: bfloat16 [512], replicated, may hold values from -3 to 3
- reparam_w2: bfloat16 [2, 512, 2048], P('section'), may hold values from -0.25 to 0.25
- reparam_b2: bfloat16 [2, 2048], P('section'), may hold values from -3 to 3
Outputs:
- activations: bfloat16 [2, 32, 1024, 1024], P('section', 'dp')
- input_grads: bfloat16 [2, 32, 1024, 1024], P('section', 'dp')
- grad_table: float32 [10, 1024], replicated
- grad_w1: float32 [1024, 512], replicated
- grad_b1: float32 [512], replicated
- grad_w2: float32 [2, 512, 2048], P('section')
- grad_b2: float32 [2, 2048], P('section')
The draws below stay inside these ranges and needn't reach their ends.
Inputs may be any that keep to these rules, and one draw needn't show every extreme that they name: `seq_length`: each row holds either one sequence of 1024 positions or four sequences of 256; both kinds occur in every draw.
All inputs are finite; a program needn't handle non-finite values.
Results may differ from the reference program's by a relative error of at most 0.015.
Values may be sent and summed in bfloat16 or wider, within the bound.
No kernel may reach another device: no remote copies, remote signals or barrier semaphores. Data moves between devices by JAX's collectives and lax.ppermute only.
A program may use at most 320 MiB of HBM per device.

```python
import jax
import jax.numpy as jnp
from jax import lax

D = 1024
HEADS = 16
HEAD_DIM = 64
FF = 4096
PREFIX = 10
RH = 512
ROW_LEN = 1024
SHORT = 256
SECTIONS = 2
ROWS = 32


def draw_seq_length(key, part):
    key = jax.random.fold_in(key, 7)
    kind_key, spot_key = jax.random.split(key)
    row_kinds = jax.random.randint(kind_key, (ROWS,), 0, 2)
    long_spot = jax.random.randint(spot_key, (), 0, ROWS)
    row_ids = jnp.arange(ROWS)
    row_kinds = jnp.where(row_ids == long_spot, 1, row_kinds)
    row_kinds = jnp.where(row_ids == (long_spot + 1) % ROWS, 0, row_kinds)
    return jnp.where(row_kinds == 1, ROW_LEN, SHORT).astype(jnp.int32)


def shard_levels(stream_key, dims, cuts, low, top_value):
    loudness = 1.0
    for dim, shards_of in cuts:
        draws = jax.random.uniform(jax.random.fold_in(jax.random.fold_in(stream_key, 6), dim), (shards_of,), jnp.float32, low / len(cuts), top_value / len(cuts))
        loudness = loudness * jnp.repeat(jnp.exp(draws), dims[dim] // shards_of).reshape((-1,) + (1,) * (len(dims) - 1 - dim))
    return loudness


def centred(stream_key, extent, scale, most, cuts=(), held_as=jnp.bfloat16):
    drawn = jax.random.normal(stream_key, extent, jnp.float32) * scale
    if len(cuts) > 0:
        drawn = shard_levels(stream_key, extent, cuts, -0.22, 0.18) * drawn
    return jnp.clip(drawn, min=-most, max=most).astype(held_as)


def setup_inputs(seed: int = 0) -> dict:
    streams_of = jax.random.split(jax.random.key(seed), 15)
    return {
        "tokens": centred(streams_of[0], (ROWS, ROW_LEN, D), 1.0, 6.0, ((0, 16),)),
        "seq_length": draw_seq_length(jax.random.fold_in(streams_of[14], 71), 0),
        "cotangent": centred(streams_of[2], (ROWS, ROW_LEN, D), 1.0, 6.0, ((0, 16),)),
        "ln_gain": jnp.clip(1.0 + 0.15 * jax.random.normal(streams_of[3], (SECTIONS, 2, D), jnp.float32), 0.25, 1.75).astype(jnp.bfloat16),
        "ln_bias": centred(streams_of[4], (SECTIONS, 2, D), 0.3, 1.796875, ((0, 2),)),
        "w_qkv": centred(streams_of[5], (SECTIONS, D, 3 * D), D ** -0.5, 0.1875, ((0, 2), (1, 16))),
        "w_out": centred(streams_of[6], (SECTIONS, D, D), (max(1, D * 8 // ROW_LEN)) ** -0.5, 2.0, ((0, 2), (1, 16))),
        "w_fc": centred(streams_of[7], (SECTIONS, D, FF), D ** -0.5, 0.1875, ((0, 2), (1, 16))),
        "w_proj": centred(streams_of[8], (SECTIONS, FF, D), FF ** -0.5, 0.09375, ((0, 2), (1, 16))),
        "prefix_table": centred(streams_of[9], (PREFIX, D), 1.0, 6.0),
        "reparam_w1": centred(streams_of[10], (D, RH), D ** -0.5, 0.1875),
        "reparam_b1": centred(streams_of[11], (RH,), 0.5, 3.0),
        "reparam_w2": centred(streams_of[12], (SECTIONS, RH, 2 * D), RH ** -0.5, 0.25, ((0, 2),)),
        "reparam_b2": centred(streams_of[13], (SECTIONS, 2 * D), 0.5, 3.0, ((0, 2),)),
    }


@jax.custom_vjp
def low(v):
    return lax.optimization_barrier(v.astype(jnp.bfloat16)).astype(jnp.float32)

@jax.custom_vjp
def low_back(v):
    return v

def low_keep(v):
    return (low(v), None)

def low_pass(kept, grad):
    return (grad,)

def back_keep(v):
    return (v, None)

def back_low(kept, grad):
    return (low(grad),)
low.defvjp(low_keep, low_pass)
low_back.defvjp(back_keep, back_low)
eps_norm = 1e-05
neg_big = -1e+30
highest_mode = lax.Precision.HIGHEST

def layer_norm(values, gain, offset):
    centre = lax.optimization_barrier(jnp.mean(values, axis=-1, keepdims=True))
    spread = values - centre
    variance = lax.optimization_barrier(jnp.mean(spread * spread, axis=-1, keepdims=True))
    return spread * lax.rsqrt(variance + eps_norm) * gain + offset

def matmul_high(left, right):
    return jnp.dot(left, right, precision=highest_mode)

def split_heads(matrix):
    return matrix.reshape(matrix.shape[0], HEADS, HEAD_DIM)

def attention(projected, prefix_kv, segment):
    length = projected.shape[0]
    queries = split_heads(projected[:, :D])
    key_rows = split_heads(jnp.concatenate([prefix_kv[:, :D], projected[:, D:2 * D]], axis=0))
    value_rows = split_heads(jnp.concatenate([prefix_kv[:, D:], projected[:, 2 * D:]], axis=0))
    raw_scores = low_back(jnp.einsum('qhd,khd->hqk', queries, key_rows, precision=highest_mode))
    positions = jnp.arange(length, dtype=jnp.int32)
    causal = (positions[None, :] <= positions[:, None]) & (segment[None, :] == segment[:, None])
    allowed = jnp.concatenate([jnp.ones((length, PREFIX), dtype=bool), causal], axis=1)
    scores = jnp.where(allowed[None], raw_scores * HEAD_DIM ** (-0.5), neg_big)
    row_max = lax.optimization_barrier(jnp.max(scores, axis=-1, keepdims=True))
    exp_scores = jnp.exp(scores - row_max)
    probabilities = exp_scores / lax.optimization_barrier(jnp.sum(exp_scores, axis=-1, keepdims=True))
    attended = jnp.einsum('hqk,khd->qhd', low(probabilities), value_rows, precision=highest_mode)
    return attended.reshape(length, D)

def layer(hidden_in, segment, weights, prefix_kv):
    gain_pair, offset_pair, w_qkv, w_out, w_fc, w_proj = weights
    normed = low(layer_norm(hidden_in, gain_pair[0], offset_pair[0]))
    projected = low(low_back(matmul_high(normed, w_qkv)))
    attended = low(low_back(attention(projected, prefix_kv, segment)))
    middle = hidden_in + low_back(matmul_high(attended, w_out))
    normed_two = low(layer_norm(middle, gain_pair[1], offset_pair[1]))
    inner_act = low_back(matmul_high(normed_two, w_fc))
    activated = low(jax.nn.gelu(inner_act, approximate=True))
    return middle + low_back(matmul_high(activated, w_proj))

def prefix_states(table, w_first, b_first, w_second, b_second):
    hidden_units = jnp.tanh(matmul_high(table, w_first) + b_first)
    return [low(matmul_high(hidden_units, w_second[section_index]) + b_second[section_index]) for section_index in range(2)]

def reference(tokens, seq_length, cotangent, ln_gain, ln_bias, w_qkv, w_out, w_fc, w_proj, prefix_table, reparam_w1, reparam_b1, reparam_w2, reparam_b2):
    layer_weights = [tuple((source_array[section_index].astype(jnp.float32) for source_array in (ln_gain, ln_bias, w_qkv, w_out, w_fc, w_proj))) for section_index in range(2)]
    positions = jnp.arange(ROW_LEN, dtype=jnp.int32)

    def forward(inputs, shift_in, table, w_first, b_first, w_second, b_second):
        prefix_kv = prefix_states(table, w_first, b_first, w_second, b_second)

        def one_row(row_pack):
            row_in, row_shift, row_length = row_pack
            segment = positions // row_length
            first_out = layer(row_in, segment, layer_weights[0], prefix_kv[0])
            handed = low(low_back(first_out + row_shift))
            return (handed, layer(handed, segment, layer_weights[1], prefix_kv[1]))
        return lax.map(jax.checkpoint(one_row), (inputs, shift_in, seq_length))
    primals = (tokens.astype(jnp.float32), jnp.zeros(tokens.shape, jnp.float32), prefix_table.astype(jnp.float32), reparam_w1.astype(jnp.float32), reparam_b1.astype(jnp.float32), reparam_w2.astype(jnp.float32), reparam_b2.astype(jnp.float32))
    (handed, final_out), pullback = jax.vjp(forward, *primals)
    gradients = pullback((jnp.zeros_like(handed), cotangent.astype(jnp.float32)))
    grad_tokens, grad_shift, grad_table, grad_w1, grad_b1, grad_w2, grad_b2 = gradients
    activations = jnp.stack([handed, final_out]).astype(jnp.bfloat16)
    input_grads = jnp.stack([grad_tokens, grad_shift]).astype(jnp.bfloat16)
    return (activations, input_grads, grad_table, grad_w1, grad_b1, grad_w2, grad_b2)
```

```python
import functools

import jax
import jax.numpy as jnp
from jax import lax
from jax.experimental import pallas as pl
from jax.experimental.pallas import tpu as pltpu
from jax.sharding import PartitionSpec as P

D = 1024
HEADS = 16
HEAD_DIM = 64
FF = 4096
PREFIX = 10
SLOTS = 16
PAIRS = 8
PAIR_DIM = 128
BLOCK = 256

eps_norm = 1e-05
neg_big = -1e30
highest_mode = lax.Precision.HIGHEST
VMEM_BYTES = 62 * 2**20
F32 = jnp.float32
BF16 = jnp.bfloat16


def dot(left, right, dims):
    return lax.dot_general(left, right, (dims, ((), ())), preferred_element_type=F32)


def dot_nn(left, right):
    return dot(left, right, ((1,), (0,)))


def dot_nt(left, right):
    return dot(left, right, ((1,), (1,)))


def dot_tn(left, right):
    return dot(left, right, ((0,), (0,)))


def normalised(values):
    centre = jnp.mean(values, axis=-1, keepdims=True)
    spread = values - centre
    variance = jnp.mean(spread * spread, axis=-1, keepdims=True)
    inverse = lax.rsqrt(variance + eps_norm)
    return spread * inverse, inverse


def layer_norm(values, gain, offset):
    return normalised(values)[0] * gain + offset


def norm_back(values, gain, upstream):
    unit, inverse = normalised(values)
    scaled = upstream * gain
    mean_scaled = jnp.mean(scaled, axis=-1, keepdims=True)
    mean_unit = jnp.mean(scaled * unit, axis=-1, keepdims=True)
    return (scaled - mean_scaled - unit * mean_unit) * inverse


SQRT_2_PI = 0.7978845608028654
CUBIC = 0.044715


def gelu_pair(values):
    cubic_part = (SQRT_2_PI * CUBIC) * (values * values)
    half_tanh = 0.5 + 0.5 * jnp.tanh(values * (SQRT_2_PI + cubic_part))
    out = values * half_tanh
    slope = half_tanh + out * ((2.0 - 2.0 * half_tanh) * (SQRT_2_PI + 3.0 * cubic_part))
    return out, slope


def matrix_of(ref):
    block = ref[...]
    return block.reshape(-1, block.shape[-1])


def params(**kwargs):
    return pltpu.CompilerParams(vmem_limit_bytes=VMEM_BYTES, **kwargs)


def row_tiles(length, size):
    return [slice(start, start + size) for start in range(0, length, size)]


def qkv_kernel(spot_ref, hidden_ref, norm_ref, weight_ref, out_ref, normed):
    step = pl.program_id(0)

    @pl.when(step == 0)
    def _():
        gain, offset = norm_ref[0:1], norm_ref[2:3]
        for rows in row_tiles(hidden_ref.shape[1], 256):
            values = hidden_ref[0, rows].astype(F32)
            normed[rows] = layer_norm(values, gain, offset).astype(BF16)

    scale = jnp.where(step == 0, HEAD_DIM**-0.5, 1.0)
    weight = matrix_of(weight_ref)
    for rows in row_tiles(out_ref.shape[0], 512):
        out_ref[rows] = (dot_nn(normed[rows], weight) * scale).astype(BF16)


def project(spot, hidden, norms, weights):
    length = hidden.shape[1]
    array, shape, index = weights
    return pl.pallas_call(
        qkv_kernel,
        grid_spec=pltpu.PrefetchScalarGridSpec(
            num_scalar_prefetch=1,
            grid=(3,),
            in_specs=[
                pl.BlockSpec((1, length, D), lambda j, s: (s[0], 0, 0)),
                pl.BlockSpec((8, D), lambda j, s: (0, 0)),
                pl.BlockSpec(shape, lambda j, s: index(j)),
            ],
            out_specs=pl.BlockSpec((length, D), lambda j, s: (0, j)),
            scratch_shapes=[pltpu.VMEM((length, D), BF16)],
        ),
        out_shape=jax.ShapeDtypeStruct((length, 3 * D), BF16),
        compiler_params=params(),
        name="norm_project",
    )(spot, hidden, norms, array)


def lane_halves(block):
    lanes = lax.broadcasted_iota(jnp.int32, block.shape, 1)
    zero = jnp.zeros_like(block)
    return jnp.where(lanes < HEAD_DIM, block, zero), jnp.where(lanes < HEAD_DIM, zero, block)


def masked_scores(prefix_scores, row_scores, lone):
    slots = lax.broadcasted_iota(jnp.int32, prefix_scores.shape, 0)
    prefix_scores = jnp.where(slots < PREFIX, prefix_scores, neg_big)
    diagonal = row_scores[-BLOCK:]
    keys = lax.broadcasted_iota(jnp.int32, diagonal.shape, 0)
    queries = lax.broadcasted_iota(jnp.int32, diagonal.shape, 1)
    diagonal = jnp.where(keys <= queries, diagonal, neg_big)
    if row_scores.shape[0] > BLOCK:
        row_scores = jnp.concatenate([row_scores[:-BLOCK], diagonal], axis=0)
    else:
        row_scores = diagonal
    return prefix_scores, row_scores


def strip_product(keys_ref, right, first, stop):
    if first == 0:
        whole = dot_nt(keys_ref[0 : SLOTS + stop], right)
        return whole[:SLOTS], whole[SLOTS:]
    return (
        dot_nt(keys_ref[0:SLOTS], right),
        dot_nt(keys_ref[SLOTS + first : SLOTS + stop], right),
    )


def attend_kernel(
    short_ref, q_ref, k_ref, v_ref, kp_ref, vp_ref, out_ref, log_ref, keys_a, keys_b, values_t, probs_p
):
    length = q_ref.shape[0]
    for rows, source in ((slice(0, SLOTS), kp_ref), (slice(SLOTS, SLOTS + length), k_ref)):
        keys_a[rows], keys_b[rows] = lane_halves(source[...])
    values_t[...] = v_ref[...].T
    prefix_values = jnp.concatenate(lane_halves(vp_ref[...]), axis=0)

    def run(short):
        for index in range(length // BLOCK):
            rows = slice(index * BLOCK, (index + 1) * BLOCK)
            first = rows.start if short else 0
            queries = q_ref[rows]
            parts = []
            for head, keys in enumerate((keys_a, keys_b)):
                prefix_scores, row_scores = masked_scores(
                    *strip_product(keys, queries, first, rows.stop), short
                )
                top = jnp.maximum(
                    jnp.max(row_scores, axis=0, keepdims=True),
                    jnp.max(prefix_scores, axis=0, keepdims=True),
                )
                row_exp = jnp.exp(row_scores - top)
                prefix_exp = jnp.exp(prefix_scores - top)
                total = jnp.sum(row_exp, axis=0, keepdims=True) + jnp.sum(
                    prefix_exp, axis=0, keepdims=True
                )
                log_ref[0, head : head + 1, rows] = top + jnp.log(total)
                inverse = 1.0 / total
                probs_p[head * SLOTS : (head + 1) * SLOTS, rows] = (prefix_exp * inverse).astype(BF16)
                span = slice(head * HEAD_DIM, (head + 1) * HEAD_DIM)
                parts.append(
                    dot_nn(values_t[span, first : rows.stop], row_exp.astype(BF16)) * inverse
                )
            both = jnp.concatenate(parts, axis=0) + dot_tn(prefix_values, probs_p[:, rows])
            out_ref[rows] = both.T.astype(BF16)

    is_short = short_ref[0] < length
    pl.when(is_short)(lambda: run(True))
    pl.when(jnp.logical_not(is_short))(lambda: run(False))


def pair_spec(length, part):
    return pl.BlockSpec((length, PAIR_DIM), lambda p, s: (0, part * PAIRS + p))


def attend(seq, projected, prefix_keys, prefix_values):
    length = projected.shape[0]
    return pl.pallas_call(
        attend_kernel,
        grid_spec=pltpu.PrefetchScalarGridSpec(
            num_scalar_prefetch=1,
            grid=(PAIRS,),
            in_specs=[
                pair_spec(length, 0),
                pair_spec(length, 1),
                pair_spec(length, 2),
                pair_spec(SLOTS, 0),
                pair_spec(SLOTS, 0),
            ],
            out_specs=[
                pair_spec(length, 0),
                pl.BlockSpec((1, 8, length), lambda p, s: (p, 0, 0)),
            ],
            scratch_shapes=[
                pltpu.VMEM((SLOTS + length, PAIR_DIM), BF16),
                pltpu.VMEM((SLOTS + length, PAIR_DIM), BF16),
                pltpu.VMEM((PAIR_DIM, length), BF16),
                pltpu.VMEM((2 * SLOTS, length), BF16),
            ],
        ),
        out_shape=[
            jax.ShapeDtypeStruct((length, D), BF16),
            jax.ShapeDtypeStruct((PAIRS, 8, length), F32),
        ],
        compiler_params=params(),
        name="attend",
    )(seq, projected, projected, projected, prefix_keys, prefix_values)


def attend_back_kernel(
    short_ref,
    q_ref,
    k_ref,
    v_ref,
    out_ref,
    grad_ref,
    kp_ref,
    vp_ref,
    log_ref,
    grads_ref,
    dkp_ref,
    dvp_ref,
    keys_a,
    keys_b,
    values_a,
    values_b,
    keys_t,
    dk,
    dv,
    dq_t,
    ds_p,
):
    length = q_ref.shape[0]
    for rows, source in ((slice(0, SLOTS), kp_ref), (slice(SLOTS, SLOTS + length), k_ref)):
        keys_a[rows], keys_b[rows] = lane_halves(source[...])
    for rows, source in ((slice(0, SLOTS), vp_ref), (slice(SLOTS, SLOTS + length), v_ref)):
        values_a[rows], values_b[rows] = lane_halves(source[...])
    keys_t[...] = k_ref[...].T
    prefix_keys = jnp.concatenate(lane_halves(kp_ref[...]), axis=0)
    dk[...] = jnp.zeros_like(dk)
    dv[...] = jnp.zeros_like(dv)

    def run(short):
        for index in range(length // BLOCK):
            rows = slice(index * BLOCK, (index + 1) * BLOCK)
            first = rows.start if short else 0
            queries, grads = q_ref[rows], grad_ref[rows]
            query_halves, grad_halves = lane_halves(queries), lane_halves(grads)
            weighted_t = (grads.astype(F32) * out_ref[rows].astype(F32)).T
            for head in range(2):
                keys, values = ((keys_a, values_a), (keys_b, values_b))[head]
                span = slice(head * HEAD_DIM, (head + 1) * HEAD_DIM)
                prefix_scores, row_scores = masked_scores(
                    *strip_product(keys, queries, first, rows.stop), short
                )
                log_sum = log_ref[0, head : head + 1, rows]
                row_probs = jnp.exp(row_scores - log_sum)
                prefix_probs = jnp.exp(prefix_scores - log_sum)
                centre = jnp.sum(weighted_t[span], axis=0, keepdims=True)
                prefix_dprob, row_dprob = strip_product(values, grads, first, rows.stop)
                row_ds = (row_probs * (row_dprob - centre)).astype(BF16)
                prefix_ds = (prefix_probs * (prefix_dprob - centre)).astype(BF16)
                row_probs = row_probs.astype(BF16)
                prefix_probs = prefix_probs.astype(BF16)
                ds_p[head * SLOTS : (head + 1) * SLOTS, rows] = prefix_ds
                for total, row_part, prefix_part, right in (
                    (dk, row_ds, prefix_ds, query_halves[head]),
                    (dv, row_probs, prefix_probs, grad_halves[head]),
                ):
                    if first == 0:
                        left = jnp.concatenate([prefix_part, row_part], axis=0)
                        total[0 : SLOTS + rows.stop] += dot_nn(left, right)
                    else:
                        total[0:SLOTS] += dot_nn(prefix_part, right)
                        total[SLOTS + first : SLOTS + rows.stop] += dot_nn(row_part, right)
                dq_t[span, rows] = dot_nn(keys_t[span, first : rows.stop], row_ds)
            both = dq_t[:, rows] + dot_tn(prefix_keys, ds_p[:, rows])
            grads_ref[0, rows] = (both.T * HEAD_DIM**-0.5).astype(BF16)

    is_short = short_ref[0] < length
    pl.when(is_short)(lambda: run(True))
    pl.when(jnp.logical_not(is_short))(lambda: run(False))
    grads_ref[1] = dk[SLOTS:].astype(BF16)
    grads_ref[2] = dv[SLOTS:].astype(BF16)
    dkp_ref[...] = dk[:SLOTS]
    dvp_ref[...] = dv[:SLOTS]


def attend_back(seq, projected, attended, grad_attended, prefix_keys, prefix_values, log_sums):
    length = projected.shape[0]
    ext = (SLOTS + length, PAIR_DIM)
    return pl.pallas_call(
        attend_back_kernel,
        grid_spec=pltpu.PrefetchScalarGridSpec(
            num_scalar_prefetch=1,
            grid=(PAIRS,),
            in_specs=[
                pair_spec(length, 0),
                pair_spec(length, 1),
                pair_spec(length, 2),
                pair_spec(length, 0),
                pair_spec(length, 0),
                pair_spec(SLOTS, 0),
                pair_spec(SLOTS, 0),
                pl.BlockSpec((1, 8, length), lambda p, s: (p, 0, 0)),
            ],
            out_specs=[
                pl.BlockSpec((3, length, PAIR_DIM), lambda p, s: (0, 0, p)),
                pair_spec(SLOTS, 0),
                pair_spec(SLOTS, 0),
            ],
            scratch_shapes=[
                pltpu.VMEM(ext, BF16),
                pltpu.VMEM(ext, BF16),
                pltpu.VMEM(ext, BF16),
                pltpu.VMEM(ext, BF16),
                pltpu.VMEM((PAIR_DIM, length), BF16),
                pltpu.VMEM(ext, F32),
                pltpu.VMEM(ext, F32),
                pltpu.VMEM((PAIR_DIM, length), F32),
                pltpu.VMEM((2 * SLOTS, length), BF16),
            ],
        ),
        out_shape=[
            jax.ShapeDtypeStruct((3, length, D), BF16),
            jax.ShapeDtypeStruct((SLOTS, D), F32),
            jax.ShapeDtypeStruct((SLOTS, D), F32),
        ],
        compiler_params=params(),
        name="attend_back",
    )(
        seq,
        projected,
        projected,
        projected,
        attended,
        grad_attended,
        prefix_keys,
        prefix_values,
        log_sums,
    )


def forward_kernel(
    spot_ref,
    attended_ref,
    hidden_ref,
    norm_ref,
    w_out_ref,
    w_fc_ref,
    w_proj_ref,
    middle_ref,
    slope_ref,
    out_ref,
    normed,
    total,
):
    step = pl.program_id(0)
    length = attended_ref.shape[0]

    @pl.when(step == 0)
    def _():
        gain, offset = norm_ref[1:2], norm_ref[3:4]
        w_out = matrix_of(w_out_ref)
        for rows in row_tiles(length, 256):
            middle = hidden_ref[0, rows].astype(F32) + dot_nn(attended_ref[rows], w_out)
            middle_ref[rows] = middle
            total[rows] = middle
            normed[rows] = layer_norm(middle, gain, offset).astype(BF16)

    w_fc, w_proj = matrix_of(w_fc_ref), matrix_of(w_proj_ref)
    for rows in row_tiles(length, 256):
        activated, slope = gelu_pair(dot_nn(normed[rows], w_fc))
        slope_ref[rows] = slope.astype(BF16)
        total[rows] += dot_nn(activated.astype(BF16), w_proj)

    @pl.when(step == pl.num_programs(0) - 1)
    def _():
        out_ref[0] = total[...].astype(BF16)


def once(shape, index):
    return pl.BlockSpec(shape, index, pipeline_mode=pl.Buffered(1))


def forward_block(spot, attended, hidden, norms, w_out, w_fc, w_proj):
    length = attended.shape[0]
    whole = lambda j, s: (0, 0)
    return pl.pallas_call(
        forward_kernel,
        grid_spec=pltpu.PrefetchScalarGridSpec(
            num_scalar_prefetch=1,
            grid=(FF // D,),
            in_specs=[
                once((length, D), whole),
                once((1, length, D), lambda j, s: (s[0], 0, 0)),
                once((8, D), whole),
                once(w_out[1], lambda j, s: w_out[2](0)),
                pl.BlockSpec(w_fc[1], lambda j, s: w_fc[2](j)),
                pl.BlockSpec(w_proj[1], lambda j, s: w_proj[2](j)),
            ],
            out_specs=[
                once((length, D), whole),
                pl.BlockSpec((length, D), lambda j, s: (0, j)),
                once((1, length, D), lambda j, s: (0, 0, 0)),
            ],
            scratch_shapes=[pltpu.VMEM((length, D), BF16), pltpu.VMEM((length, D), F32)],
        ),
        out_shape=[
            jax.ShapeDtypeStruct((length, D), F32),
            jax.ShapeDtypeStruct((length, FF), BF16),
            jax.ShapeDtypeStruct((1, length, D), BF16),
        ],
        compiler_params=params(),
        name="forward_block",
    )(spot, attended, hidden, norms, w_out[0], w_fc[0], w_proj[0])


def finish_backward(upstream_ref, middle_ref, grad_total, norm_ref, w_out_ref, grad_middle_ref, grad_attended_ref):
    gain = norm_ref[1:2]
    w_out = matrix_of(w_out_ref)
    for rows in row_tiles(middle_ref.shape[0], 256):
        grad_middle = upstream_ref[0, rows].astype(F32) + norm_back(
            middle_ref[rows], gain, grad_total[rows]
        )
        grad_middle_ref[rows] = grad_middle
        grad_attended_ref[rows] = dot_nt(grad_middle.astype(BF16), w_out).astype(BF16)


def turn_kernel(
    spot_ref,
    attended_ref,
    hidden_ref,
    upstream_ref,
    norm_ref,
    w_out_ref,
    w_fc_ref,
    w_proj_ref,
    out_ref,
    grad_middle_ref,
    grad_attended_ref,
    normed,
    middle,
    total,
    grad_total,
):
    step = pl.program_id(0)
    length = attended_ref.shape[0]

    @pl.when(step == 0)
    def _():
        gain, offset = norm_ref[1:2], norm_ref[3:4]
        w_out = matrix_of(w_out_ref)
        for rows in row_tiles(length, 256):
            values = hidden_ref[0, rows].astype(F32) + dot_nn(attended_ref[rows], w_out)
            middle[rows] = values
            total[rows] = values
            normed[rows] = layer_norm(values, gain, offset).astype(BF16)
        grad_total[...] = jnp.zeros_like(grad_total)

    w_fc, w_proj = matrix_of(w_fc_ref), matrix_of(w_proj_ref)
    for rows in row_tiles(length, 256):
        inner = dot_nn(normed[rows], w_fc)
        grad_act = dot_nt(upstream_ref[0, rows], w_proj)
        activated, slope = gelu_pair(inner)
        total[rows] += dot_nn(activated.astype(BF16), w_proj)
        grad_total[rows] += dot_nt((grad_act * slope).astype(BF16), w_fc)

    @pl.when(step == pl.num_programs(0) - 1)
    def _():
        out_ref[0] = total[...].astype(BF16)
        finish_backward(
            upstream_ref, middle, grad_total, norm_ref, w_out_ref, grad_middle_ref, grad_attended_ref
        )


def turn_block(spot, attended, hidden, upstream, norms, w_out, w_fc, w_proj):
    length = attended.shape[0]
    whole = lambda j, s: (0, 0)
    return pl.pallas_call(
        turn_kernel,
        grid_spec=pltpu.PrefetchScalarGridSpec(
            num_scalar_prefetch=1,
            grid=(FF // D,),
            in_specs=[
                once((length, D), whole),
                once((1, length, D), lambda j, s: (0, 0, 0)),
                once((1, length, D), lambda j, s: (s[0], 0, 0)),
                once((8, D), whole),
                once(w_out[1], lambda j, s: w_out[2](0)),
                pl.BlockSpec(w_fc[1], lambda j, s: w_fc[2](j)),
                pl.BlockSpec(w_proj[1], lambda j, s: w_proj[2](j)),
            ],
            out_specs=[
                once((1, length, D), lambda j, s: (0, 0, 0)),
                once((length, D), whole),
                once((length, D), whole),
            ],
            scratch_shapes=[
                pltpu.VMEM((length, D), BF16),
                pltpu.VMEM((length, D), F32),
                pltpu.VMEM((length, D), F32),
                pltpu.VMEM((length, D), F32),
            ],
        ),
        out_shape=[
            jax.ShapeDtypeStruct((1, length, D), BF16),
            jax.ShapeDtypeStruct((length, D), F32),
            jax.ShapeDtypeStruct((length, D), BF16),
        ],
        compiler_params=params(),
        name="turn_block",
    )(spot, attended, hidden, upstream, norms, w_out[0], w_fc[0], w_proj[0])


def backward_kernel(
    upstream_ref,
    slope_ref,
    middle_ref,
    norm_ref,
    w_out_ref,
    w_fc_ref,
    w_proj_ref,
    grad_middle_ref,
    grad_attended_ref,
    grad_total,
):
    step = pl.program_id(0)

    @pl.when(step == 0)
    def _():
        grad_total[...] = jnp.zeros_like(grad_total)

    w_fc, w_proj = matrix_of(w_fc_ref), matrix_of(w_proj_ref)
    for rows in row_tiles(middle_ref.shape[0], 256):
        grad_act = dot_nt(upstream_ref[0, rows], w_proj)
        grad_inner = (grad_act * slope_ref[rows].astype(F32)).astype(BF16)
        grad_total[rows] += dot_nt(grad_inner, w_fc)

    @pl.when(step == pl.num_programs(0) - 1)
    def _():
        finish_backward(
            upstream_ref, middle_ref, grad_total, norm_ref, w_out_ref, grad_middle_ref, grad_attended_ref
        )


def backward_block(upstream, slope, middle, norms, w_out, w_fc, w_proj):
    length = middle.shape[0]
    whole = lambda j: (0, 0)
    return pl.pallas_call(
        backward_kernel,
        grid=(FF // D,),
        in_specs=[
            once((1, length, D), lambda j: (0, 0, 0)),
            pl.BlockSpec((length, D), lambda j: (0, j)),
            once((length, D), whole),
            once((8, D), whole),
            once(w_out[1], lambda j: w_out[2](0)),
            pl.BlockSpec(w_fc[1], w_fc[2]),
            pl.BlockSpec(w_proj[1], w_proj[2]),
        ],
        out_specs=[once((length, D), whole), once((length, D), whole)],
        scratch_shapes=[pltpu.VMEM((length, D), F32)],
        out_shape=[
            jax.ShapeDtypeStruct((length, D), F32),
            jax.ShapeDtypeStruct((length, D), BF16),
        ],
        compiler_params=params(),
        name="backward_block",
    )(upstream, slope, middle, norms, w_out[0], w_fc[0], w_proj[0])


def unproject_kernel(spot_ref, grads_ref, hidden_ref, grad_middle_ref, norm_ref, weight_ref, out_ref, total):
    step = pl.program_id(0)
    weight = matrix_of(weight_ref)

    @pl.when(step == 0)
    def _():
        for rows in row_tiles(total.shape[0], 512):
            total[rows] = dot_nt(grads_ref[0, rows], weight)

    @pl.when(step == 1)
    def _():
        for rows in row_tiles(total.shape[0], 512):
            total[rows] += dot_nt(grads_ref[0, rows], weight)

    @pl.when(step == 2)
    def _():
        gain = norm_ref[0:1]
        for rows in row_tiles(total.shape[0], 256):
            grad_normed = total[rows] + dot_nt(grads_ref[0, rows], weight)
            values = hidden_ref[0, rows].astype(F32)
            grad = grad_middle_ref[rows] + norm_back(values, gain, grad_normed)
            out_ref[0, rows] = grad.astype(BF16)


def unproject(spot, grads, hidden, grad_middle, norms, weights):
    length = hidden.shape[1]
    array, shape, index = weights
    whole = lambda j, s: (0, 0)
    return pl.pallas_call(
        unproject_kernel,
        grid_spec=pltpu.PrefetchScalarGridSpec(
            num_scalar_prefetch=1,
            grid=(3,),
            in_specs=[
                pl.BlockSpec((1, length, D), lambda j, s: (j, 0, 0)),
                once((1, length, D), lambda j, s: (s[0], 0, 0)),
                once((length, D), whole),
                once((8, D), whole),
                pl.BlockSpec(shape, lambda j, s: index(j)),
            ],
            out_specs=once((1, length, D), lambda j, s: (0, 0, 0)),
            scratch_shapes=[pltpu.VMEM((length, D), F32)],
        ),
        out_shape=jax.ShapeDtypeStruct((1, length, D), BF16),
        compiler_params=params(),
        name="unproject",
    )(spot, grads, hidden, grad_middle, norms, array)


def swap_sections(values):
    return lax.ppermute(values, "section", [(0, 1), (1, 0)])


def per_section(section_index, own):
    other = swap_sections(own)
    is_first = section_index == 0
    return jnp.where(is_first, own, other), jnp.where(is_first, other, own)


def gather_weights(w_qkv, w_out, w_fc, w_proj):
    rows = w_qkv.shape[1]
    shards = D // rows
    columns = lambda matrix: jnp.moveaxis(matrix.reshape(rows, -1, D), 1, 0).reshape(-1, D)
    shard = jnp.concatenate(
        [columns(w_qkv[0]), columns(w_out[0]), columns(w_fc[0]), w_proj[0]], axis=0
    )
    every = lax.all_gather(shard, ("dp", "section"), axis=0)
    every = every.reshape(shards, 2, 12 * rows, D)
    layers = []
    for layer in range(2):
        if rows % 16 == 0:
            block = (shards, 1, rows, D)
            ff_shards = shards // 4

            def at(first, layer=layer):
                return lambda j: (0, layer, first + j, 0)

            layers.append(
                (
                    (every, block, at(0)),
                    (every, block, at(3)),
                    (every, block, at(4)),
                    (every, (ff_shards, 1, 4 * rows, D), lambda j, layer=layer: (j, layer, 2, 0)),
                )
            )
        else:
            mine = every[:, layer]
            straight = jnp.moveaxis(mine[:, : 8 * rows].reshape(shards, 8, rows, D), 1, 0)
            straight = straight.reshape(1, 8 * D, D)
            proj = mine[:, 8 * rows :].reshape(1, FF, D)

            def at(first):
                return lambda j: (0, first + j, 0)

            block = (1, D, D)
            layers.append(
                (
                    (straight, block, at(0)),
                    (straight, block, at(3)),
                    (straight, block, at(4)),
                    (proj, block, at(0)),
                )
            )
    return layers


def reparam_hidden(table, w_first, b_first):
    return jnp.tanh(jnp.dot(table, w_first, precision=highest_mode) + b_first)


def reparam_out(hidden_units, w_second, b_second):
    return jnp.dot(hidden_units, w_second, precision=highest_mode) + b_second


def sum_dp(values):
    count = lax.axis_size("dp")
    step = 1
    while step < count:
        pairs = [(i, i ^ step) for i in range(count)]
        values = values + lax.ppermute(values, "dp", pairs)
        step *= 2
    return values


def per_device(
    tokens,
    seq_length,
    cotangent,
    ln_gain,
    ln_bias,
    w_qkv,
    w_out,
    w_fc,
    w_proj,
    prefix_table,
    reparam_w1,
    reparam_b1,
    reparam_w2,
    reparam_b2,
):
    section_index = lax.axis_index("section")
    is_first = section_index == 0
    layers = gather_weights(w_qkv, w_out, w_fc, w_proj)

    table_values = prefix_table.astype(F32)
    first_weight = reparam_w1.astype(F32)
    first_bias = reparam_b1.astype(F32)
    second_weight = reparam_w2[0].astype(F32)
    second_bias = reparam_b2[0].astype(F32)
    hidden_units = reparam_hidden(table_values, first_weight, first_bias)
    prefix_kv = reparam_out(hidden_units, second_weight, second_bias).astype(BF16)
    pad = ((0, SLOTS - PREFIX), (0, 0))
    small = jnp.concatenate(
        [
            jnp.pad(prefix_kv[:, :D], pad),
            jnp.pad(prefix_kv[:, D:], pad),
            ln_gain[0],
            ln_bias[0],
            jnp.zeros((4, D), BF16),
        ],
        axis=0,
    )
    small_pair = per_section(section_index, small)
    prefix_pair = [(part[:SLOTS], part[SLOTS : 2 * SLOTS]) for part in small_pair]
    norm_pair = [part[2 * SLOTS :].astype(F32) for part in small_pair]

    spot = section_index.astype(jnp.int32)[None]
    none = jnp.zeros((1,), jnp.int32)
    seq = lax.dynamic_slice_in_dim(seq_length, section_index, 1, 0)

    qkv_first, out_first, fc_first, proj_first = layers[0]
    qkv_last, out_last, fc_last, proj_last = layers[1]

    projected_first = project(spot, tokens, norm_pair[0], qkv_first)
    attended_first, log_first = attend(seq, projected_first, *prefix_pair[0])
    middle, slope, handed = forward_block(
        spot, attended_first, tokens, norm_pair[0], out_first, fc_first, proj_first
    )
    projected = project(none, handed, norm_pair[1], qkv_last)
    attended, log_sums = attend(seq, projected, *prefix_pair[1])
    final, grad_middle, grad_attended = turn_block(
        spot, attended, handed, cotangent, norm_pair[1], out_last, fc_last, proj_last
    )
    grads, dkp_last, dvp_last = attend_back(
        seq, projected, attended, grad_attended, *prefix_pair[1], log_sums
    )
    grad_handed = unproject(none, grads, handed, grad_middle, norm_pair[1], qkv_last)
    grad_middle, grad_attended = backward_block(
        grad_handed, slope, middle, norm_pair[0], out_first, fc_first, proj_first
    )
    grads, dkp_first, dvp_first = attend_back(
        seq, projected_first, attended_first, grad_attended, *prefix_pair[0], log_first
    )
    grad_tokens = unproject(spot, grads, tokens, grad_middle, norm_pair[0], qkv_first)

    def gathered_rows(first, last):
        kept = jnp.where(is_first, first, last)
        received = swap_sections(jnp.where(is_first, last, first))
        return jnp.concatenate(
            [jnp.where(is_first, kept, received), jnp.where(is_first, received, kept)], axis=0
        )

    activations = gathered_rows(handed, final)
    input_grads = gathered_rows(grad_tokens, grad_handed)

    prefix_first = jnp.concatenate([dkp_first[:PREFIX], dvp_first[:PREFIX]], axis=1)
    prefix_last = jnp.concatenate([dkp_last[:PREFIX], dvp_last[:PREFIX]], axis=1)
    kept = jnp.where(is_first, prefix_first, prefix_last)
    received = swap_sections(jnp.where(is_first, prefix_last, prefix_first))
    prefix_total = sum_dp(kept + received)

    grad_hidden, grad_w2, grad_b2 = jax.vjp(reparam_out, hidden_units, second_weight, second_bias)[
        1
    ](prefix_total)
    grad_hidden = grad_hidden + swap_sections(grad_hidden)
    grad_table, grad_w1, grad_b1 = jax.vjp(reparam_hidden, table_values, first_weight, first_bias)[
        1
    ](grad_hidden)
    return (
        activations[None],
        input_grads[None],
        grad_table,
        grad_w1,
        grad_b1,
        grad_w2[None],
        grad_b2[None],
    )


def solution(mesh):
    in_specs = (
        P("dp", None, None),
        P("dp"),
        P("dp", None, None),
        P("section", None, None),
        P("section", None, None),
        P("section", "dp", None),
        P("section", "dp", None),
        P("section", "dp", None),
        P("section", "dp", None),
        P(),
        P(),
        P(),
        P("section", None, None),
        P("section", None),
    )
    out_specs = (
        P("section", "dp", None, None),
        P("section", "dp", None, None),
        P(),
        P(),
        P(),
        P("section", None, None),
        P("section", None),
    )
    return jax.shard_map(
        per_device, mesh=mesh, in_specs=in_specs, out_specs=out_specs, check_vma=False
    )
```

```python
import functools

import jax
import jax.numpy as jnp
from jax import lax
from jax.experimental import pallas as pl
from jax.experimental.pallas import tpu as pltpu
from jax.sharding import PartitionSpec as P

D = 1024
HEADS = 16
HEAD_DIM = 64
FF = 4096
PREFIX = 10
SLOTS = 16
PAIRS = 8
PAIR_DIM = 128
BLOCK = 256

eps_norm = 1e-05
neg_big = -1e30
highest_mode = lax.Precision.HIGHEST
VMEM_BYTES = 62 * 2**20
F32 = jnp.float32
BF16 = jnp.bfloat16


def dot(left, right, dims):
    return lax.dot_general(left, right, (dims, ((), ())), preferred_element_type=F32)


def dot_nn(left, right):
    return dot(left, right, ((1,), (0,)))


def dot_nt(left, right):
    return dot(left, right, ((1,), (1,)))


def dot_tn(left, right):
    return dot(left, right, ((0,), (0,)))


def normalised(values):
    centre = jnp.mean(values, axis=-1, keepdims=True)
    spread = values - centre
    variance = jnp.mean(spread * spread, axis=-1, keepdims=True)
    inverse = lax.rsqrt(variance + eps_norm)
    return spread * inverse, inverse


def layer_norm(values, gain, offset):
    return normalised(values)[0] * gain + offset


def norm_back(values, gain, upstream):
    unit, inverse = normalised(values)
    scaled = upstream * gain
    mean_scaled = jnp.mean(scaled, axis=-1, keepdims=True)
    mean_unit = jnp.mean(scaled * unit, axis=-1, keepdims=True)
    return (scaled - mean_scaled - unit * mean_unit) * inverse


SQRT_2_PI = 0.7978845608028654
CUBIC = 0.044715


def gelu_pair(values):
    cubic_part = (SQRT_2_PI * CUBIC) * (values * values)
    half_tanh = 0.5 + 0.5 * jnp.tanh(values * (SQRT_2_PI + cubic_part))
    out = values * half_tanh
    slope = half_tanh + out * ((2.0 - 2.0 * half_tanh) * (SQRT_2_PI + 3.0 * cubic_part))
    return out, slope


def params(**kwargs):
    return pltpu.CompilerParams(vmem_limit_bytes=VMEM_BYTES, **kwargs)


def cost(micros):
    return pl.CostEstimate(flops=int(micros * 1.15e9), bytes_accessed=2**20, transcendentals=0)


SHARDS = 16
HALF = 128
SHARD_ROWS = 64
BLOCKS = FF // D


def load_across(array, half, row, target, semaphore):
    return pltpu.make_async_copy(array.at[:, half, pl.ds(row, SHARD_ROWS)], target, semaphore)


def load_qkv(array, row, part, weights, semaphores):
    half, inner = divmod(part, 2)
    return load_across(
        array, half, row + inner * SHARD_ROWS, weights.at[part], semaphores.at[part]
    )


def load_out(array, row, target, semaphore):
    return load_across(array, 1, row + SHARD_ROWS, target, semaphore)


def load_up(array, row, block, target, semaphore):
    half, inner = divmod(block, 2)
    return load_across(array, half, row + inner * SHARD_ROWS, target, semaphore)


def load_down(array, row, block, target, semaphore):
    few = SHARDS // BLOCKS
    return pltpu.make_async_copy(
        array.at[pl.ds(block * few, few), :, pl.ds(row, HALF)], target, semaphore
    )


def across_scratch(count):
    return pltpu.VMEM((count, SHARDS, SHARD_ROWS, D), BF16)


def down_scratch():
    return pltpu.VMEM((BLOCKS, SHARDS // BLOCKS, 2, HALF, D), BF16)


def matrix(ref, *index):
    return ref[index].reshape(D, D) if index else ref[...].reshape(D, D)


ANY = pl.BlockSpec(memory_space=pl.ANY)


def once(shape, index):
    return pl.BlockSpec(shape, index, pipeline_mode=pl.Buffered(1))


def row_tiles(length, size):
    return [slice(start, start + size) for start in range(0, length, size)]


CHUNK = 16


def put_pairs(ref, rows, values):
    for pair in range(PAIRS):
        ref[pair, rows] = values[:, pair * PAIR_DIM : (pair + 1) * PAIR_DIM]


def get_pairs(ref, rows, *lead):
    return jnp.concatenate([ref[(*lead, pair, rows)] for pair in range(PAIRS)], axis=1)


def chunks(rows, size=CHUNK):
    return [slice(start, start + size) for start in range(rows.start, rows.stop, size)]


def shifted(rows, by):
    return slice(rows.start + by, rows.stop + by)


def qkv_kernel(row, spot_ref, hidden_ref, norm_ref, array, out_ref, normed, weights, semaphores):
    step = pl.program_id(0)
    loads = [load_qkv(array, row, part, weights, semaphores) for part in range(3)]
    length = hidden_ref.shape[1]
    tiles = row_tiles(length, 512)

    @pl.when(step == 0)
    def _():
        loads[0].start()
        gain, offset = norm_ref[0:1], norm_ref[2:3]
        for rows in chunks(slice(0, length)):
            values = hidden_ref[0, rows].astype(F32)
            normed[rows] = layer_norm(values, gain, offset).astype(BF16)
        loads[0].wait()
        loads[1].start()
        loads[2].start()
        for rows in tiles:
            queries = dot_nn(normed[rows], matrix(weights, 0))
            put_pairs(out_ref, rows, (queries * HEAD_DIM**-0.5).astype(BF16))

    for part in (1, 2):

        @pl.when(step == part)
        def _(part=part):
            loads[part].wait()
            for rows in tiles:
                put_pairs(out_ref, rows, dot_nn(normed[rows], matrix(weights, part)).astype(BF16))


def project(spot, which, hidden, norms, place):
    length = hidden.shape[1]
    return pl.pallas_call(
        functools.partial(qkv_kernel, place[1]),
        grid_spec=pltpu.PrefetchScalarGridSpec(
            num_scalar_prefetch=1,
            grid=(3,),
            in_specs=[
                once((1, length, D), lambda j, s: (s[which], 0, 0)),
                once((8, D), lambda j, s: (0, 0)),
                ANY,
            ],
            out_specs=pl.BlockSpec((PAIRS, length, PAIR_DIM), lambda j, s: (j, 0, 0)),
            scratch_shapes=[
                pltpu.VMEM((length, D), BF16),
                across_scratch(3),
                pltpu.SemaphoreType.DMA((3,)),
            ],
        ),
        out_shape=jax.ShapeDtypeStruct((3 * PAIRS, length, PAIR_DIM), BF16),
        compiler_params=params(),
        cost_estimate=cost(12),
        name="norm_project",
    )(spot, hidden, norms, place[0])


def lane_halves(block):
    lanes = lax.broadcasted_iota(jnp.int32, block.shape, 1)
    zero = jnp.zeros_like(block)
    return jnp.where(lanes < HEAD_DIM, block, zero), jnp.where(lanes < HEAD_DIM, zero, block)


def key_spans(first, stop):
    if first == 0:
        return [slice(0, SLOTS + stop)]
    return [slice(0, SLOTS), slice(SLOTS + first, SLOTS + stop)]


def read_spans(ref, spans, *rest):
    parts = [ref[(span, *rest)] for span in spans]
    return parts[0] if len(parts) == 1 else jnp.concatenate(parts, axis=0)


def cut_spans(values, spans):
    start = 0
    for span in spans:
        size = span.stop - span.start
        yield span, values[start : start + size]
        start += size


def strips(length, short):
    return [
        (rows, slice(2 * rows.start, 2 * rows.stop), rows.start if short else 0)
        for rows in row_tiles(length, BLOCK)
    ]


def stacked_halves(block):
    return jnp.concatenate(lane_halves(block), axis=0)


def own_heads(product):
    return jnp.concatenate([product[:HEAD_DIM, :BLOCK], product[HEAD_DIM:, BLOCK:]], axis=0)


def either_length(length_ref, length, run):
    short = length_ref[0] < length
    pl.when(short)(lambda: run(True))
    pl.when(jnp.logical_not(short))(lambda: run(False))


def allowed(rows, first_diagonal):
    shape = (rows.stop - rows.start, 2 * BLOCK)
    keys = lax.broadcasted_iota(jnp.int32, shape, 0) + rows.start
    if rows.stop <= SLOTS:
        return keys < PREFIX
    queries = lax.broadcasted_iota(jnp.int32, shape, 1) % BLOCK
    return keys - first_diagonal <= queries


def eight_rows(values, reduce):
    return reduce(values.reshape(-1, 8, values.shape[-1]), axis=0)


def attend_kernel(
    seq_ref, q_ref, k_ref, v_ref, kp_ref, vp_ref, out_ref, probs_ref, scale_ref, keys, values_t, scores
):
    length = q_ref.shape[1]
    keys[:SLOTS], keys[SLOTS:] = kp_ref[0], k_ref[0]
    values_t[...] = v_ref[0].T
    prefix_values = vp_ref[0]

    def run(short):
        def scored(strip, slot):
            rows, _, first = strip
            count = SLOTS + rows.stop - first
            scores[slot, :count] = dot_nt(
                read_spans(keys, key_spans(first, rows.stop)), stacked_halves(q_ref[0, rows])
            )

        todo = strips(length, short)
        scored(todo[0], 0)
        for index, (rows, columns, first) in enumerate(todo):
            slot = index % 2
            if index + 1 < len(todo):
                scored(todo[index + 1], 1 - slot)
            count = SLOTS + rows.stop - first
            parts = chunks(slice(0, count))
            top = None
            for part in parts:
                values = scores[slot, part]
                if part.stop <= SLOTS or part.start >= count - BLOCK:
                    values = jnp.where(allowed(part, count - BLOCK), values, neg_big)
                    scores[slot, part] = values
                values = eight_rows(values, jnp.max)
                top = values if top is None else jnp.maximum(top, values)
            top = jnp.max(top, axis=0, keepdims=True)
            total = None
            for part in parts:
                values = jnp.exp(scores[slot, part] - top)
                place = part if part.stop <= SLOTS else shifted(part, first)
                probs_ref[0, place, columns] = values.astype(BF16)
                values = eight_rows(values, jnp.sum)
                total = values if total is None else total + values
            inverse = 1.0 / jnp.sum(total, axis=0, keepdims=True)
            both = dot_nn(
                values_t[:, first : rows.stop],
                probs_ref[0, SLOTS + first : SLOTS + rows.stop, columns],
            ) + dot_tn(prefix_values, probs_ref[0, :SLOTS, columns])
            inverse = jnp.concatenate(
                [
                    jnp.broadcast_to(inverse[:, :BLOCK], (HEAD_DIM, BLOCK)),
                    jnp.broadcast_to(inverse[:, BLOCK:], (HEAD_DIM, BLOCK)),
                ],
                axis=0,
            )
            out_ref[0, rows] = (own_heads(both) * inverse).T.astype(BF16)
            scale_ref[0, rows] = inverse.T

    either_length(seq_ref, length, run)


def pair_spec(length, part):
    return pl.BlockSpec((1, length, PAIR_DIM), lambda p, s: (part * PAIRS + p, 0, 0))


def probs_spec(length):
    return pl.BlockSpec((1, SLOTS + length, 2 * length), lambda p, s: (p, 0, 0))


def attend(seq, projected, prefix_keys, prefix_values):
    length = projected.shape[1]
    return pl.pallas_call(
        attend_kernel,
        grid_spec=pltpu.PrefetchScalarGridSpec(
            num_scalar_prefetch=1,
            grid=(PAIRS,),
            in_specs=[
                pair_spec(length, 0),
                pair_spec(length, 1),
                pair_spec(length, 2),
                pair_spec(SLOTS, 0),
                pair_spec(SLOTS, 0),
            ],
            out_specs=[pair_spec(length, 0), probs_spec(length), pair_spec(length, 0)],
            scratch_shapes=[
                pltpu.VMEM((SLOTS + length, PAIR_DIM), BF16),
                pltpu.VMEM((PAIR_DIM, length), BF16),
                pltpu.VMEM((2, SLOTS + length, 2 * BLOCK), F32),
            ],
        ),
        out_shape=[
            jax.ShapeDtypeStruct((PAIRS, length, PAIR_DIM), BF16),
            jax.ShapeDtypeStruct((PAIRS, SLOTS + length, 2 * length), BF16),
            jax.ShapeDtypeStruct((PAIRS, length, PAIR_DIM), F32),
        ],
        compiler_params=params(),
        cost_estimate=cost(30),
        name="attend",
    )(seq, projected, projected, projected, prefix_keys, prefix_values)


def attend_back_kernel(
    seq_ref,
    q_ref,
    k_ref,
    v_ref,
    out_ref,
    grad_ref,
    kp_ref,
    vp_ref,
    probs_ref,
    scale_ref,
    grads_ref,
    dkp_ref,
    dvp_ref,
    values,
    keys_t,
    dk,
    dv,
    dprobs,
    ds,
):
    length = q_ref.shape[1]
    values[:SLOTS], values[SLOTS:] = vp_ref[0], v_ref[0]
    keys_t[...] = k_ref[0].T
    prefix_keys = kp_ref[0]
    dk[...] = jnp.zeros_like(dk)
    dv[...] = jnp.zeros_like(dv)

    def run(short):
        def prepared(strip, slot):
            rows, _, first = strip
            grads = (grad_ref[0, rows].astype(F32) * scale_ref[0, rows]).astype(BF16)
            halves = stacked_halves(grads)
            weighted_t = (grads.astype(F32) * out_ref[0, rows].astype(F32)).T
            centre = jnp.concatenate(
                [
                    jnp.sum(weighted_t[:HEAD_DIM], axis=0, keepdims=True),
                    jnp.sum(weighted_t[HEAD_DIM:], axis=0, keepdims=True),
                ],
                axis=1,
            )
            dprobs[slot, : SLOTS + rows.stop - first] = dot_nt(
                read_spans(values, key_spans(first, rows.stop)), halves
            )
            return halves, centre

        todo = strips(length, short)
        ahead = prepared(todo[0], 0)
        for index, (rows, columns, first) in enumerate(todo):
            slot = index % 2
            spans = key_spans(first, rows.stop)
            grad_halves, centre = ahead
            if index + 1 < len(todo):
                ahead = prepared(todo[index + 1], 1 - slot)
            count = SLOTS + rows.stop - first
            for part in chunks(slice(0, count)):
                place = part if part.stop <= SLOTS else shifted(part, first)
                probs = probs_ref[0, place, columns].astype(F32)
                ds[slot, part] = (probs * (dprobs[slot, part] - centre)).astype(BF16)
            for total, left, right in (
                (dv, read_spans(probs_ref.at[0], spans, columns), grad_halves),
                (dk, ds[slot, :count], stacked_halves(q_ref[0, rows])),
            ):
                for span, part in cut_spans(dot_nn(left, right), spans):
                    total[span] += part
            both = dot_nn(keys_t[:, first : rows.stop], ds[slot, SLOTS:count]) + dot_tn(
                prefix_keys, ds[slot, :SLOTS]
            )
            grads_ref[0, 0, rows] = (own_heads(both).T * HEAD_DIM**-0.5).astype(BF16)

    either_length(seq_ref, length, run)
    grads_ref[1, 0] = dk[SLOTS:].astype(BF16)
    grads_ref[2, 0] = dv[SLOTS:].astype(BF16)
    dkp_ref[0] = dk[:SLOTS]
    dvp_ref[0] = dv[:SLOTS]


def attend_back(seq, projected, attended, grad_attended, prefix_keys, prefix_values, probs, scale):
    length = projected.shape[1]
    ext = (SLOTS + length, PAIR_DIM)
    return pl.pallas_call(
        attend_back_kernel,
        grid_spec=pltpu.PrefetchScalarGridSpec(
            num_scalar_prefetch=1,
            grid=(PAIRS,),
            in_specs=[
                pair_spec(length, 0),
                pair_spec(length, 1),
                pair_spec(length, 2),
                pair_spec(length, 0),
                pair_spec(length, 0),
                pair_spec(SLOTS, 0),
                pair_spec(SLOTS, 0),
                probs_spec(length),
                pair_spec(length, 0),
            ],
            out_specs=[
                pl.BlockSpec((3, 1, length, PAIR_DIM), lambda p, s: (0, p, 0, 0)),
                pair_spec(SLOTS, 0),
                pair_spec(SLOTS, 0),
            ],
            scratch_shapes=[
                pltpu.VMEM(ext, BF16),
                pltpu.VMEM((PAIR_DIM, length), BF16),
                pltpu.VMEM(ext, F32),
                pltpu.VMEM(ext, F32),
                pltpu.VMEM((2, SLOTS + length, 2 * BLOCK), F32),
                pltpu.VMEM((2, SLOTS + length, 2 * BLOCK), BF16),
            ],
        ),
        out_shape=[
            jax.ShapeDtypeStruct((3, PAIRS, length, PAIR_DIM), BF16),
            jax.ShapeDtypeStruct((PAIRS, SLOTS, PAIR_DIM), F32),
            jax.ShapeDtypeStruct((PAIRS, SLOTS, PAIR_DIM), F32),
        ],
        compiler_params=params(),
        cost_estimate=cost(30),
        name="attend_back",
    )(
        seq,
        projected,
        projected,
        projected,
        attended,
        grad_attended,
        prefix_keys,
        prefix_values,
        probs,
        scale,
    )


def middle_kernel(row, spot_ref, attended_ref, hidden_ref, norm_ref, array, middle_ref, normed_ref, weights, semaphores):
    step = pl.program_id(0)
    load = load_out(array, row, weights.at[0], semaphores.at[0])

    @pl.when(step == 0)
    def _():
        load.start()
        load.wait()

    middle_ref[...] = dot_nn(get_pairs(attended_ref, slice(None)), matrix(weights, 0))
    gain, offset = norm_ref[1:2], norm_ref[3:4]
    for rows in chunks(slice(0, middle_ref.shape[0])):
        middle = hidden_ref[0, rows].astype(F32) + middle_ref[rows]
        middle_ref[rows] = middle
        normed_ref[rows] = layer_norm(middle, gain, offset).astype(BF16)


def middle_block(spot, which, attended, hidden, norms, place):
    length = attended.shape[1]
    tile = pl.BlockSpec((256, D), lambda m, s: (m, 0))
    return pl.pallas_call(
        functools.partial(middle_kernel, place[1]),
        grid_spec=pltpu.PrefetchScalarGridSpec(
            num_scalar_prefetch=1,
            grid=(length // 256,),
            in_specs=[
                pl.BlockSpec((PAIRS, 256, PAIR_DIM), lambda m, s: (0, m, 0)),
                pl.BlockSpec((1, 256, D), lambda m, s: (s[which], m, 0)),
                once((8, D), lambda m, s: (0, 0)),
                ANY,
            ],
            out_specs=[tile, tile],
            scratch_shapes=[across_scratch(1), pltpu.SemaphoreType.DMA((1,))],
        ),
        out_shape=[
            jax.ShapeDtypeStruct((length, D), F32),
            jax.ShapeDtypeStruct((length, D), BF16),
        ],
        compiler_params=params(),
        cost_estimate=cost(5),
        name="middle_block",
    )(spot, attended, hidden, norms, place[0])


def feed_forward_loads(up, down, rows, up_weights, down_weights, semaphores):
    return [
        (
            load_up(up, rows[0], block, up_weights.at[block], semaphores.at[0, block]),
            load_down(down, rows[1], block, down_weights.at[block], semaphores.at[1, block]),
        )
        for block in range(BLOCKS)
    ]


def start_all(loads):
    for pair in loads:
        for load in pair:
            load.start()


def wait_step(loads, step):
    for block, pair in enumerate(loads):

        @pl.when(step == block)
        def _(pair=pair):
            for load in pair:
                load.wait()


def wait_for(target, semaphore):
    pltpu.make_async_copy(target, target, semaphore).wait()


def feed_forward_scratch():
    return [across_scratch(BLOCKS), down_scratch(), pltpu.SemaphoreType.DMA((2, BLOCKS))]


def forward_kernel(
    rows_at,
    normed_ref,
    middle_ref,
    up,
    down,
    slope_ref,
    out_ref,
    total,
    inner,
    activated,
    up_weights,
    down_weights,
    semaphores,
):
    step = pl.program_id(0)
    tiles = row_tiles(middle_ref.shape[0], TILE)
    loads = feed_forward_loads(up, down, rows_at, up_weights, down_weights, semaphores)

    @pl.when(step == 0)
    def _():
        start_all(loads[:1])
        total[...] = middle_ref[...]

    wait_step(loads, step)
    for later in range(1, BLOCKS):
        pl.when(step == later - 1)(lambda later=later: start_all(loads[later : later + 1]))
    w_fc, w_proj = matrix(up_weights, step), matrix(down_weights, step)
    inner[tiles[0]] = dot_nn(normed_ref[tiles[0]], w_fc)
    for index, rows in enumerate(tiles):
        if index + 1 < len(tiles):
            inner[tiles[index + 1]] = dot_nn(normed_ref[tiles[index + 1]], w_fc)
        for part in chunks(rows):
            value, slope = gelu_pair(inner[part])
            activated[part] = value.astype(BF16)
            slope_ref[part] = slope.astype(BF16)
        total[rows] += dot_nn(activated[rows], w_proj)

    @pl.when(step == pl.num_programs(0) - 1)
    def _():
        out_ref[0] = total[...].astype(BF16)


def forward_block(normed, middle, up, down):
    length = normed.shape[0]
    whole = lambda j: (0, 0)
    return pl.pallas_call(
        functools.partial(forward_kernel, (up[1], down[1])),
        grid=(BLOCKS,),
        in_specs=[once((length, D), whole), once((length, D), whole), ANY, ANY],
        out_specs=[
            pl.BlockSpec((length, D), lambda j: (0, j)),
            once((1, length, D), lambda j: (0, 0, 0)),
        ],
        scratch_shapes=[whole_scratch(F32), whole_scratch(F32), whole_scratch(BF16)]
        + feed_forward_scratch(),
        out_shape=[
            jax.ShapeDtypeStruct((length, FF), BF16),
            jax.ShapeDtypeStruct((1, length, D), BF16),
        ],
        compiler_params=params(),
        cost_estimate=cost(25),
        name="forward_block",
    )(normed, middle, up[0], down[0])


FINISH = 256


def finish_backward(upstream, middle, grad_total, norm_ref, w_out, grad_middle, grad_attended, stores):
    gain = norm_ref[1:2]
    for index, rows in enumerate(row_tiles(D, FINISH)):
        for part in chunks(rows):
            grad = upstream[part].astype(F32) + norm_back(middle[part], gain, grad_total[part])
            grad_middle[part] = grad.astype(BF16)
        put_pairs(grad_attended, rows, dot_nt(grad_middle[rows], w_out).astype(BF16))
        for store in stores(rows, index):
            store.start()
    for index, rows in enumerate(row_tiles(D, FINISH)):
        for store in stores(rows, index):
            store.wait()


def turn_kernel(
    rows_at,
    spot_ref,
    norm_ref,
    normed_ref,
    middle_ref,
    upstream_ref,
    attention,
    up,
    down,
    out_ref,
    grad_middle_ref,
    grad_attended_ref,
    normed,
    middle,
    upstream,
    total,
    grad_total,
    inner,
    grad_act,
    out,
    grad_middle,
    grad_attended,
    up_weights,
    down_weights,
    out_weights,
    semaphores,
    load_semaphores,
    store_semaphores,
):
    activated, grad_inner = grad_middle, out
    loads = feed_forward_loads(up, down, rows_at[1:], up_weights, down_weights, semaphores)
    copy = pltpu.make_async_copy
    get_normed = copy(normed_ref, normed, load_semaphores.at[0])
    get_upstream = copy(upstream_ref.at[spot_ref[0]], upstream, load_semaphores.at[1])
    get_middle = copy(middle_ref, middle, load_semaphores.at[2])
    get_out = load_out(attention, rows_at[0], out_weights, load_semaphores.at[3])
    get_normed.start()
    loads[0][0].start()
    total[...] = jnp.zeros_like(total)
    grad_total[...] = jnp.zeros_like(grad_total)
    get_normed.wait()
    get_upstream.start()
    loads[0][1].start()

    def step(block, carry):
        wait_for(up_weights.at[block], semaphores.at[0, block])
        tiles = row_tiles(D, TILE)
        w_fc = matrix(up_weights, block)
        inner[0] = dot_nn(normed[tiles[0]], w_fc)
        pl.when(block == 0)(get_upstream.wait)
        wait_for(down_weights.at[block], semaphores.at[1, block])
        w_proj = matrix(down_weights, block)
        for later in range(1, BLOCKS):
            pl.when(block == later - 1)(lambda later=later: start_all(loads[later : later + 1]))

        @pl.when(block == BLOCKS - 1)
        def _():
            get_middle.start()
            get_out.start()

        grad_act[0] = dot_nt(upstream[tiles[0]], w_proj)
        for index, rows in enumerate(tiles):
            slot = index % 2
            if index + 1 < len(tiles):
                inner[1 - slot] = dot_nn(normed[tiles[index + 1]], w_fc)
                grad_act[1 - slot] = dot_nt(upstream[tiles[index + 1]], w_proj)
            for part in chunks(rows):
                here = shifted(part, -rows.start)
                value, slope = gelu_pair(inner[slot, here])
                activated[part] = value.astype(BF16)
                grad_inner[part] = (grad_act[slot, here] * slope).astype(BF16)
            total[rows] += dot_nn(activated[rows], w_proj)
            grad_total[rows] += dot_nt(grad_inner[rows], w_fc)
        return carry

    lax.fori_loop(0, BLOCKS, step, 0)
    get_middle.wait()
    for part in chunks(slice(0, D)):
        out[part] = (total[part] + middle[part]).astype(BF16)
    put_out = copy(out, out_ref.at[0], store_semaphores.at[0, 0])
    put_out.start()
    get_out.wait()

    def stores(rows, index):
        return (
            copy(grad_middle.at[rows], grad_middle_ref.at[rows], store_semaphores.at[1, index]),
            copy(grad_attended.at[:, rows], grad_attended_ref.at[:, rows], store_semaphores.at[2, index]),
        )

    finish_backward(
        upstream, middle, grad_total, norm_ref, matrix(out_weights), grad_middle, grad_attended, stores
    )
    put_out.wait()


TILE = 512
SCALARS = pl.BlockSpec(memory_space=pltpu.SMEM)
IN_VMEM = pl.BlockSpec(memory_space=pltpu.VMEM)


def whole_scratch(dtype):
    return pltpu.VMEM((D, D), dtype)


def turn_block(spot, normed, middle, upstream, norms, attention, up, down):
    length = normed.shape[0]
    return pl.pallas_call(
        functools.partial(turn_kernel, (attention[1], up[1], down[1])),
        in_specs=[SCALARS, IN_VMEM] + [ANY] * 6,
        out_specs=[ANY] * 3,
        scratch_shapes=[
            whole_scratch(BF16),
            whole_scratch(F32),
            whole_scratch(BF16),
            whole_scratch(F32),
            whole_scratch(F32),
            pltpu.VMEM((2, TILE, D), F32),
            pltpu.VMEM((2, TILE, D), F32),
            whole_scratch(BF16),
            whole_scratch(BF16),
            pltpu.VMEM((PAIRS, D, PAIR_DIM), BF16),
            across_scratch(BLOCKS),
            down_scratch(),
            pltpu.VMEM((SHARDS, SHARD_ROWS, D), BF16),
            pltpu.SemaphoreType.DMA((2, BLOCKS)),
            pltpu.SemaphoreType.DMA((4,)),
            pltpu.SemaphoreType.DMA((3, D // FINISH)),
        ],
        out_shape=[
            jax.ShapeDtypeStruct((1, length, D), BF16),
            jax.ShapeDtypeStruct((length, D), BF16),
            jax.ShapeDtypeStruct((PAIRS, length, PAIR_DIM), BF16),
        ],
        compiler_params=params(),
        cost_estimate=cost(42),
        name="turn_block",
    )(spot, norms, normed, middle, upstream, attention[0], up[0], down[0])


def backward_kernel(
    rows_at,
    norm_ref,
    slope_ref,
    middle_ref,
    upstream_ref,
    attention,
    up,
    down,
    grad_middle_ref,
    grad_attended_ref,
    slope,
    middle,
    upstream,
    grad_total,
    grad_act,
    grad_middle,
    grad_attended,
    up_weights,
    down_weights,
    out_weights,
    semaphores,
    load_semaphores,
    store_semaphores,
):
    grad_inner = grad_middle
    loads = feed_forward_loads(up, down, rows_at[1:], up_weights, down_weights, semaphores)
    copy = pltpu.make_async_copy
    get_upstream = copy(upstream_ref.at[0], upstream, load_semaphores.at[BLOCKS])
    get_middle = copy(middle_ref, middle, load_semaphores.at[BLOCKS + 1])
    get_out = load_out(attention, rows_at[0], out_weights, load_semaphores.at[BLOCKS + 2])
    get_slopes = [
        copy(slope_ref.at[:, pl.ds(block * D, D)], slope.at[block], load_semaphores.at[block])
        for block in range(BLOCKS)
    ]
    get_upstream.start()
    loads[0][1].start()
    grad_total[...] = jnp.zeros_like(grad_total)
    get_upstream.wait()
    get_slopes[0].start()
    loads[0][0].start()

    def step(block, carry):
        wait_for(down_weights.at[block], semaphores.at[1, block])
        w_proj = matrix(down_weights, block)
        tiles = row_tiles(D, TILE)
        grad_act[tiles[0]] = dot_nt(upstream[tiles[0]], w_proj)
        wait_for(slope.at[block], load_semaphores.at[block])
        wait_for(up_weights.at[block], semaphores.at[0, block])
        w_fc = matrix(up_weights, block)
        for later in range(1, BLOCKS):

            @pl.when(block == later - 1)
            def _(later=later):
                loads[later][1].start()
                get_slopes[later].start()
                loads[later][0].start()

        @pl.when(block == BLOCKS - 1)
        def _():
            get_middle.start()
            get_out.start()

        for index, rows in enumerate(tiles):
            if index + 1 < len(tiles):
                grad_act[tiles[index + 1]] = dot_nt(upstream[tiles[index + 1]], w_proj)
            for part in chunks(rows):
                grad_inner[part] = (grad_act[part] * slope[block, part].astype(F32)).astype(BF16)
            grad_total[rows] += dot_nt(grad_inner[rows], w_fc)
        return carry

    lax.fori_loop(0, BLOCKS, step, 0)
    get_middle.wait()
    get_out.wait()

    def stores(rows, index):
        return (
            copy(grad_middle.at[rows], grad_middle_ref.at[rows], store_semaphores.at[0, index]),
            copy(grad_attended.at[:, rows], grad_attended_ref.at[:, rows], store_semaphores.at[1, index]),
        )

    finish_backward(
        upstream, middle, grad_total, norm_ref, matrix(out_weights), grad_middle, grad_attended, stores
    )


def backward_block(upstream, slope, middle, norms, attention, up, down):
    length = middle.shape[0]
    return pl.pallas_call(
        functools.partial(backward_kernel, (attention[1], up[1], down[1])),
        in_specs=[IN_VMEM] + [ANY] * 6,
        out_specs=[ANY] * 2,
        scratch_shapes=[
            pltpu.VMEM((BLOCKS, D, D), BF16),
            whole_scratch(F32),
            whole_scratch(BF16),
            whole_scratch(F32),
            whole_scratch(F32),
            whole_scratch(BF16),
            pltpu.VMEM((PAIRS, D, PAIR_DIM), BF16),
            across_scratch(BLOCKS),
            down_scratch(),
            pltpu.VMEM((SHARDS, SHARD_ROWS, D), BF16),
            pltpu.SemaphoreType.DMA((2, BLOCKS)),
            pltpu.SemaphoreType.DMA((BLOCKS + 3,)),
            pltpu.SemaphoreType.DMA((2, D // FINISH)),
        ],
        out_shape=[
            jax.ShapeDtypeStruct((length, D), BF16),
            jax.ShapeDtypeStruct((PAIRS, length, PAIR_DIM), BF16),
        ],
        compiler_params=params(),
        cost_estimate=cost(25),
        name="backward_block",
    )(norms, slope, middle, upstream, attention[0], up[0], down[0])


UNPROJECT = 256


def unproject_kernel(
    row,
    which,
    spot_ref,
    norm_ref,
    grads_ref,
    hidden_ref,
    grad_middle_ref,
    array,
    out_ref,
    grads,
    hidden,
    grad_middle,
    out,
    total,
    weights,
    semaphores,
    load_semaphores,
    store_semaphores,
):
    copy = pltpu.make_async_copy
    tiles = row_tiles(D, UNPROJECT)
    get_weights = [load_qkv(array, row, part, weights, semaphores) for part in range(3)]
    get_grads = [
        [
            copy(
                grads_ref.at[part, :, rows], grads.at[part, :, rows], load_semaphores.at[index, part]
            )
            for part in range(3)
        ]
        for index, rows in enumerate(tiles)
    ]
    get_rest = [
        [
            copy(hidden_ref.at[spot_ref[which], rows], hidden.at[rows], load_semaphores.at[index, 3]),
            copy(grad_middle_ref.at[rows], grad_middle.at[rows], load_semaphores.at[index, 4]),
        ]
        for index, rows in enumerate(tiles)
    ]
    for part in range(3):
        get_weights[part].start()
        get_grads[0][part].start()
    stores = []
    gain = norm_ref[0:1]

    def finish(index, rows):
        for load in get_rest[index]:
            load.wait()
        for part in chunks(rows):
            here = shifted(part, -rows.start)
            back = norm_back(hidden[part].astype(F32), gain, total[index % 2, here])
            out[part] = (grad_middle[part].astype(F32) + back).astype(BF16)
        stores.append(copy(out.at[rows], out_ref.at[0, rows], store_semaphores.at[index]))
        stores[-1].start()

    for index, rows in enumerate(tiles):
        product = None
        for part in range(3):
            if index == 0:
                get_weights[part].wait()
            get_grads[index][part].wait()
            if part == 0:
                following = get_grads[index + 1] if index + 1 < len(tiles) else []
                for load in following + get_rest[index]:
                    load.start()
            term = dot_nt(get_pairs(grads, rows, part), matrix(weights, part))
            product = term if product is None else product + term
        total[index % 2] = product
        if index:
            finish(index - 1, tiles[index - 1])
    finish(len(tiles) - 1, tiles[-1])
    for store in stores:
        store.wait()


def unproject(spot, which, grads, hidden, grad_middle, norms, place):
    length = hidden.shape[1]
    count = D // UNPROJECT
    return pl.pallas_call(
        functools.partial(unproject_kernel, place[1], which),
        in_specs=[SCALARS, IN_VMEM] + [ANY] * 4,
        out_specs=ANY,
        scratch_shapes=[
            pltpu.VMEM((3, PAIRS, D, PAIR_DIM), BF16),
            whole_scratch(BF16),
            whole_scratch(BF16),
            whole_scratch(BF16),
            pltpu.VMEM((2, UNPROJECT, D), F32),
            across_scratch(3),
            pltpu.SemaphoreType.DMA((3,)),
            pltpu.SemaphoreType.DMA((count, 5)),
            pltpu.SemaphoreType.DMA((count,)),
        ],
        out_shape=jax.ShapeDtypeStruct((1, length, D), BF16),
        compiler_params=params(),
        cost_estimate=cost(11),
        name="unproject",
    )(spot, norms, grads, hidden, grad_middle, place[0])


def swap_sections(values):
    return lax.ppermute(values, "section", [(0, 1), (1, 0)])


def per_section(section_index, own):
    other = swap_sections(own)
    is_first = section_index == 0
    return jnp.where(is_first, own, other), jnp.where(is_first, other, own)


def halves(w_qkv, w_out, w_fc, w_proj):
    columns = lambda matrix: jnp.moveaxis(matrix.reshape(SHARD_ROWS, -1, D), 1, 0)
    attention = jnp.concatenate([columns(w_qkv), w_out[None]], axis=0).reshape(2, HALF, D)
    up = columns(w_fc).reshape(2, HALF, D)
    down = w_proj.reshape(2, HALF, D)
    return jnp.stack([attention, up, down], axis=1)


def gather_weights(is_first, w_qkv, w_out, w_fc, w_proj):
    if D // w_qkv.shape[1] == SHARDS:
        own = halves(w_qkv[0], w_out[0], w_fc[0], w_proj[0])
        received = swap_sections(jnp.where(is_first, own[1], own[0]))
        first = jnp.where(is_first, own[0], received)
        last = jnp.where(is_first, received, own[1])
        early = jnp.concatenate([first.reshape(3 * HALF, D), last[0]], axis=0)
        gather = lambda rows: lax.all_gather(rows, ("dp", "section"), axis=0).reshape(
            SHARDS, 2, -1, D
        )
        early, late = gather(early), gather(last[1:].reshape(2 * HALF, D))
    else:
        whole = lambda matrix: lax.all_gather(matrix[0], ("dp", "section"), axis=0)
        every = [whole(matrix) for matrix in (w_qkv, w_out, w_fc, w_proj)]
        layers = []
        for layer in range(2):
            mine = [matrix[layer::2] for matrix in every]
            shards = [matrix.reshape(SHARDS, -1, matrix.shape[-1]) for matrix in mine]
            layers.append(jax.vmap(halves)(*shards).reshape(SHARDS, 2, 3 * HALF, D))
        early = jnp.concatenate([layers[0], layers[1][:, :, :HALF]], axis=2)
        late = layers[1][:, :, HALF:]
    return (
        [(early, 0), (early, HALF), (early, 2 * HALF)],
        [(early, 3 * HALF), (late, 0), (late, HALF)],
    )


def reparam_hidden(table, w_first, b_first):
    return jnp.tanh(jnp.dot(table, w_first, precision=highest_mode) + b_first)


def reparam_out(hidden_units, w_second, b_second):
    return jnp.dot(hidden_units, w_second, precision=highest_mode) + b_second


def sum_dp(values):
    count = lax.axis_size("dp")
    step = 1
    while step < count:
        pairs = [(i, i ^ step) for i in range(count)]
        values = values + lax.ppermute(values, "dp", pairs)
        step *= 2
    return values


def per_device(
    tokens,
    seq_length,
    cotangent,
    ln_gain,
    ln_bias,
    w_qkv,
    w_out,
    w_fc,
    w_proj,
    prefix_table,
    reparam_w1,
    reparam_b1,
    reparam_w2,
    reparam_b2,
):
    section_index = lax.axis_index("section")
    is_first = section_index == 0
    first, last = gather_weights(is_first, w_qkv, w_out, w_fc, w_proj)
    spot = jnp.stack([section_index, jnp.zeros_like(section_index)]).astype(jnp.int32)
    seq = lax.dynamic_slice_in_dim(seq_length, section_index, 1, 0)

    table_values = prefix_table.astype(F32)
    first_weight = reparam_w1.astype(F32)
    first_bias = reparam_b1.astype(F32)
    second_weight = reparam_w2[0].astype(F32)
    second_bias = reparam_b2[0].astype(F32)
    hidden_units = reparam_hidden(table_values, first_weight, first_bias)
    prefix_kv = reparam_out(hidden_units, second_weight, second_bias).astype(BF16)
    pad = ((0, SLOTS - PREFIX), (0, 0))
    small = jnp.concatenate(
        [
            jnp.pad(prefix_kv[:, :D], pad),
            jnp.pad(prefix_kv[:, D:], pad),
            ln_gain[0],
            ln_bias[0],
            jnp.zeros((4, D), BF16),
        ],
        axis=0,
    )
    small_pair = per_section(section_index, small)
    pairs_apart = lambda rows: jnp.moveaxis(rows.reshape(SLOTS, PAIRS, PAIR_DIM), 1, 0)
    prefix_pair = [
        (pairs_apart(part[:SLOTS]), pairs_apart(part[SLOTS : 2 * SLOTS])) for part in small_pair
    ]
    norm_pair = [part[2 * SLOTS :].astype(F32) for part in small_pair]

    prefix_first, prefix_last = prefix_pair
    projected_first = project(spot, 0, tokens, norm_pair[0], first[0])
    attended_first, *probs_first = attend(seq, projected_first, *prefix_first)
    middle_first, normed = middle_block(spot, 0, attended_first, tokens, norm_pair[0], first[0])
    slope, handed = forward_block(normed, middle_first, *first[1:])
    projected = project(spot, 1, handed, norm_pair[1], last[0])
    attended, *probs = attend(seq, projected, *prefix_last)
    middle, normed = middle_block(spot, 1, attended, handed, norm_pair[1], last[0])
    final, grad_middle, grad_attended = turn_block(
        spot, normed, middle, cotangent, norm_pair[1], *last
    )
    grads, dkp_last, dvp_last = attend_back(
        seq, projected, attended, grad_attended, *prefix_last, *probs
    )
    grad_handed = unproject(spot, 1, grads, handed, grad_middle, norm_pair[1], last[0])
    grad_middle, grad_attended = backward_block(
        grad_handed, slope, middle_first, norm_pair[0], *first
    )
    grads, dkp_first, dvp_first = attend_back(
        seq, projected_first, attended_first, grad_attended, *prefix_first, *probs_first
    )
    grad_tokens = unproject(spot, 0, grads, tokens, grad_middle, norm_pair[0], first[0])

    def gathered_rows(first, last):
        kept = jnp.where(is_first, first, last)
        received = swap_sections(jnp.where(is_first, last, first))
        return jnp.concatenate(
            [jnp.where(is_first, kept, received), jnp.where(is_first, received, kept)], axis=0
        )

    activations = gathered_rows(handed, final)
    input_grads = gathered_rows(grad_tokens, grad_handed)

    pairs_joined = lambda rows: jnp.moveaxis(rows[:, :PREFIX], 0, 1).reshape(PREFIX, D)
    grad_first = jnp.concatenate([pairs_joined(dkp_first), pairs_joined(dvp_first)], axis=1)
    grad_last = jnp.concatenate([pairs_joined(dkp_last), pairs_joined(dvp_last)], axis=1)
    kept = jnp.where(is_first, grad_first, grad_last)
    received = swap_sections(jnp.where(is_first, grad_last, grad_first))
    prefix_total = sum_dp(kept + received)

    grad_hidden, grad_w2, grad_b2 = jax.vjp(reparam_out, hidden_units, second_weight, second_bias)[
        1
    ](prefix_total)
    grad_hidden = grad_hidden + swap_sections(grad_hidden)
    grad_table, grad_w1, grad_b1 = jax.vjp(reparam_hidden, table_values, first_weight, first_bias)[
        1
    ](grad_hidden)
    return (
        activations[None],
        input_grads[None],
        grad_table,
        grad_w1,
        grad_b1,
        grad_w2[None],
        grad_b2[None],
    )


def solution(mesh):
    in_specs = (
        P("dp", None, None),
        P("dp"),
        P("dp", None, None),
        P("section", None, None),
        P("section", None, None),
        P("section", "dp", None),
        P("section", "dp", None),
        P("section", "dp", None),
        P("section", "dp", None),
        P(),
        P(),
        P(),
        P("section", None, None),
        P("section", None),
    )
    out_specs = (
        P("section", "dp", None, None),
        P("section", "dp", None, None),
        P(),
        P(),
        P(),
        P("section", None, None),
        P("section", None),
    )
    return jax.shard_map(
        per_device, mesh=mesh, in_specs=in_specs, out_specs=out_specs, check_vma=False
    )
```

```python
import functools

import jax
import jax.numpy as jnp
from jax import lax
from jax.experimental import pallas as pl
from jax.experimental.pallas import tpu as pltpu
from jax.sharding import PartitionSpec as P

D = 1024
HEADS = 16
HEAD_DIM = 64
FF = 4096
PREFIX = 10
SLOTS = 16
BOTH = 24
PAIRS = 8
PAIR_DIM = 128
BLOCK = 256

eps_norm = 1e-05
neg_big = -1e30
highest_mode = lax.Precision.HIGHEST
VMEM_BYTES = 62 * 2**20
F32 = jnp.float32
BF16 = jnp.bfloat16


def dot(left, right, dims):
    return lax.dot_general(left, right, (dims, ((), ())), preferred_element_type=F32)


def dot_nn(left, right):
    return dot(left, right, ((1,), (0,)))


def dot_nt(left, right):
    return dot(left, right, ((1,), (1,)))


def dot_tn(left, right):
    return dot(left, right, ((0,), (0,)))


def normalised(values):
    centre = jnp.mean(values, axis=-1, keepdims=True)
    spread = values - centre
    variance = jnp.mean(spread * spread, axis=-1, keepdims=True)
    inverse = lax.rsqrt(variance + eps_norm)
    return spread * inverse, inverse


def layer_norm(values, gain, offset):
    return normalised(values)[0] * gain + offset


def norm_back(values, gain, upstream):
    unit, inverse = normalised(values)
    scaled = upstream * gain
    mean_scaled = jnp.mean(scaled, axis=-1, keepdims=True)
    mean_unit = jnp.mean(scaled * unit, axis=-1, keepdims=True)
    return (scaled - mean_scaled - unit * mean_unit) * inverse


SQRT_2_PI = 0.7978845608028654
CUBIC = 0.044715


def gelu_pair(values):
    cubic_part = (SQRT_2_PI * CUBIC) * (values * values)
    half_tanh = 0.5 + 0.5 * jnp.tanh(values * (SQRT_2_PI + cubic_part))
    out = values * half_tanh
    slope = half_tanh + out * ((2.0 - 2.0 * half_tanh) * (SQRT_2_PI + 3.0 * cubic_part))
    return out, slope


def params(**kwargs):
    return pltpu.CompilerParams(vmem_limit_bytes=VMEM_BYTES, **kwargs)


def cost(micros):
    return pl.CostEstimate(flops=int(micros * 1.15e9), bytes_accessed=2**20, transcendentals=0)


SHARDS = 16
HALF = 128
SHARD_ROWS = 64
BLOCKS = FF // D


def load_across(array, half, row, target, semaphore):
    return pltpu.make_async_copy(array.at[:, half, pl.ds(row, SHARD_ROWS)], target, semaphore)


def load_qkv(array, row, part, weights, semaphores):
    half, inner = divmod(part, 2)
    return load_across(
        array, half, row + inner * SHARD_ROWS, weights.at[part], semaphores.at[part]
    )


def load_out(array, row, target, semaphore):
    return load_across(array, 1, row + SHARD_ROWS, target, semaphore)


def load_up(array, row, block, target, semaphore):
    half, inner = divmod(block, 2)
    return load_across(array, half, row + inner * SHARD_ROWS, target, semaphore)


def load_down(array, row, block, target, semaphore):
    few = SHARDS // BLOCKS
    return pltpu.make_async_copy(
        array.at[pl.ds(block * few, few), :, pl.ds(row, HALF)], target, semaphore
    )


def across_scratch(count):
    return pltpu.VMEM((count, SHARDS, SHARD_ROWS, D), BF16)


def down_scratch():
    return pltpu.VMEM((BLOCKS, SHARDS // BLOCKS, 2, HALF, D), BF16)


def matrix(ref, *index):
    return ref[index].reshape(D, D) if index else ref[...].reshape(D, D)


ANY = pl.BlockSpec(memory_space=pl.ANY)


def once(shape, index):
    return pl.BlockSpec(shape, index, pipeline_mode=pl.Buffered(1))


def row_tiles(length, size):
    return [slice(start, start + size) for start in range(0, length, size)]


CHUNK = 16


def put_pairs(ref, rows, values):
    for pair in range(PAIRS):
        ref[pair, rows] = values[:, pair * PAIR_DIM : (pair + 1) * PAIR_DIM]


def get_pairs(ref, rows, *lead):
    return jnp.concatenate([ref[(*lead, pair, rows)] for pair in range(PAIRS)], axis=1)


def chunks(rows, size=CHUNK):
    return [slice(start, start + size) for start in range(rows.start, rows.stop, size)]


def shifted(rows, by):
    return slice(rows.start + by, rows.stop + by)


def qkv_kernel(row, spot_ref, hidden_ref, norm_ref, array, out_ref, normed, weights, semaphores):
    step = pl.program_id(0)
    loads = [load_qkv(array, row, part, weights, semaphores) for part in range(3)]
    length = hidden_ref.shape[1]
    tiles = row_tiles(length, 512)

    @pl.when(step == 0)
    def _():
        loads[0].start()
        gain, offset = norm_ref[0:1], norm_ref[2:3]
        for rows in chunks(slice(0, length)):
            values = hidden_ref[0, rows].astype(F32)
            normed[rows] = layer_norm(values, gain, offset).astype(BF16)
        loads[0].wait()
        loads[1].start()
        loads[2].start()
        for rows in tiles:
            queries = dot_nn(normed[rows], matrix(weights, 0))
            put_pairs(out_ref, rows, (queries * HEAD_DIM**-0.5).astype(BF16))

    for part in (1, 2):

        @pl.when(step == part)
        def _(part=part):
            loads[part].wait()
            for rows in tiles:
                put_pairs(out_ref, rows, dot_nn(normed[rows], matrix(weights, part)).astype(BF16))


def project(spot, which, hidden, norms, place):
    length = hidden.shape[1]
    return pl.pallas_call(
        functools.partial(qkv_kernel, place[1]),
        grid_spec=pltpu.PrefetchScalarGridSpec(
            num_scalar_prefetch=1,
            grid=(3,),
            in_specs=[
                once((1, length, D), lambda j, s: (s[which], 0, 0)),
                once((8, D), lambda j, s: (0, 0)),
                ANY,
            ],
            out_specs=pl.BlockSpec((PAIRS, length, PAIR_DIM), lambda j, s: (j, 0, 0)),
            scratch_shapes=[
                pltpu.VMEM((length, D), BF16),
                across_scratch(3),
                pltpu.SemaphoreType.DMA((3,)),
            ],
        ),
        out_shape=jax.ShapeDtypeStruct((3 * PAIRS, length, PAIR_DIM), BF16),
        compiler_params=params(),
        cost_estimate=cost(12),
        name="norm_project",
    )(spot, hidden, norms, place[0])


def lane_halves(block):
    lanes = lax.broadcasted_iota(jnp.int32, block.shape, 1)
    zero = jnp.zeros_like(block)
    return jnp.where(lanes < HEAD_DIM, block, zero), jnp.where(lanes < HEAD_DIM, zero, block)


def key_spans(first, stop):
    if first == 0:
        return [slice(0, SLOTS + stop)]
    return [slice(0, SLOTS), slice(SLOTS + first, SLOTS + stop)]


def read_spans(ref, spans, *rest):
    parts = [ref[(span, *rest)] for span in spans]
    return parts[0] if len(parts) == 1 else jnp.concatenate(parts, axis=0)


def cut_spans(values, spans):
    start = 0
    for span in spans:
        size = span.stop - span.start
        yield span, values[start : start + size]
        start += size


def strips(length, short):
    return [
        (rows, slice(2 * rows.start, 2 * rows.stop), rows.start if short else 0)
        for rows in row_tiles(length, BLOCK)
    ]


def stacked_halves(block):
    return jnp.concatenate(lane_halves(block), axis=0)


def own_heads(product):
    return jnp.concatenate([product[:HEAD_DIM, :BLOCK], product[HEAD_DIM:, BLOCK:]], axis=0)


def either_length(length_ref, length, run):
    short = length_ref[0] < length
    pl.when(short)(lambda: run(True))
    pl.when(jnp.logical_not(short))(lambda: run(False))


def allowed(rows, first_diagonal):
    shape = (rows.stop - rows.start, 2 * BLOCK)
    keys = lax.broadcasted_iota(jnp.int32, shape, 0) + rows.start
    if rows.stop <= SLOTS:
        return keys < PREFIX
    queries = lax.broadcasted_iota(jnp.int32, shape, 1) % BLOCK
    return keys - first_diagonal <= queries


def eight_rows(values, reduce):
    return reduce(values.reshape(-1, 8, values.shape[-1]), axis=0)


def attend_kernel(
    seq_ref, q_ref, k_ref, v_ref, kp_ref, vp_ref, out_ref, probs_ref, scale_ref, keys, values_t, scores
):
    length = q_ref.shape[1]
    keys[:SLOTS], keys[SLOTS:] = kp_ref[0], k_ref[0]
    values_t[...] = v_ref[0].T
    prefix_values = vp_ref[0]

    def run(short):
        def scored(strip, slot):
            rows, _, first = strip
            count = SLOTS + rows.stop - first
            scores[slot, :count] = dot_nt(
                read_spans(keys, key_spans(first, rows.stop)), stacked_halves(q_ref[0, rows])
            )

        todo = strips(length, short)
        scored(todo[0], 0)
        for index, (rows, columns, first) in enumerate(todo):
            slot = index % 2
            if index + 1 < len(todo):
                scored(todo[index + 1], 1 - slot)
            count = SLOTS + rows.stop - first
            parts = chunks(slice(0, count))
            top = None
            for part in parts:
                values = scores[slot, part]
                if part.stop <= SLOTS or part.start >= count - BLOCK:
                    values = jnp.where(allowed(part, count - BLOCK), values, neg_big)
                    scores[slot, part] = values
                values = eight_rows(values, jnp.max)
                top = values if top is None else jnp.maximum(top, values)
            top = jnp.max(top, axis=0, keepdims=True)
            total = None
            for part in parts:
                values = jnp.exp(scores[slot, part] - top)
                place = part if part.stop <= SLOTS else shifted(part, first)
                probs_ref[0, place, columns] = values.astype(BF16)
                values = eight_rows(values, jnp.sum)
                total = values if total is None else total + values
            inverse = 1.0 / jnp.sum(total, axis=0, keepdims=True)
            both = dot_nn(
                values_t[:, first : rows.stop],
                probs_ref[0, SLOTS + first : SLOTS + rows.stop, columns],
            ) + dot_tn(prefix_values, probs_ref[0, :SLOTS, columns])
            inverse = jnp.concatenate(
                [
                    jnp.broadcast_to(inverse[:, :BLOCK], (HEAD_DIM, BLOCK)),
                    jnp.broadcast_to(inverse[:, BLOCK:], (HEAD_DIM, BLOCK)),
                ],
                axis=0,
            )
            out_ref[0, rows] = (own_heads(both) * inverse).T.astype(BF16)
            scale_ref[0, rows] = inverse.T

    either_length(seq_ref, length, run)


def pair_spec(length, part):
    return pl.BlockSpec((1, length, PAIR_DIM), lambda p, s: (part * PAIRS + p, 0, 0))


def probs_spec(length):
    return pl.BlockSpec((1, SLOTS + length, 2 * length), lambda p, s: (p, 0, 0))


def attend(seq, projected, prefix_keys, prefix_values):
    length = projected.shape[1]
    return pl.pallas_call(
        attend_kernel,
        grid_spec=pltpu.PrefetchScalarGridSpec(
            num_scalar_prefetch=1,
            grid=(PAIRS,),
            in_specs=[
                pair_spec(length, 0),
                pair_spec(length, 1),
                pair_spec(length, 2),
                pair_spec(SLOTS, 0),
                pair_spec(SLOTS, 0),
            ],
            out_specs=[pair_spec(length, 0), probs_spec(length), pair_spec(length, 0)],
            scratch_shapes=[
                pltpu.VMEM((SLOTS + length, PAIR_DIM), BF16),
                pltpu.VMEM((PAIR_DIM, length), BF16),
                pltpu.VMEM((2, SLOTS + length, 2 * BLOCK), F32),
            ],
        ),
        out_shape=[
            jax.ShapeDtypeStruct((PAIRS, length, PAIR_DIM), BF16),
            jax.ShapeDtypeStruct((PAIRS, SLOTS + length, 2 * length), BF16),
            jax.ShapeDtypeStruct((PAIRS, length, PAIR_DIM), F32),
        ],
        compiler_params=params(),
        cost_estimate=cost(30),
        name="attend",
    )(seq, projected, projected, projected, prefix_keys, prefix_values)


def attend_back_kernel(
    seq_ref,
    q_ref,
    k_ref,
    v_ref,
    out_ref,
    grad_ref,
    kp_ref,
    vp_ref,
    probs_ref,
    scale_ref,
    grads_ref,
    prefix_ref,
    values,
    keys_t,
    dk,
    dv,
    dprobs,
    ds,
):
    length = q_ref.shape[1]
    values[:SLOTS], values[SLOTS:] = vp_ref[0], v_ref[0]
    keys_t[...] = k_ref[0].T
    prefix_keys = kp_ref[0]
    dk[...] = jnp.zeros_like(dk)
    dv[...] = jnp.zeros_like(dv)

    def run(short):
        def prepared(strip, slot):
            rows, _, first = strip
            grads = (grad_ref[0, rows].astype(F32) * scale_ref[0, rows]).astype(BF16)
            halves = stacked_halves(grads)
            weighted_t = (grads.astype(F32) * out_ref[0, rows].astype(F32)).T
            centre = jnp.concatenate(
                [
                    jnp.sum(weighted_t[:HEAD_DIM], axis=0, keepdims=True),
                    jnp.sum(weighted_t[HEAD_DIM:], axis=0, keepdims=True),
                ],
                axis=1,
            )
            dprobs[slot, : SLOTS + rows.stop - first] = dot_nt(
                read_spans(values, key_spans(first, rows.stop)), halves
            )
            return halves, centre

        todo = strips(length, short)
        ahead = prepared(todo[0], 0)
        for index, (rows, columns, first) in enumerate(todo):
            slot = index % 2
            spans = key_spans(first, rows.stop)
            grad_halves, centre = ahead
            if index + 1 < len(todo):
                ahead = prepared(todo[index + 1], 1 - slot)
            count = SLOTS + rows.stop - first
            for part in chunks(slice(0, count)):
                place = part if part.stop <= SLOTS else shifted(part, first)
                probs = probs_ref[0, place, columns].astype(F32)
                ds[slot, part] = (probs * (dprobs[slot, part] - centre)).astype(BF16)
            for total, left, right in (
                (dv, read_spans(probs_ref.at[0], spans, columns), grad_halves),
                (dk, ds[slot, :count], stacked_halves(q_ref[0, rows])),
            ):
                for span, part in cut_spans(dot_nn(left, right), spans):
                    total[span] += part
            both = dot_nn(keys_t[:, first : rows.stop], ds[slot, SLOTS:count]) + dot_tn(
                prefix_keys, ds[slot, :SLOTS]
            )
            grads_ref[0, 0, rows] = (own_heads(both).T * HEAD_DIM**-0.5).astype(BF16)

    either_length(seq_ref, length, run)
    grads_ref[1, 0] = dk[SLOTS:].astype(BF16)
    grads_ref[2, 0] = dv[SLOTS:].astype(BF16)
    prefix_ref[0, :PREFIX] = dk[:PREFIX]
    prefix_ref[0, PREFIX : 2 * PREFIX] = dv[:PREFIX]
    prefix_ref[0, 2 * PREFIX :] = jnp.zeros_like(prefix_ref[0, 2 * PREFIX :])


def attend_back(seq, projected, attended, grad_attended, prefix_keys, prefix_values, probs, scale):
    length = projected.shape[1]
    ext = (SLOTS + length, PAIR_DIM)
    return pl.pallas_call(
        attend_back_kernel,
        grid_spec=pltpu.PrefetchScalarGridSpec(
            num_scalar_prefetch=1,
            grid=(PAIRS,),
            in_specs=[
                pair_spec(length, 0),
                pair_spec(length, 1),
                pair_spec(length, 2),
                pair_spec(length, 0),
                pair_spec(length, 0),
                pair_spec(SLOTS, 0),
                pair_spec(SLOTS, 0),
                probs_spec(length),
                pair_spec(length, 0),
            ],
            out_specs=[
                pl.BlockSpec((3, 1, length, PAIR_DIM), lambda p, s: (0, p, 0, 0)),
                pair_spec(BOTH, 0),
            ],
            scratch_shapes=[
                pltpu.VMEM(ext, BF16),
                pltpu.VMEM((PAIR_DIM, length), BF16),
                pltpu.VMEM(ext, F32),
                pltpu.VMEM(ext, F32),
                pltpu.VMEM((2, SLOTS + length, 2 * BLOCK), F32),
                pltpu.VMEM((2, SLOTS + length, 2 * BLOCK), BF16),
            ],
        ),
        out_shape=[
            jax.ShapeDtypeStruct((3, PAIRS, length, PAIR_DIM), BF16),
            jax.ShapeDtypeStruct((PAIRS, BOTH, PAIR_DIM), F32),
        ],
        compiler_params=params(),
        cost_estimate=cost(30),
        name="attend_back",
    )(
        seq,
        projected,
        projected,
        projected,
        attended,
        grad_attended,
        prefix_keys,
        prefix_values,
        probs,
        scale,
    )


def middle_kernel(row, spot_ref, attended_ref, hidden_ref, norm_ref, array, middle_ref, normed_ref, weights, semaphores):
    step = pl.program_id(0)
    load = load_out(array, row, weights.at[0], semaphores.at[0])

    @pl.when(step == 0)
    def _():
        load.start()
        load.wait()

    middle_ref[...] = dot_nn(get_pairs(attended_ref, slice(None)), matrix(weights, 0))
    gain, offset = norm_ref[1:2], norm_ref[3:4]
    for rows in chunks(slice(0, middle_ref.shape[0])):
        middle = hidden_ref[0, rows].astype(F32) + middle_ref[rows]
        middle_ref[rows] = middle
        normed_ref[rows] = layer_norm(middle, gain, offset).astype(BF16)


def middle_block(spot, which, attended, hidden, norms, place):
    length = attended.shape[1]
    tile = pl.BlockSpec((256, D), lambda m, s: (m, 0))
    return pl.pallas_call(
        functools.partial(middle_kernel, place[1]),
        grid_spec=pltpu.PrefetchScalarGridSpec(
            num_scalar_prefetch=1,
            grid=(length // 256,),
            in_specs=[
                pl.BlockSpec((PAIRS, 256, PAIR_DIM), lambda m, s: (0, m, 0)),
                pl.BlockSpec((1, 256, D), lambda m, s: (s[which], m, 0)),
                once((8, D), lambda m, s: (0, 0)),
                ANY,
            ],
            out_specs=[tile, tile],
            scratch_shapes=[across_scratch(1), pltpu.SemaphoreType.DMA((1,))],
        ),
        out_shape=[
            jax.ShapeDtypeStruct((length, D), F32),
            jax.ShapeDtypeStruct((length, D), BF16),
        ],
        compiler_params=params(),
        cost_estimate=cost(5),
        name="middle_block",
    )(spot, attended, hidden, norms, place[0])


def feed_forward_loads(up, down, rows, up_weights, down_weights, semaphores):
    return [
        (
            load_up(up, rows[0], block, up_weights.at[block], semaphores.at[0, block]),
            load_down(down, rows[1], block, down_weights.at[block], semaphores.at[1, block]),
        )
        for block in range(BLOCKS)
    ]


def start_all(loads):
    for pair in loads:
        for load in pair:
            load.start()


def wait_step(loads, step):
    for block, pair in enumerate(loads):

        @pl.when(step == block)
        def _(pair=pair):
            for load in pair:
                load.wait()


def wait_for(target, semaphore):
    pltpu.make_async_copy(target, target, semaphore).wait()


def feed_forward_scratch():
    return [across_scratch(BLOCKS), down_scratch(), pltpu.SemaphoreType.DMA((2, BLOCKS))]


def forward_kernel(
    rows_at,
    normed_ref,
    middle_ref,
    up,
    down,
    slope_ref,
    out_ref,
    total,
    inner,
    activated,
    up_weights,
    down_weights,
    semaphores,
):
    step = pl.program_id(0)
    tiles = row_tiles(middle_ref.shape[0], TILE)
    loads = feed_forward_loads(up, down, rows_at, up_weights, down_weights, semaphores)

    @pl.when(step == 0)
    def _():
        start_all(loads[:1])
        total[...] = middle_ref[...]

    wait_step(loads, step)
    for later in range(1, BLOCKS):
        pl.when(step == later - 1)(lambda later=later: start_all(loads[later : later + 1]))
    w_fc, w_proj = matrix(up_weights, step), matrix(down_weights, step)
    inner[tiles[0]] = dot_nn(normed_ref[tiles[0]], w_fc)
    for index, rows in enumerate(tiles):
        if index + 1 < len(tiles):
            inner[tiles[index + 1]] = dot_nn(normed_ref[tiles[index + 1]], w_fc)
        for part in chunks(rows):
            value, slope = gelu_pair(inner[part])
            activated[part] = value.astype(BF16)
            slope_ref[part] = slope.astype(BF16)
        total[rows] += dot_nn(activated[rows], w_proj)

    @pl.when(step == pl.num_programs(0) - 1)
    def _():
        out_ref[0] = total[...].astype(BF16)


def forward_block(normed, middle, up, down):
    length = normed.shape[0]
    whole = lambda j: (0, 0)
    return pl.pallas_call(
        functools.partial(forward_kernel, (up[1], down[1])),
        grid=(BLOCKS,),
        in_specs=[once((length, D), whole), once((length, D), whole), ANY, ANY],
        out_specs=[
            pl.BlockSpec((length, D), lambda j: (0, j)),
            once((1, length, D), lambda j: (0, 0, 0)),
        ],
        scratch_shapes=[whole_scratch(F32), whole_scratch(F32), whole_scratch(BF16)]
        + feed_forward_scratch(),
        out_shape=[
            jax.ShapeDtypeStruct((length, FF), BF16),
            jax.ShapeDtypeStruct((1, length, D), BF16),
        ],
        compiler_params=params(),
        cost_estimate=cost(25),
        name="forward_block",
    )(normed, middle, up[0], down[0])


FINISH = 256


def finish_backward(upstream, middle, grad_total, norm_ref, w_out, grad_middle, grad_attended, stores):
    gain = norm_ref[1:2]
    for index, rows in enumerate(row_tiles(D, FINISH)):
        for part in chunks(rows):
            grad = upstream[part].astype(F32) + norm_back(middle[part], gain, grad_total[part])
            grad_middle[part] = grad.astype(BF16)
        put_pairs(grad_attended, rows, dot_nt(grad_middle[rows], w_out).astype(BF16))
        for store in stores(rows, index):
            store.start()
    for index, rows in enumerate(row_tiles(D, FINISH)):
        for store in stores(rows, index):
            store.wait()


def turn_kernel(
    rows_at,
    spot_ref,
    norm_ref,
    normed_ref,
    middle_ref,
    upstream_ref,
    hidden_ref,
    attention,
    up,
    down,
    out_ref,
    sent_ref,
    grad_middle_ref,
    grad_attended_ref,
    normed,
    middle,
    upstream,
    total,
    grad_total,
    inner,
    grad_act,
    out,
    grad_middle,
    grad_attended,
    up_weights,
    down_weights,
    out_weights,
    semaphores,
    load_semaphores,
    store_semaphores,
):
    activated, grad_inner = grad_middle, out
    loads = feed_forward_loads(up, down, rows_at[1:], up_weights, down_weights, semaphores)
    copy = pltpu.make_async_copy
    get_normed = copy(normed_ref, normed, load_semaphores.at[0])
    get_upstream = copy(upstream_ref.at[spot_ref[0]], upstream, load_semaphores.at[1])
    get_middle = copy(middle_ref, middle, load_semaphores.at[2])
    get_out = load_out(attention, rows_at[0], out_weights, load_semaphores.at[3])
    get_normed.start()
    loads[0][0].start()
    total[...] = jnp.zeros_like(total)
    grad_total[...] = jnp.zeros_like(grad_total)
    get_normed.wait()
    get_upstream.start()
    loads[0][1].start()

    def step(block, carry):
        wait_for(up_weights.at[block], semaphores.at[0, block])
        tiles = row_tiles(D, TILE)
        w_fc = matrix(up_weights, block)
        inner[0] = dot_nn(normed[tiles[0]], w_fc)
        pl.when(block == 0)(get_upstream.wait)
        wait_for(down_weights.at[block], semaphores.at[1, block])
        w_proj = matrix(down_weights, block)
        for later in range(1, BLOCKS):
            pl.when(block == later - 1)(lambda later=later: start_all(loads[later : later + 1]))

        @pl.when(block == BLOCKS - 1)
        def _():
            get_middle.start()
            get_out.start()

        grad_act[0] = dot_nt(upstream[tiles[0]], w_proj)
        for index, rows in enumerate(tiles):
            slot = index % 2
            if index + 1 < len(tiles):
                inner[1 - slot] = dot_nn(normed[tiles[index + 1]], w_fc)
                grad_act[1 - slot] = dot_nt(upstream[tiles[index + 1]], w_proj)
            for part in chunks(rows):
                here = shifted(part, -rows.start)
                value, slope = gelu_pair(inner[slot, here])
                activated[part] = value.astype(BF16)
                grad_inner[part] = (grad_act[slot, here] * slope).astype(BF16)
            total[rows] += dot_nn(activated[rows], w_proj)
            grad_total[rows] += dot_nt(grad_inner[rows], w_fc)
        return carry

    lax.fori_loop(0, BLOCKS, step, 0)
    get_middle.wait()
    for part in chunks(slice(0, D)):
        out[part] = (total[part] + middle[part]).astype(BF16)
    put_out = copy(out, out_ref.at[0], store_semaphores.at[0, 0])
    put_out.start()
    put_sent = copy(out, sent_ref.at[0], store_semaphores.at[0, 1])
    get_hidden = copy(hidden_ref.at[0], normed, load_semaphores.at[4])
    put_hidden = copy(normed, sent_ref.at[0], store_semaphores.at[0, 1])
    pl.when(spot_ref[0] == 0)(put_sent.start)
    pl.when(spot_ref[0] != 0)(get_hidden.start)
    get_out.wait()

    def stores(rows, index):
        return (
            copy(grad_middle.at[rows], grad_middle_ref.at[rows], store_semaphores.at[1, index]),
            copy(grad_attended.at[:, rows], grad_attended_ref.at[:, rows], store_semaphores.at[2, index]),
        )

    finish_backward(
        upstream, middle, grad_total, norm_ref, matrix(out_weights), grad_middle, grad_attended, stores
    )
    put_out.wait()

    @pl.when(spot_ref[0] != 0)
    def _():
        get_hidden.wait()
        put_hidden.start()

    put_sent.wait()


TILE = 512
SCALARS = pl.BlockSpec(memory_space=pltpu.SMEM)
IN_VMEM = pl.BlockSpec(memory_space=pltpu.VMEM)


def whole_scratch(dtype):
    return pltpu.VMEM((D, D), dtype)


def turn_block(spot, normed, middle, upstream, hidden, norms, attention, up, down):
    length = normed.shape[0]
    return pl.pallas_call(
        functools.partial(turn_kernel, (attention[1], up[1], down[1])),
        in_specs=[SCALARS, IN_VMEM] + [ANY] * 7,
        out_specs=[ANY] * 4,
        scratch_shapes=[
            whole_scratch(BF16),
            whole_scratch(F32),
            whole_scratch(BF16),
            whole_scratch(F32),
            whole_scratch(F32),
            pltpu.VMEM((2, TILE, D), F32),
            pltpu.VMEM((2, TILE, D), F32),
            whole_scratch(BF16),
            whole_scratch(BF16),
            pltpu.VMEM((PAIRS, D, PAIR_DIM), BF16),
            across_scratch(BLOCKS),
            down_scratch(),
            pltpu.VMEM((SHARDS, SHARD_ROWS, D), BF16),
            pltpu.SemaphoreType.DMA((2, BLOCKS)),
            pltpu.SemaphoreType.DMA((5,)),
            pltpu.SemaphoreType.DMA((3, D // FINISH)),
        ],
        out_shape=[
            jax.ShapeDtypeStruct((1, length, D), BF16),
            jax.ShapeDtypeStruct((1, length, D), BF16),
            jax.ShapeDtypeStruct((length, D), BF16),
            jax.ShapeDtypeStruct((PAIRS, length, PAIR_DIM), BF16),
        ],
        compiler_params=params(),
        cost_estimate=cost(42),
        name="turn_block",
    )(spot, norms, normed, middle, upstream, hidden, attention[0], up[0], down[0])


def backward_kernel(
    rows_at,
    spot_ref,
    norm_ref,
    slope_ref,
    middle_ref,
    upstream_ref,
    first_ref,
    last_ref,
    received_ref,
    attention,
    up,
    down,
    activations_ref,
    grad_middle_ref,
    grad_attended_ref,
    slope,
    middle,
    upstream,
    grad_total,
    grad_act,
    grad_middle,
    grad_attended,
    up_weights,
    down_weights,
    out_weights,
    semaphores,
    load_semaphores,
    store_semaphores,
    activations,
    output_semaphores,
):
    grad_inner = grad_middle
    section = spot_ref[0]
    loads = feed_forward_loads(up, down, rows_at[1:], up_weights, down_weights, semaphores)
    copy = pltpu.make_async_copy
    get_upstream = copy(upstream_ref.at[0], upstream, load_semaphores.at[BLOCKS])
    get_middle = copy(middle_ref, middle, load_semaphores.at[BLOCKS + 1])
    get_out = load_out(attention, rows_at[0], out_weights, load_semaphores.at[BLOCKS + 2])
    take = copy(received_ref.at[0], activations.at[1 - section], output_semaphores.at[0])
    keep_first = copy(first_ref.at[0], activations.at[section], output_semaphores.at[1])
    keep_last = copy(last_ref.at[0], activations.at[section], output_semaphores.at[1])
    put_activations = copy(activations, activations_ref, output_semaphores.at[2])
    get_slopes = [
        copy(slope_ref.at[:, pl.ds(block * D, D)], slope.at[block], load_semaphores.at[block])
        for block in range(BLOCKS)
    ]
    get_upstream.start()
    loads[0][1].start()
    grad_total[...] = jnp.zeros_like(grad_total)
    get_upstream.wait()
    get_slopes[0].start()
    loads[0][0].start()

    def step(block, carry):
        wait_for(down_weights.at[block], semaphores.at[1, block])
        w_proj = matrix(down_weights, block)
        tiles = row_tiles(D, TILE)
        grad_act[tiles[0]] = dot_nt(upstream[tiles[0]], w_proj)
        wait_for(slope.at[block], load_semaphores.at[block])
        wait_for(up_weights.at[block], semaphores.at[0, block])
        w_fc = matrix(up_weights, block)
        for later in range(1, BLOCKS):

            @pl.when(block == later - 1)
            def _(later=later):
                loads[later][1].start()
                get_slopes[later].start()
                loads[later][0].start()

        @pl.when(block == BLOCKS - 1)
        def _():
            get_middle.start()
            get_out.start()

        @pl.when(block == 1)
        def _():
            take.start()
            pl.when(section == 0)(keep_first.start)
            pl.when(section != 0)(keep_last.start)

        @pl.when(block == 2)
        def _():
            take.wait()
            keep_first.wait()
            put_activations.start()

        for index, rows in enumerate(tiles):
            if index + 1 < len(tiles):
                grad_act[tiles[index + 1]] = dot_nt(upstream[tiles[index + 1]], w_proj)
            for part in chunks(rows):
                grad_inner[part] = (grad_act[part] * slope[block, part].astype(F32)).astype(BF16)
            grad_total[rows] += dot_nt(grad_inner[rows], w_fc)
        return carry

    lax.fori_loop(0, BLOCKS, step, 0)
    get_middle.wait()
    get_out.wait()

    def stores(rows, index):
        return (
            copy(grad_middle.at[rows], grad_middle_ref.at[rows], store_semaphores.at[0, index]),
            copy(grad_attended.at[:, rows], grad_attended_ref.at[:, rows], store_semaphores.at[1, index]),
        )

    finish_backward(
        upstream, middle, grad_total, norm_ref, matrix(out_weights), grad_middle, grad_attended, stores
    )
    put_activations.wait()


def backward_block(spot, upstream, slope, middle, outputs, norms, attention, up, down):
    length = middle.shape[0]
    return pl.pallas_call(
        functools.partial(backward_kernel, (attention[1], up[1], down[1])),
        in_specs=[SCALARS, IN_VMEM] + [ANY] * 9,
        out_specs=[ANY] * 3,
        scratch_shapes=[
            pltpu.VMEM((BLOCKS, D, D), BF16),
            whole_scratch(F32),
            whole_scratch(BF16),
            whole_scratch(F32),
            whole_scratch(F32),
            whole_scratch(BF16),
            pltpu.VMEM((PAIRS, D, PAIR_DIM), BF16),
            across_scratch(BLOCKS),
            down_scratch(),
            pltpu.VMEM((SHARDS, SHARD_ROWS, D), BF16),
            pltpu.SemaphoreType.DMA((2, BLOCKS)),
            pltpu.SemaphoreType.DMA((BLOCKS + 3,)),
            pltpu.SemaphoreType.DMA((2, D // FINISH)),
            pltpu.VMEM((2, D, D), BF16),
            pltpu.SemaphoreType.DMA((3,)),
        ],
        out_shape=[
            jax.ShapeDtypeStruct((2, length, D), BF16),
            jax.ShapeDtypeStruct((length, D), BF16),
            jax.ShapeDtypeStruct((PAIRS, length, PAIR_DIM), BF16),
        ],
        compiler_params=params(),
        cost_estimate=cost(25),
        name="backward_block",
    )(spot, norms, slope, middle, upstream, *outputs, attention[0], up[0], down[0])


UNPROJECT = 256


def unproject_kernel(
    row,
    which,
    spot_ref,
    norm_ref,
    grads_ref,
    hidden_ref,
    grad_middle_ref,
    array,
    *refs,
):
    last = (*refs[:3], *refs[-2:]) if len(refs) > 10 else None
    out_ref, *refs = (refs[3:5], *refs[5:-2]) if last else refs
    unproject_body(
        row, which, spot_ref, norm_ref, grads_ref, hidden_ref, grad_middle_ref, array, last, out_ref, *refs
    )


def unproject_body(
    row,
    which,
    spot_ref,
    norm_ref,
    grads_ref,
    hidden_ref,
    grad_middle_ref,
    array,
    last,
    out_ref,
    grads,
    hidden,
    grad_middle,
    out,
    total,
    weights,
    semaphores,
    load_semaphores,
    store_semaphores,
):
    copy = pltpu.make_async_copy
    tiles = row_tiles(D, UNPROJECT)
    if last:
        kept_ref, received_ref, outputs_ref, rows_of_two, last_semaphores = last
        get_others = [
            copy(received_ref.at[0], rows_of_two.at[0], last_semaphores.at[0]),
            copy(kept_ref.at[0], rows_of_two.at[1], last_semaphores.at[1]),
        ]
        put_others = copy(rows_of_two, outputs_ref, last_semaphores.at[2])

    get_weights = [load_qkv(array, row, part, weights, semaphores) for part in range(3)]
    get_grads = [
        [
            copy(
                grads_ref.at[part, :, rows], grads.at[part, :, rows], load_semaphores.at[index, part]
            )
            for part in range(3)
        ]
        for index, rows in enumerate(tiles)
    ]
    get_rest = [
        [
            copy(hidden_ref.at[spot_ref[which], rows], hidden.at[rows], load_semaphores.at[index, 3]),
            copy(grad_middle_ref.at[rows], grad_middle.at[rows], load_semaphores.at[index, 4]),
        ]
        for index, rows in enumerate(tiles)
    ]
    for part in range(3):
        get_weights[part].start()
        get_grads[0][part].start()
    stores = []
    gain = norm_ref[0:1]

    def finish(index, rows):
        for load in get_rest[index]:
            load.wait()
        for part in chunks(rows):
            here = shifted(part, -rows.start)
            back = norm_back(hidden[part].astype(F32), gain, total[index % 2, here])
            out[part] = (grad_middle[part].astype(F32) + back).astype(BF16)
        if last:
            piece, start = divmod(rows.start, D // 2)
            target = out_ref[piece].at[0, start : start + UNPROJECT]
        else:
            target = out_ref.at[0, rows]
        stores.append(copy(out.at[rows], target, store_semaphores.at[index]))
        if last:
            pl.when(spot_ref[0] != 0)(stores[-1].start)
            straight = copy(out.at[rows], outputs_ref.at[0, rows], store_semaphores.at[index])
            pl.when(spot_ref[0] == 0)(straight.start)
        else:
            stores[-1].start()

    for index, rows in enumerate(tiles):
        if last and index == 1:

            @pl.when(spot_ref[0] != 0)
            def _():
                for other in get_others:
                    other.start()

        if last and index == 3:

            @pl.when(spot_ref[0] != 0)
            def _():
                for other in get_others:
                    other.wait()
                put_others.start()

        product = None
        for part in range(3):
            if index == 0:
                get_weights[part].wait()
            get_grads[index][part].wait()
            if part == 0:
                following = get_grads[index + 1] if index + 1 < len(tiles) else []
                for load in following + get_rest[index]:
                    load.start()
            term = dot_nt(get_pairs(grads, rows, part), matrix(weights, part))
            product = term if product is None else product + term
        total[index % 2] = product
        if index:
            finish(index - 1, tiles[index - 1])
    finish(len(tiles) - 1, tiles[-1])
    for store in stores:
        store.wait()
    if last:
        pl.when(spot_ref[0] != 0)(put_others.wait)


def unproject(spot, which, grads, hidden, grad_middle, norms, place, others=()):
    length = hidden.shape[1]
    count = D // UNPROJECT
    row = jax.ShapeDtypeStruct((1, length, D), BF16)
    piece = jax.ShapeDtypeStruct((1, length // 2, D), BF16)
    return pl.pallas_call(
        functools.partial(unproject_kernel, place[1], which),
        in_specs=[SCALARS, IN_VMEM] + [ANY] * (4 + len(others)),
        out_specs=[ANY] * 3 if others else ANY,
        scratch_shapes=[
            pltpu.VMEM((3, PAIRS, D, PAIR_DIM), BF16),
            whole_scratch(BF16),
            whole_scratch(BF16),
            whole_scratch(BF16),
            pltpu.VMEM((2, UNPROJECT, D), F32),
            across_scratch(3),
            pltpu.SemaphoreType.DMA((3,)),
            pltpu.SemaphoreType.DMA((count, 5)),
            pltpu.SemaphoreType.DMA((count,)),
        ]
        + ([pltpu.VMEM((2, D, D), BF16), pltpu.SemaphoreType.DMA((3,))] if others else []),
        out_shape=[jax.ShapeDtypeStruct((2, length, D), BF16), piece, piece] if others else row,
        compiler_params=params(),
        cost_estimate=cost(11),
        name="unproject",
    )(spot, norms, grads, hidden, grad_middle, place[0], *others)


def place_kernel(spot_ref, outputs_in, top_ref, bottom_ref, outputs_ref, buffer, semaphores):
    del outputs_in
    half = D // 2
    tiles = row_tiles(D, 256)
    loads = [
        pltpu.make_async_copy(
            (bottom_ref if rows.start >= half else top_ref).at[0, pl.ds(rows.start % half, 256)],
            buffer.at[rows],
            semaphores.at[0, index],
        )
        for index, rows in enumerate(tiles)
    ]
    stores = [
        pltpu.make_async_copy(buffer.at[rows], outputs_ref.at[1, rows], semaphores.at[1, index])
        for index, rows in enumerate(tiles)
    ]

    @pl.when(spot_ref[0] == 0)
    def _():
        for load in loads:
            load.start()
        for load, store in zip(loads, stores):
            load.wait()
            store.start()
        for store in stores:
            store.wait()


def place_received(spot, outputs, pieces):
    return pl.pallas_call(
        place_kernel,
        in_specs=[SCALARS, ANY, ANY, ANY],
        out_specs=ANY,
        scratch_shapes=[whole_scratch(BF16), pltpu.SemaphoreType.DMA((2, 4))],
        out_shape=jax.ShapeDtypeStruct(outputs.shape, outputs.dtype),
        input_output_aliases={1: 0},
        compiler_params=params(),
        cost_estimate=cost(2),
        name="place_received",
    )(spot, outputs, *pieces)


def three_terms(values):
    high = values.astype(BF16)
    rest = values - high.astype(F32)
    middle = rest.astype(BF16)
    return high, middle, (rest - middle.astype(F32)).astype(BF16)


def exact_nt(values, right):
    count = values.shape[0]
    product = dot_nt(jnp.concatenate(three_terms(values), axis=0), right)
    return (product[2 * count :] + product[count : 2 * count]) + product[:count]


def exact_tn(left, right):
    high, middle, low = three_terms(left)
    first, second, third = three_terms(right)
    return dot_tn(
        jnp.concatenate([low, middle, high, middle, high, high], axis=0),
        jnp.concatenate([first, second, third, first, second, first], axis=0),
    )


def joined(ref):
    return jnp.concatenate(
        [
            ref[pair, part * PREFIX : (part + 1) * PREFIX]
            for part in range(2)
            for pair in range(PAIRS)
        ],
        axis=1,
    )


def hidden_kernel(total_ref, w2_ref, out_ref, total):
    total[...] = jnp.zeros_like(total)
    total[:PREFIX] = joined(total_ref)
    out_ref[...] = exact_nt(total[...], w2_ref[0])


def hidden_back(total, w2):
    return pl.pallas_call(
        hidden_kernel,
        in_specs=[IN_VMEM] * 2,
        out_specs=IN_VMEM,
        scratch_shapes=[pltpu.VMEM((SLOTS, 2 * D), F32)],
        out_shape=jax.ShapeDtypeStruct((SLOTS, w2.shape[1]), F32),
        compiler_params=params(),
        cost_estimate=cost(2),
        name="hidden_back",
    )(total, w2)


def second_kernel(total_ref, hidden_ref, w2_out, b2_out, total):
    total[...] = jnp.zeros_like(total)
    total[:PREFIX] = joined(total_ref)
    for columns in row_tiles(2 * D, 512):
        w2_out[0, :, columns] = exact_tn(hidden_ref[...], total[:, columns])
    b2_out[...] = jnp.sum(total[...], axis=0, keepdims=True)


def second_back(total, hidden):
    rh = hidden.shape[1]
    return pl.pallas_call(
        second_kernel,
        in_specs=[IN_VMEM] * 2,
        out_specs=[IN_VMEM] * 2,
        scratch_shapes=[pltpu.VMEM((SLOTS, 2 * D), F32)],
        out_shape=[
            jax.ShapeDtypeStruct((1, rh, 2 * D), F32),
            jax.ShapeDtypeStruct((1, 2 * D), F32),
        ],
        compiler_params=params(),
        cost_estimate=cost(3),
        name="second_back",
    )(total, hidden)


def first_kernel(own_ref, other_ref, hidden_ref, table_ref, w1_ref, table_out, w1_out, b1_out):
    hidden = hidden_ref[...]
    grad_pre = (own_ref[...] + other_ref[...]) * (1.0 - hidden * hidden)
    b1_out[...] = jnp.sum(grad_pre, axis=0, keepdims=True)
    w1_out[...] = exact_tn(table_ref[...].astype(F32), grad_pre)
    table_out[...] = exact_nt(grad_pre, w1_ref[...])[:PREFIX]


def first_back(own, other, hidden, table, w1):
    return pl.pallas_call(
        first_kernel,
        in_specs=[IN_VMEM] * 5,
        out_specs=[IN_VMEM] * 3,
        out_shape=[
            jax.ShapeDtypeStruct((PREFIX, D), F32),
            jax.ShapeDtypeStruct(w1.shape, F32),
            jax.ShapeDtypeStruct((1, w1.shape[1]), F32),
        ],
        compiler_params=params(),
        cost_estimate=cost(2),
        name="first_back",
    )(own, other, hidden, table, w1)


def swap_sections(values):
    return lax.ppermute(values, "section", [(0, 1), (1, 0)])


def per_section(section_index, own):
    other = swap_sections(own)
    is_first = section_index == 0
    return jnp.where(is_first, own, other), jnp.where(is_first, other, own)


def halves(w_qkv, w_out, w_fc, w_proj):
    columns = lambda matrix: jnp.moveaxis(matrix.reshape(SHARD_ROWS, -1, D), 1, 0)
    attention = jnp.concatenate([columns(w_qkv), w_out[None]], axis=0).reshape(2, HALF, D)
    up = columns(w_fc).reshape(2, HALF, D)
    down = w_proj.reshape(2, HALF, D)
    return jnp.stack([attention, up, down], axis=1)


def gather_weights(is_first, w_qkv, w_out, w_fc, w_proj):
    if D // w_qkv.shape[1] == SHARDS:
        own = halves(w_qkv[0], w_out[0], w_fc[0], w_proj[0])
        received = swap_sections(jnp.where(is_first, own[1], own[0]))
        first = jnp.where(is_first, own[0], received)
        last = jnp.where(is_first, received, own[1])
        early = jnp.concatenate([first.reshape(3 * HALF, D), last[0]], axis=0)
        gather = lambda rows: lax.all_gather(rows, ("dp", "section"), axis=0).reshape(
            SHARDS, 2, -1, D
        )
        early, late = gather(early), gather(last[1:].reshape(2 * HALF, D))
    else:
        whole = lambda matrix: lax.all_gather(matrix[0], ("dp", "section"), axis=0)
        every = [whole(matrix) for matrix in (w_qkv, w_out, w_fc, w_proj)]
        layers = []
        for layer in range(2):
            mine = [matrix[layer::2] for matrix in every]
            shards = [matrix.reshape(SHARDS, -1, matrix.shape[-1]) for matrix in mine]
            layers.append(jax.vmap(halves)(*shards).reshape(SHARDS, 2, 3 * HALF, D))
        early = jnp.concatenate([layers[0], layers[1][:, :, :HALF]], axis=2)
        late = layers[1][:, :, HALF:]
    return (
        [(early, 0), (early, HALF), (early, 2 * HALF)],
        [(early, 3 * HALF), (late, 0), (late, HALF)],
    )


def reparam_hidden(table, w_first, b_first):
    return jnp.tanh(jnp.dot(table, w_first, precision=highest_mode) + b_first)


def reparam_out(hidden_units, w_second, b_second):
    return jnp.dot(hidden_units, w_second, precision=highest_mode) + b_second


def sum_dp(values):
    count = lax.axis_size("dp")
    moved = lambda bits: lax.ppermute(values, "dp", [(i, i ^ bits) for i in range(count)])
    step = count
    while step > 1:
        if step % 4 == 0:
            step //= 4
            values = (values + moved(step)) + (moved(2 * step) + moved(3 * step))
        else:
            step //= 2
            values = values + moved(step)
    return values


def per_device(
    tokens,
    seq_length,
    cotangent,
    ln_gain,
    ln_bias,
    w_qkv,
    w_out,
    w_fc,
    w_proj,
    prefix_table,
    reparam_w1,
    reparam_b1,
    reparam_w2,
    reparam_b2,
):
    section_index = lax.axis_index("section")
    is_first = section_index == 0
    first, last = gather_weights(is_first, w_qkv, w_out, w_fc, w_proj)
    spot = jnp.stack([section_index, jnp.zeros_like(section_index)]).astype(jnp.int32)
    seq = lax.dynamic_slice_in_dim(seq_length, section_index, 1, 0)

    table_values = prefix_table.astype(F32)
    first_weight = reparam_w1.astype(F32)
    first_bias = reparam_b1.astype(F32)
    second_weight = reparam_w2[0].astype(F32)
    second_bias = reparam_b2[0].astype(F32)
    hidden_units = reparam_hidden(table_values, first_weight, first_bias)
    prefix_kv = reparam_out(hidden_units, second_weight, second_bias).astype(BF16)
    pad = ((0, SLOTS - PREFIX), (0, 0))
    small = jnp.concatenate(
        [
            jnp.pad(prefix_kv[:, :D], pad),
            jnp.pad(prefix_kv[:, D:], pad),
            ln_gain[0],
            ln_bias[0],
            jnp.zeros((4, D), BF16),
        ],
        axis=0,
    )
    small_pair = per_section(section_index, small)
    pairs_apart = lambda rows: jnp.moveaxis(rows.reshape(SLOTS, PAIRS, PAIR_DIM), 1, 0)
    prefix_pair = [
        (pairs_apart(part[:SLOTS]), pairs_apart(part[SLOTS : 2 * SLOTS])) for part in small_pair
    ]
    norm_pair = [part[2 * SLOTS :].astype(F32) for part in small_pair]

    prefix_first, prefix_last = prefix_pair
    projected_first = project(spot, 0, tokens, norm_pair[0], first[0])
    attended_first, *probs_first = attend(seq, projected_first, *prefix_first)
    middle_first, normed = middle_block(spot, 0, attended_first, tokens, norm_pair[0], first[0])
    slope, handed = forward_block(normed, middle_first, *first[1:])
    projected = project(spot, 1, handed, norm_pair[1], last[0])
    attended, *probs = attend(seq, projected, *prefix_last)
    middle, normed = middle_block(spot, 1, attended, handed, norm_pair[1], last[0])
    final, sent, grad_middle, grad_attended = turn_block(
        spot, normed, middle, cotangent, handed, norm_pair[1], *last
    )
    received = swap_sections(sent)
    grads, prefix_grad_last = attend_back(
        seq, projected, attended, grad_attended, *prefix_last, *probs
    )
    grad_handed = unproject(spot, 1, grads, handed, grad_middle, norm_pair[1], last[0])
    received_grad = lax.ppermute(grad_handed, "section", [(0, 1)])
    activations, grad_middle, grad_attended = backward_block(
        spot, grad_handed, slope, middle_first, (handed, final, received), norm_pair[0], *first
    )
    grads, prefix_grad_first = attend_back(
        seq,
        projected_first,
        attended_first,
        grad_attended,
        *prefix_first,
        *probs_first,
    )
    input_grads, *pieces = unproject(
        spot,
        0,
        grads,
        tokens,
        grad_middle,
        norm_pair[0],
        first[0],
        (grad_handed, received_grad),
    )
    pieces = [lax.ppermute(piece, "section", [(1, 0)]) for piece in pieces]
    input_grads = place_received(spot, input_grads, pieces)

    kept = jnp.where(is_first, prefix_grad_first, prefix_grad_last)
    sent = jnp.where(is_first, prefix_grad_last, prefix_grad_first)
    total = sum_dp(kept + swap_sections(sent))
    slots = lambda rows: jnp.pad(rows, ((0, SLOTS - PREFIX), (0, 0)))
    hidden_slots, table_slots = slots(hidden_units), slots(prefix_table)
    grad_hidden = hidden_back(total, reparam_w2)
    grad_w2, grad_b2 = second_back(total, hidden_slots)
    grad_table, grad_w1, grad_b1 = first_back(
        grad_hidden, swap_sections(grad_hidden), hidden_slots, table_slots, reparam_w1
    )
    return (
        activations[None],
        input_grads[None],
        grad_table,
        grad_w1,
        grad_b1[0],
        grad_w2,
        grad_b2,
    )


def solution(mesh):
    in_specs = (
        P("dp", None, None),
        P("dp"),
        P("dp", None, None),
        P("section", None, None),
        P("section", None, None),
        P("section", "dp", None),
        P("section", "dp", None),
        P("section", "dp", None),
        P("section", "dp", None),
        P(),
        P(),
        P(),
        P("section", None, None),
        P("section", None),
    )
    out_specs = (
        P("section", "dp", None, None),
        P("section", "dp", None, None),
        P(),
        P(),
        P(),
        P("section", None, None),
        P("section", None),
    )
    return jax.shard_map(
        per_device, mesh=mesh, in_specs=in_specs, out_specs=out_specs, check_vma=False
    )
```

```python
import functools

import jax
import jax.numpy as jnp
from jax import lax
from jax.experimental import pallas as pl
from jax.experimental.pallas import tpu as pltpu
from jax.sharding import PartitionSpec as P

D = 1024
HEADS = 16
HEAD_DIM = 64
FF = 4096
PREFIX = 10
SLOTS = 16
BOTH = 24
PAIRS = 8
PAIR_DIM = 128
BLOCK = 256

eps_norm = 1e-05
neg_big = -1e30
highest_mode = lax.Precision.HIGHEST
VMEM_BYTES = 62 * 2**20
F32 = jnp.float32
BF16 = jnp.bfloat16


def dot(left, right, dims):
    return lax.dot_general(left, right, (dims, ((), ())), preferred_element_type=F32)


def dot_nn(left, right):
    return dot(left, right, ((1,), (0,)))


def dot_nt(left, right):
    return dot(left, right, ((1,), (1,)))


def dot_tn(left, right):
    return dot(left, right, ((0,), (0,)))


def normalised(values):
    centre = jnp.mean(values, axis=-1, keepdims=True)
    spread = values - centre
    variance = jnp.mean(spread * spread, axis=-1, keepdims=True)
    inverse = lax.rsqrt(variance + eps_norm)
    return spread * inverse, inverse


def layer_norm(values, gain, offset):
    return normalised(values)[0] * gain + offset


def norm_back(values, gain, upstream):
    unit, inverse = normalised(values)
    scaled = upstream * gain
    mean_scaled = jnp.mean(scaled, axis=-1, keepdims=True)
    mean_unit = jnp.mean(scaled * unit, axis=-1, keepdims=True)
    return (scaled - mean_scaled - unit * mean_unit) * inverse


SQRT_2_PI = 0.7978845608028654
CUBIC = 0.044715


def gelu_pair(values):
    cubic_part = (SQRT_2_PI * CUBIC) * (values * values)
    half_tanh = 0.5 + 0.5 * jnp.tanh(values * (SQRT_2_PI + cubic_part))
    out = values * half_tanh
    slope = half_tanh + out * ((2.0 - 2.0 * half_tanh) * (SQRT_2_PI + 3.0 * cubic_part))
    return out, slope


def params(**kwargs):
    return pltpu.CompilerParams(vmem_limit_bytes=VMEM_BYTES, **kwargs)


def cost(micros):
    return pl.CostEstimate(flops=int(micros * 1.15e9), bytes_accessed=2**20, transcendentals=0)


SHARDS = 16
HALF = 128
SHARD_ROWS = 64
BLOCKS = FF // D


def load_across(array, half, row, target, semaphore):
    return pltpu.make_async_copy(array.at[:, half, pl.ds(row, SHARD_ROWS)], target, semaphore)


def load_qkv(array, row, part, weights, semaphores):
    half, inner = divmod(part, 2)
    return load_across(
        array, half, row + inner * SHARD_ROWS, weights.at[part], semaphores.at[part]
    )


def load_out(array, row, target, semaphore):
    return load_across(array, 1, row + SHARD_ROWS, target, semaphore)


def load_up(array, row, block, target, semaphore):
    half, inner = divmod(block, 2)
    return load_across(array, half, row + inner * SHARD_ROWS, target, semaphore)


def load_down(array, row, block, target, semaphore):
    few = SHARDS // BLOCKS
    return pltpu.make_async_copy(
        array.at[pl.ds(block * few, few), :, pl.ds(row, HALF)], target, semaphore
    )


def across_scratch(count):
    return pltpu.VMEM((count, SHARDS, SHARD_ROWS, D), BF16)


def down_scratch():
    return pltpu.VMEM((BLOCKS, SHARDS // BLOCKS, 2, HALF, D), BF16)


def matrix(ref, *index):
    return ref[index].reshape(D, D) if index else ref[...].reshape(D, D)


ANY = pl.BlockSpec(memory_space=pl.ANY)
TILE = 512
SCALARS = pl.BlockSpec(memory_space=pltpu.SMEM)
IN_VMEM = pl.BlockSpec(memory_space=pltpu.VMEM)


def whole_scratch(dtype):
    return pltpu.VMEM((D, D), dtype)


def once(shape, index):
    return pl.BlockSpec(shape, index, pipeline_mode=pl.Buffered(1))


def row_tiles(length, size):
    return [slice(start, start + size) for start in range(0, length, size)]


CHUNK = 16


def put_pairs(ref, rows, values):
    for pair in range(PAIRS):
        ref[pair, rows] = values[:, pair * PAIR_DIM : (pair + 1) * PAIR_DIM]


def get_pairs(ref, rows, *lead):
    return jnp.concatenate([ref[(*lead, pair, rows)] for pair in range(PAIRS)], axis=1)


def chunks(rows, size=CHUNK):
    return [slice(start, start + size) for start in range(rows.start, rows.stop, size)]


def shifted(rows, by):
    return slice(rows.start + by, rows.stop + by)


def qkv_kernel(row, spot_ref, hidden_ref, norm_ref, array, out_ref, normed, weights, semaphores):
    step = pl.program_id(0)
    loads = [load_qkv(array, row, part, weights, semaphores) for part in range(3)]
    length = hidden_ref.shape[1]
    tiles = row_tiles(length, 256)

    @pl.when(step == 0)
    def _():
        loads[0].start()
        gain, offset = norm_ref[0:1], norm_ref[2:3]

        def norm(tile):
            for rows in chunks(tile):
                values = hidden_ref[0, rows].astype(F32)
                normed[rows] = layer_norm(values, gain, offset).astype(BF16)

        norm(tiles[0])
        loads[0].wait()
        loads[1].start()
        loads[2].start()
        for index, rows in enumerate(tiles):
            if index + 1 < len(tiles):
                norm(tiles[index + 1])
            queries = dot_nn(normed[rows], matrix(weights, 0))
            put_pairs(out_ref, rows, (queries * HEAD_DIM**-0.5).astype(BF16))

    for part in (1, 2):

        @pl.when(step == part)
        def _(part=part):
            loads[part].wait()
            for rows in tiles:
                put_pairs(out_ref, rows, dot_nn(normed[rows], matrix(weights, part)).astype(BF16))


def project(spot, which, hidden, norms, place):
    length = hidden.shape[1]
    return pl.pallas_call(
        functools.partial(qkv_kernel, place[1]),
        grid_spec=pltpu.PrefetchScalarGridSpec(
            num_scalar_prefetch=1,
            grid=(3,),
            in_specs=[
                once((1, length, D), lambda j, s: (s[which], 0, 0)),
                once((8, D), lambda j, s: (0, 0)),
                ANY,
            ],
            out_specs=pl.BlockSpec((PAIRS, length, PAIR_DIM), lambda j, s: (j, 0, 0)),
            scratch_shapes=[
                pltpu.VMEM((length, D), BF16),
                across_scratch(3),
                pltpu.SemaphoreType.DMA((3,)),
            ],
        ),
        out_shape=jax.ShapeDtypeStruct((3 * PAIRS, length, PAIR_DIM), BF16),
        compiler_params=params(),
        cost_estimate=cost(12),
        name="norm_project",
    )(spot, hidden, norms, place[0])


def lane_halves(block):
    lanes = lax.broadcasted_iota(jnp.int32, block.shape, 1)
    zero = jnp.zeros_like(block)
    return jnp.where(lanes < HEAD_DIM, block, zero), jnp.where(lanes < HEAD_DIM, zero, block)


def key_spans(first, stop):
    if first == 0:
        return [slice(0, SLOTS + stop)]
    return [slice(0, SLOTS), slice(SLOTS + first, SLOTS + stop)]


def read_spans(ref, spans, *rest):
    parts = [ref[(span, *rest)] for span in spans]
    return parts[0] if len(parts) == 1 else jnp.concatenate(parts, axis=0)


def cut_spans(values, spans):
    start = 0
    for span in spans:
        size = span.stop - span.start
        yield span, values[start : start + size]
        start += size


def strips(length, short):
    return [
        (rows, slice(2 * rows.start, 2 * rows.stop), rows.start if short else 0)
        for rows in row_tiles(length, BLOCK)
    ]


def stacked_halves(block):
    return jnp.concatenate(lane_halves(block), axis=0)


def own_heads(product):
    return jnp.concatenate([product[:HEAD_DIM, :BLOCK], product[HEAD_DIM:, BLOCK:]], axis=0)


def either_length(length_ref, length, run):
    short = length_ref[0] < length
    pl.when(short)(lambda: run(True))
    pl.when(jnp.logical_not(short))(lambda: run(False))


def allowed(rows, first_diagonal):
    shape = (rows.stop - rows.start, 2 * BLOCK)
    keys = lax.broadcasted_iota(jnp.int32, shape, 0) + rows.start
    if rows.stop <= SLOTS:
        return keys < PREFIX
    queries = lax.broadcasted_iota(jnp.int32, shape, 1) % BLOCK
    return keys - first_diagonal <= queries


def eight_rows(values, reduce):
    return reduce(values.reshape(-1, 8, values.shape[-1]), axis=0)


def attend_kernel(
    seq_ref, q_ref, k_ref, v_ref, kp_ref, vp_ref, out_ref, probs_ref, scale_ref, keys, values_t, scores
):
    length = q_ref.shape[1]
    keys[:SLOTS], keys[SLOTS:] = kp_ref[0], k_ref[0]
    values_t[...] = v_ref[0].T
    prefix_values = vp_ref[0]

    def run(short):
        def scored(strip, slot):
            rows, _, first = strip
            count = SLOTS + rows.stop - first
            scores[slot, :count] = dot_nt(
                read_spans(keys, key_spans(first, rows.stop)), stacked_halves(q_ref[0, rows])
            )

        todo = strips(length, short)
        scored(todo[0], 0)
        for index, (rows, columns, first) in enumerate(todo):
            slot = index % 2
            if index + 1 < len(todo):
                scored(todo[index + 1], 1 - slot)
            count = SLOTS + rows.stop - first
            parts = chunks(slice(0, count))
            top = None
            for part in parts:
                values = scores[slot, part]
                if part.stop <= SLOTS or part.start >= count - BLOCK:
                    values = jnp.where(allowed(part, count - BLOCK), values, neg_big)
                    scores[slot, part] = values
                values = eight_rows(values, jnp.max)
                top = values if top is None else jnp.maximum(top, values)
            top = jnp.max(top, axis=0, keepdims=True)
            total = None
            for part in parts:
                values = jnp.exp(scores[slot, part] - top)
                place = part if part.stop <= SLOTS else shifted(part, first)
                probs_ref[0, place, columns] = values.astype(BF16)
                values = eight_rows(values, jnp.sum)
                total = values if total is None else total + values
            inverse = 1.0 / jnp.sum(total, axis=0, keepdims=True)
            both = dot_nn(
                values_t[:, first : rows.stop],
                probs_ref[0, SLOTS + first : SLOTS + rows.stop, columns],
            ) + dot_tn(prefix_values, probs_ref[0, :SLOTS, columns])
            inverse = jnp.concatenate(
                [
                    jnp.broadcast_to(inverse[:, :BLOCK], (HEAD_DIM, BLOCK)),
                    jnp.broadcast_to(inverse[:, BLOCK:], (HEAD_DIM, BLOCK)),
                ],
                axis=0,
            )
            out_ref[0, rows] = (own_heads(both) * inverse).T.astype(BF16)
            scale_ref[0, rows] = inverse.T

    either_length(seq_ref, length, run)


def pair_spec(length, part):
    return pl.BlockSpec((1, length, PAIR_DIM), lambda p, s: (part * PAIRS + p, 0, 0))


def probs_spec(length):
    return pl.BlockSpec((1, SLOTS + length, 2 * length), lambda p, s: (p, 0, 0))


def attend(seq, projected, prefix_keys, prefix_values):
    length = projected.shape[1]
    return pl.pallas_call(
        attend_kernel,
        grid_spec=pltpu.PrefetchScalarGridSpec(
            num_scalar_prefetch=1,
            grid=(PAIRS,),
            in_specs=[
                pair_spec(length, 0),
                pair_spec(length, 1),
                pair_spec(length, 2),
                pair_spec(SLOTS, 0),
                pair_spec(SLOTS, 0),
            ],
            out_specs=[pair_spec(length, 0), probs_spec(length), pair_spec(length, 0)],
            scratch_shapes=[
                pltpu.VMEM((SLOTS + length, PAIR_DIM), BF16),
                pltpu.VMEM((PAIR_DIM, length), BF16),
                pltpu.VMEM((2, SLOTS + length, 2 * BLOCK), F32),
            ],
        ),
        out_shape=[
            jax.ShapeDtypeStruct((PAIRS, length, PAIR_DIM), BF16),
            jax.ShapeDtypeStruct((PAIRS, SLOTS + length, 2 * length), BF16),
            jax.ShapeDtypeStruct((PAIRS, length, PAIR_DIM), F32),
        ],
        compiler_params=params(),
        cost_estimate=cost(30),
        name="attend",
    )(seq, projected, projected, projected, prefix_keys, prefix_values)


def attend_back_kernel(
    seq_ref,
    q_ref,
    k_ref,
    v_ref,
    out_ref,
    grad_ref,
    kp_ref,
    vp_ref,
    probs_ref,
    scale_ref,
    grads_ref,
    prefix_ref,
    values,
    keys_t,
    dk,
    dv,
    dprobs,
    ds,
):
    length = q_ref.shape[1]
    values[:SLOTS], values[SLOTS:] = vp_ref[0], v_ref[0]
    keys_t[...] = k_ref[0].T
    prefix_keys = kp_ref[0]
    dk[...] = jnp.zeros_like(dk)
    dv[...] = jnp.zeros_like(dv)

    def run(short):
        def prepared(strip, slot):
            rows, _, first = strip
            grads = (grad_ref[0, rows].astype(F32) * scale_ref[0, rows]).astype(BF16)
            halves = stacked_halves(grads)
            weighted_t = (grads.astype(F32) * out_ref[0, rows].astype(F32)).T
            centre = jnp.concatenate(
                [
                    jnp.sum(weighted_t[:HEAD_DIM], axis=0, keepdims=True),
                    jnp.sum(weighted_t[HEAD_DIM:], axis=0, keepdims=True),
                ],
                axis=1,
            )
            dprobs[slot, : SLOTS + rows.stop - first] = dot_nt(
                read_spans(values, key_spans(first, rows.stop)), halves
            )
            return halves, centre

        todo = strips(length, short)
        ahead = prepared(todo[0], 0)
        for index, (rows, columns, first) in enumerate(todo):
            slot = index % 2
            spans = key_spans(first, rows.stop)
            grad_halves, centre = ahead
            if index + 1 < len(todo):
                ahead = prepared(todo[index + 1], 1 - slot)
            count = SLOTS + rows.stop - first
            for part in chunks(slice(0, count)):
                place = part if part.stop <= SLOTS else shifted(part, first)
                probs = probs_ref[0, place, columns].astype(F32)
                ds[slot, part] = (probs * (dprobs[slot, part] - centre)).astype(BF16)
            for total, left, right in (
                (dv, read_spans(probs_ref.at[0], spans, columns), grad_halves),
                (dk, ds[slot, :count], stacked_halves(q_ref[0, rows])),
            ):
                for span, part in cut_spans(dot_nn(left, right), spans):
                    total[span] += part
            both = dot_nn(keys_t[:, first : rows.stop], ds[slot, SLOTS:count]) + dot_tn(
                prefix_keys, ds[slot, :SLOTS]
            )
            grads_ref[0, 0, rows] = (own_heads(both).T * HEAD_DIM**-0.5).astype(BF16)

    either_length(seq_ref, length, run)
    grads_ref[1, 0] = dk[SLOTS:].astype(BF16)
    grads_ref[2, 0] = dv[SLOTS:].astype(BF16)
    prefix_ref[0, :PREFIX] = dk[:PREFIX]
    prefix_ref[0, PREFIX : 2 * PREFIX] = dv[:PREFIX]
    prefix_ref[0, 2 * PREFIX :] = jnp.zeros_like(prefix_ref[0, 2 * PREFIX :])


def attend_back(seq, projected, attended, grad_attended, prefix_keys, prefix_values, probs, scale):
    length = projected.shape[1]
    ext = (SLOTS + length, PAIR_DIM)
    return pl.pallas_call(
        attend_back_kernel,
        grid_spec=pltpu.PrefetchScalarGridSpec(
            num_scalar_prefetch=1,
            grid=(PAIRS,),
            in_specs=[
                pair_spec(length, 0),
                pair_spec(length, 1),
                pair_spec(length, 2),
                pair_spec(length, 0),
                pair_spec(length, 0),
                pair_spec(SLOTS, 0),
                pair_spec(SLOTS, 0),
                probs_spec(length),
                pair_spec(length, 0),
            ],
            out_specs=[
                pl.BlockSpec((3, 1, length, PAIR_DIM), lambda p, s: (0, p, 0, 0)),
                pair_spec(BOTH, 0),
            ],
            scratch_shapes=[
                pltpu.VMEM(ext, BF16),
                pltpu.VMEM((PAIR_DIM, length), BF16),
                pltpu.VMEM(ext, F32),
                pltpu.VMEM(ext, F32),
                pltpu.VMEM((2, SLOTS + length, 2 * BLOCK), F32),
                pltpu.VMEM((2, SLOTS + length, 2 * BLOCK), BF16),
            ],
        ),
        out_shape=[
            jax.ShapeDtypeStruct((3, PAIRS, length, PAIR_DIM), BF16),
            jax.ShapeDtypeStruct((PAIRS, BOTH, PAIR_DIM), F32),
        ],
        compiler_params=params(),
        cost_estimate=cost(30),
        name="attend_back",
    )(
        seq,
        projected,
        projected,
        projected,
        attended,
        grad_attended,
        prefix_keys,
        prefix_values,
        probs,
        scale,
    )


def middle_kernel(
    row,
    which,
    spot_ref,
    norm_ref,
    attended_ref,
    hidden_ref,
    array,
    middle_ref,
    normed_ref,
    attended,
    hidden,
    middle,
    normed,
    weights,
    semaphores,
    load_semaphores,
    store_semaphores,
):
    copy = pltpu.make_async_copy
    tiles = row_tiles(D, 256)
    get_weights = load_out(array, row, weights, semaphores.at[0])
    get_attended = [
        copy(attended_ref.at[:, rows], attended.at[:, rows], load_semaphores.at[0, index])
        for index, rows in enumerate(tiles)
    ]
    get_hidden = [
        copy(hidden_ref.at[spot_ref[which], rows], hidden.at[rows], load_semaphores.at[1, index])
        for index, rows in enumerate(tiles)
    ]
    get_weights.start()
    for loads in zip(get_attended, get_hidden):
        for load in loads:
            load.start()
    gain, offset = norm_ref[1:2], norm_ref[3:4]
    stores = []

    def finish(index, rows):
        get_hidden[index].wait()
        for part in chunks(rows):
            values = hidden[part].astype(F32) + middle[part]
            middle[part] = values
            normed[part] = layer_norm(values, gain, offset).astype(BF16)
        for source, target, kind in ((middle, middle_ref, 0), (normed, normed_ref, 1)):
            stores.append(copy(source.at[rows], target.at[rows], store_semaphores.at[kind, index]))
            stores[-1].start()

    get_weights.wait()
    for index, rows in enumerate(tiles):
        get_attended[index].wait()
        middle[rows] = dot_nn(get_pairs(attended, rows), matrix(weights))
        if index:
            finish(index - 1, tiles[index - 1])
    finish(len(tiles) - 1, tiles[-1])
    for store in stores:
        store.wait()


def middle_block(spot, which, attended, hidden, norms, place):
    length = attended.shape[1]
    count = D // 256
    return pl.pallas_call(
        functools.partial(middle_kernel, place[1], which),
        in_specs=[SCALARS, IN_VMEM] + [ANY] * 3,
        out_specs=[ANY] * 2,
        scratch_shapes=[
            pltpu.VMEM((PAIRS, D, PAIR_DIM), BF16),
            whole_scratch(BF16),
            whole_scratch(F32),
            whole_scratch(BF16),
            pltpu.VMEM((SHARDS, SHARD_ROWS, D), BF16),
            pltpu.SemaphoreType.DMA((1,)),
            pltpu.SemaphoreType.DMA((2, count)),
            pltpu.SemaphoreType.DMA((2, count)),
        ],
        out_shape=[
            jax.ShapeDtypeStruct((length, D), F32),
            jax.ShapeDtypeStruct((length, D), BF16),
        ],
        compiler_params=params(),
        cost_estimate=cost(5),
        name="middle_block",
    )(spot, norms, attended, hidden, place[0])


def feed_forward_loads(up, down, rows, up_weights, down_weights, semaphores):
    return [
        (
            load_up(up, rows[0], block, up_weights.at[block], semaphores.at[0, block]),
            load_down(down, rows[1], block, down_weights.at[block], semaphores.at[1, block]),
        )
        for block in range(BLOCKS)
    ]


def start_all(loads):
    for pair in loads:
        for load in pair:
            load.start()


def wait_step(loads, step):
    for block, pair in enumerate(loads):

        @pl.when(step == block)
        def _(pair=pair):
            for load in pair:
                load.wait()


def wait_for(target, semaphore):
    pltpu.make_async_copy(target, target, semaphore).wait()


def feed_forward_scratch():
    return [across_scratch(BLOCKS), down_scratch(), pltpu.SemaphoreType.DMA((2, BLOCKS))]


def forward_kernel(
    rows_at,
    normed_ref,
    middle_ref,
    up,
    down,
    slope_ref,
    out_ref,
    total,
    inner,
    activated,
    up_weights,
    down_weights,
    semaphores,
):
    step = pl.program_id(0)
    tiles = row_tiles(middle_ref.shape[0], TILE)
    loads = feed_forward_loads(up, down, rows_at, up_weights, down_weights, semaphores)

    @pl.when(step == 0)
    def _():
        start_all(loads[:1])
        total[...] = middle_ref[...]

    wait_step(loads, step)
    for later in range(1, BLOCKS):
        pl.when(step == later - 1)(lambda later=later: start_all(loads[later : later + 1]))
    w_fc, w_proj = matrix(up_weights, step), matrix(down_weights, step)
    inner[tiles[0]] = dot_nn(normed_ref[tiles[0]], w_fc)
    for index, rows in enumerate(tiles):
        if index + 1 < len(tiles):
            inner[tiles[index + 1]] = dot_nn(normed_ref[tiles[index + 1]], w_fc)
        for part in chunks(rows):
            value, slope = gelu_pair(inner[part])
            activated[part] = value.astype(BF16)
            slope_ref[part] = slope.astype(BF16)
        total[rows] += dot_nn(activated[rows], w_proj)

    @pl.when(step == pl.num_programs(0) - 1)
    def _():
        out_ref[0] = total[...].astype(BF16)


def forward_block(normed, middle, up, down):
    length = normed.shape[0]
    whole = lambda j: (0, 0)
    return pl.pallas_call(
        functools.partial(forward_kernel, (up[1], down[1])),
        grid=(BLOCKS,),
        in_specs=[once((length, D), whole), once((length, D), whole), ANY, ANY],
        out_specs=[
            pl.BlockSpec((length, D), lambda j: (0, j)),
            once((1, length, D), lambda j: (0, 0, 0)),
        ],
        scratch_shapes=[whole_scratch(F32), whole_scratch(F32), whole_scratch(BF16)]
        + feed_forward_scratch(),
        out_shape=[
            jax.ShapeDtypeStruct((length, FF), BF16),
            jax.ShapeDtypeStruct((1, length, D), BF16),
        ],
        compiler_params=params(),
        cost_estimate=cost(25),
        name="forward_block",
    )(normed, middle, up[0], down[0])


FINISH = 256


def finish_backward(upstream, middle, grad_total, norm_ref, w_out, grad_middle, grad_attended, stores):
    gain = norm_ref[1:2]
    for index, rows in enumerate(row_tiles(D, FINISH)):
        for part in chunks(rows):
            grad = upstream[part].astype(F32) + norm_back(middle[part], gain, grad_total[part])
            grad_middle[part] = grad.astype(BF16)
        put_pairs(grad_attended, rows, dot_nt(grad_middle[rows], w_out).astype(BF16))
        for store in stores(rows, index):
            store.start()
    for index, rows in enumerate(row_tiles(D, FINISH)):
        for store in stores(rows, index):
            store.wait()


def turn_kernel(
    rows_at,
    spot_ref,
    norm_ref,
    normed_ref,
    middle_ref,
    upstream_ref,
    hidden_ref,
    attention,
    up,
    down,
    out_ref,
    sent_ref,
    grad_middle_ref,
    grad_attended_ref,
    normed,
    middle,
    upstream,
    total,
    grad_total,
    inner,
    grad_act,
    out,
    grad_middle,
    grad_attended,
    up_weights,
    down_weights,
    out_weights,
    semaphores,
    load_semaphores,
    store_semaphores,
):
    activated, grad_inner = grad_middle, out
    loads = feed_forward_loads(up, down, rows_at[1:], up_weights, down_weights, semaphores)
    copy = pltpu.make_async_copy
    get_normed = copy(normed_ref, normed, load_semaphores.at[0])
    get_upstream = copy(upstream_ref.at[spot_ref[0]], upstream, load_semaphores.at[1])
    get_middle = copy(middle_ref, middle, load_semaphores.at[2])
    get_out = load_out(attention, rows_at[0], out_weights, load_semaphores.at[3])
    get_normed.start()
    loads[0][0].start()
    total[...] = jnp.zeros_like(total)
    grad_total[...] = jnp.zeros_like(grad_total)
    get_normed.wait()
    get_upstream.start()
    loads[0][1].start()

    def step(block, carry):
        wait_for(up_weights.at[block], semaphores.at[0, block])
        tiles = row_tiles(D, TILE)
        w_fc = matrix(up_weights, block)
        inner[0] = dot_nn(normed[tiles[0]], w_fc)
        pl.when(block == 0)(get_upstream.wait)
        wait_for(down_weights.at[block], semaphores.at[1, block])
        w_proj = matrix(down_weights, block)
        for later in range(1, BLOCKS):
            pl.when(block == later - 1)(lambda later=later: start_all(loads[later : later + 1]))

        @pl.when(block == BLOCKS - 1)
        def _():
            get_middle.start()
            get_out.start()

        grad_act[0] = dot_nt(upstream[tiles[0]], w_proj)
        for index, rows in enumerate(tiles):
            slot = index % 2
            if index + 1 < len(tiles):
                inner[1 - slot] = dot_nn(normed[tiles[index + 1]], w_fc)
                grad_act[1 - slot] = dot_nt(upstream[tiles[index + 1]], w_proj)
            for part in chunks(rows):
                here = shifted(part, -rows.start)
                value, slope = gelu_pair(inner[slot, here])
                activated[part] = value.astype(BF16)
                grad_inner[part] = (grad_act[slot, here] * slope).astype(BF16)
            total[rows] += dot_nn(activated[rows], w_proj)
            grad_total[rows] += dot_nt(grad_inner[rows], w_fc)
        return carry

    lax.fori_loop(0, BLOCKS, step, 0)
    get_middle.wait()
    for part in chunks(slice(0, D)):
        out[part] = (total[part] + middle[part]).astype(BF16)
    put_out = copy(out, out_ref.at[0], store_semaphores.at[0, 0])
    put_out.start()
    put_sent = copy(out, sent_ref.at[0], store_semaphores.at[0, 1])
    get_hidden = copy(hidden_ref.at[0], normed, load_semaphores.at[4])
    put_hidden = copy(normed, sent_ref.at[0], store_semaphores.at[0, 1])
    pl.when(spot_ref[0] == 0)(put_sent.start)
    pl.when(spot_ref[0] != 0)(get_hidden.start)
    get_out.wait()

    def stores(rows, index):
        return (
            copy(grad_middle.at[rows], grad_middle_ref.at[rows], store_semaphores.at[1, index]),
            copy(grad_attended.at[:, rows], grad_attended_ref.at[:, rows], store_semaphores.at[2, index]),
        )

    finish_backward(
        upstream, middle, grad_total, norm_ref, matrix(out_weights), grad_middle, grad_attended, stores
    )
    put_out.wait()

    @pl.when(spot_ref[0] != 0)
    def _():
        get_hidden.wait()
        put_hidden.start()

    put_sent.wait()


def turn_block(spot, normed, middle, upstream, hidden, norms, attention, up, down):
    length = normed.shape[0]
    return pl.pallas_call(
        functools.partial(turn_kernel, (attention[1], up[1], down[1])),
        in_specs=[SCALARS, IN_VMEM] + [ANY] * 7,
        out_specs=[ANY] * 4,
        scratch_shapes=[
            whole_scratch(BF16),
            whole_scratch(F32),
            whole_scratch(BF16),
            whole_scratch(F32),
            whole_scratch(F32),
            pltpu.VMEM((2, TILE, D), F32),
            pltpu.VMEM((2, TILE, D), F32),
            whole_scratch(BF16),
            whole_scratch(BF16),
            pltpu.VMEM((PAIRS, D, PAIR_DIM), BF16),
            across_scratch(BLOCKS),
            down_scratch(),
            pltpu.VMEM((SHARDS, SHARD_ROWS, D), BF16),
            pltpu.SemaphoreType.DMA((2, BLOCKS)),
            pltpu.SemaphoreType.DMA((5,)),
            pltpu.SemaphoreType.DMA((3, D // FINISH)),
        ],
        out_shape=[
            jax.ShapeDtypeStruct((1, length, D), BF16),
            jax.ShapeDtypeStruct((1, length, D), BF16),
            jax.ShapeDtypeStruct((length, D), BF16),
            jax.ShapeDtypeStruct((PAIRS, length, PAIR_DIM), BF16),
        ],
        compiler_params=params(),
        cost_estimate=cost(42),
        name="turn_block",
    )(spot, norms, normed, middle, upstream, hidden, attention[0], up[0], down[0])


def backward_kernel(
    rows_at,
    spot_ref,
    norm_ref,
    slope_ref,
    middle_ref,
    upstream_ref,
    first_ref,
    last_ref,
    received_ref,
    attention,
    up,
    down,
    activations_ref,
    grad_middle_ref,
    grad_attended_ref,
    slope,
    middle,
    upstream,
    grad_total,
    grad_act,
    grad_middle,
    grad_attended,
    up_weights,
    down_weights,
    out_weights,
    semaphores,
    load_semaphores,
    store_semaphores,
    activations,
    output_semaphores,
):
    grad_inner = grad_middle
    section = spot_ref[0]
    loads = feed_forward_loads(up, down, rows_at[1:], up_weights, down_weights, semaphores)
    copy = pltpu.make_async_copy
    get_upstream = copy(upstream_ref.at[0], upstream, load_semaphores.at[BLOCKS])
    get_middle = copy(middle_ref, middle, load_semaphores.at[BLOCKS + 1])
    get_out = load_out(attention, rows_at[0], out_weights, load_semaphores.at[BLOCKS + 2])
    take = copy(received_ref.at[0], activations.at[1 - section], output_semaphores.at[0])
    keep_first = copy(first_ref.at[0], activations.at[section], output_semaphores.at[1])
    keep_last = copy(last_ref.at[0], activations.at[section], output_semaphores.at[1])
    put_activations = copy(activations, activations_ref, output_semaphores.at[2])
    get_slopes = [
        copy(slope_ref.at[:, pl.ds(block * D, D)], slope.at[block], load_semaphores.at[block])
        for block in range(BLOCKS)
    ]
    get_upstream.start()
    loads[0][1].start()
    grad_total[...] = jnp.zeros_like(grad_total)
    get_upstream.wait()
    get_slopes[0].start()
    loads[0][0].start()

    def step(block, carry):
        wait_for(down_weights.at[block], semaphores.at[1, block])
        w_proj = matrix(down_weights, block)
        tiles = row_tiles(D, TILE)
        grad_act[tiles[0]] = dot_nt(upstream[tiles[0]], w_proj)
        wait_for(slope.at[block], load_semaphores.at[block])
        wait_for(up_weights.at[block], semaphores.at[0, block])
        w_fc = matrix(up_weights, block)
        for later in range(1, BLOCKS):

            @pl.when(block == later - 1)
            def _(later=later):
                loads[later][1].start()
                get_slopes[later].start()
                loads[later][0].start()

        @pl.when(block == BLOCKS - 1)
        def _():
            get_middle.start()
            get_out.start()

        @pl.when(block == 1)
        def _():
            take.start()
            pl.when(section == 0)(keep_first.start)
            pl.when(section != 0)(keep_last.start)

        @pl.when(block == 2)
        def _():
            take.wait()
            keep_first.wait()
            put_activations.start()

        for index, rows in enumerate(tiles):
            if index + 1 < len(tiles):
                grad_act[tiles[index + 1]] = dot_nt(upstream[tiles[index + 1]], w_proj)
            for part in chunks(rows):
                grad_inner[part] = (grad_act[part] * slope[block, part].astype(F32)).astype(BF16)
            grad_total[rows] += dot_nt(grad_inner[rows], w_fc)
        return carry

    lax.fori_loop(0, BLOCKS, step, 0)
    get_middle.wait()
    get_out.wait()

    def stores(rows, index):
        return (
            copy(grad_middle.at[rows], grad_middle_ref.at[rows], store_semaphores.at[0, index]),
            copy(grad_attended.at[:, rows], grad_attended_ref.at[:, rows], store_semaphores.at[1, index]),
        )

    finish_backward(
        upstream, middle, grad_total, norm_ref, matrix(out_weights), grad_middle, grad_attended, stores
    )
    put_activations.wait()


def backward_block(spot, upstream, slope, middle, outputs, norms, attention, up, down):
    length = middle.shape[0]
    return pl.pallas_call(
        functools.partial(backward_kernel, (attention[1], up[1], down[1])),
        in_specs=[SCALARS, IN_VMEM] + [ANY] * 9,
        out_specs=[ANY] * 3,
        scratch_shapes=[
            pltpu.VMEM((BLOCKS, D, D), BF16),
            whole_scratch(F32),
            whole_scratch(BF16),
            whole_scratch(F32),
            whole_scratch(F32),
            whole_scratch(BF16),
            pltpu.VMEM((PAIRS, D, PAIR_DIM), BF16),
            across_scratch(BLOCKS),
            down_scratch(),
            pltpu.VMEM((SHARDS, SHARD_ROWS, D), BF16),
            pltpu.SemaphoreType.DMA((2, BLOCKS)),
            pltpu.SemaphoreType.DMA((BLOCKS + 3,)),
            pltpu.SemaphoreType.DMA((2, D // FINISH)),
            pltpu.VMEM((2, D, D), BF16),
            pltpu.SemaphoreType.DMA((3,)),
        ],
        out_shape=[
            jax.ShapeDtypeStruct((2, length, D), BF16),
            jax.ShapeDtypeStruct((length, D), BF16),
            jax.ShapeDtypeStruct((PAIRS, length, PAIR_DIM), BF16),
        ],
        compiler_params=params(),
        cost_estimate=cost(25),
        name="backward_block",
    )(spot, norms, slope, middle, upstream, *outputs, attention[0], up[0], down[0])


UNPROJECT = 256


def unproject_kernel(
    row,
    which,
    spot_ref,
    norm_ref,
    grads_ref,
    hidden_ref,
    grad_middle_ref,
    array,
    *refs,
):
    last = (*refs[:3], *refs[-2:]) if len(refs) > 10 else None
    out_ref, *refs = (refs[3:5], *refs[5:-2]) if last else refs
    unproject_body(
        row, which, spot_ref, norm_ref, grads_ref, hidden_ref, grad_middle_ref, array, last, out_ref, *refs
    )


def unproject_body(
    row,
    which,
    spot_ref,
    norm_ref,
    grads_ref,
    hidden_ref,
    grad_middle_ref,
    array,
    last,
    out_ref,
    grads,
    hidden,
    grad_middle,
    out,
    total,
    weights,
    semaphores,
    load_semaphores,
    store_semaphores,
):
    copy = pltpu.make_async_copy
    tiles = row_tiles(D, UNPROJECT)
    if last:
        kept_ref, received_ref, outputs_ref, rows_of_two, last_semaphores = last
        get_others = [
            copy(received_ref.at[0], rows_of_two.at[0], last_semaphores.at[0]),
            copy(kept_ref.at[0], rows_of_two.at[1], last_semaphores.at[1]),
        ]
        put_others = copy(rows_of_two, outputs_ref, last_semaphores.at[2])

    get_weights = [load_qkv(array, row, part, weights, semaphores) for part in range(3)]
    get_grads = [
        copy(grads_ref.at[part], grads.at[part], load_semaphores.at[0, part]) for part in range(3)
    ]
    get_hidden = copy(hidden_ref.at[spot_ref[which]], hidden, load_semaphores.at[1, 0])
    get_grad_middle = copy(grad_middle_ref, grad_middle, load_semaphores.at[1, 1])

    def start_part(part):
        get_weights[part].start()
        get_grads[part].start()

    start_part(0)
    stores = []
    gain = norm_ref[0:1]

    def finish(index, rows):
        for part in chunks(rows):
            back = norm_back(hidden[part].astype(F32), gain, total[part])
            out[part] = (grad_middle[part].astype(F32) + back).astype(BF16)
        if last:
            piece, start = divmod(rows.start, D // 2)
            target = out_ref[piece].at[0, start : start + UNPROJECT]
        else:
            target = out_ref.at[0, rows]
        stores.append(copy(out.at[rows], target, store_semaphores.at[index]))
        if last:
            pl.when(spot_ref[0] != 0)(stores[-1].start)
            straight = copy(out.at[rows], outputs_ref.at[0, rows], store_semaphores.at[index])
            pl.when(spot_ref[0] == 0)(straight.start)
        else:
            stores[-1].start()

    for part in range(3):
        get_weights[part].wait()
        get_grads[part].wait()
        if part < 2:
            start_part(part + 1)
        if part == 1:
            get_hidden.start()
            get_grad_middle.start()
        if part == 2:
            get_hidden.wait()
            get_grad_middle.wait()
        if part == 2 and last:

            @pl.when(spot_ref[0] != 0)
            def _():
                for other in get_others:
                    other.start()

        for index, rows in enumerate(tiles):
            term = dot_nt(get_pairs(grads, rows, part), matrix(weights, part))
            total[rows] = term if part == 0 else total[rows] + term
            if part == 2 and index:
                finish(index - 1, tiles[index - 1])
            if part == 2 and last and index == len(tiles) - 1:

                @pl.when(spot_ref[0] != 0)
                def _():
                    for other in get_others:
                        other.wait()
                    put_others.start()

    finish(len(tiles) - 1, tiles[-1])
    for store in stores:
        store.wait()
    if last:
        pl.when(spot_ref[0] != 0)(put_others.wait)


def unproject(spot, which, grads, hidden, grad_middle, norms, place, others=()):
    length = hidden.shape[1]
    count = D // UNPROJECT
    row = jax.ShapeDtypeStruct((1, length, D), BF16)
    piece = jax.ShapeDtypeStruct((1, length // 2, D), BF16)
    return pl.pallas_call(
        functools.partial(unproject_kernel, place[1], which),
        in_specs=[SCALARS, IN_VMEM] + [ANY] * (4 + len(others)),
        out_specs=[ANY] * 3 if others else ANY,
        scratch_shapes=[
            pltpu.VMEM((3, PAIRS, D, PAIR_DIM), BF16),
            whole_scratch(BF16),
            whole_scratch(BF16),
            whole_scratch(BF16),
            whole_scratch(F32),
            across_scratch(3),
            pltpu.SemaphoreType.DMA((3,)),
            pltpu.SemaphoreType.DMA((2, 3)),
            pltpu.SemaphoreType.DMA((count,)),
        ]
        + ([pltpu.VMEM((2, D, D), BF16), pltpu.SemaphoreType.DMA((3,))] if others else []),
        out_shape=[jax.ShapeDtypeStruct((2, length, D), BF16), piece, piece] if others else row,
        compiler_params=params(),
        cost_estimate=cost(11),
        name="unproject",
    )(spot, norms, grads, hidden, grad_middle, place[0], *others)


def three_terms(values):
    high = values.astype(BF16)
    rest = values - high.astype(F32)
    middle = rest.astype(BF16)
    return high, middle, (rest - middle.astype(F32)).astype(BF16)


def exact_nt(values, right):
    count = values.shape[0]
    product = dot_nt(jnp.concatenate(three_terms(values), axis=0), right)
    return (product[2 * count :] + product[count : 2 * count]) + product[:count]


def exact_tn(left, right):
    high, middle, low = three_terms(left)
    first, second, third = three_terms(right)
    return dot_tn(
        jnp.concatenate([low, middle, high, middle, high, high], axis=0),
        jnp.concatenate([first, second, third, first, second, first], axis=0),
    )


def joined(ref):
    return jnp.concatenate(
        [
            ref[pair, part * PREFIX : (part + 1) * PREFIX]
            for part in range(2)
            for pair in range(PAIRS)
        ],
        axis=1,
    )


def hidden_kernel(total_ref, w2_ref, out_ref, total):
    total[...] = jnp.zeros_like(total)
    total[:PREFIX] = joined(total_ref)
    out_ref[...] = exact_nt(total[...], w2_ref[0])


def hidden_back(total, w2):
    return pl.pallas_call(
        hidden_kernel,
        in_specs=[IN_VMEM] * 2,
        out_specs=IN_VMEM,
        scratch_shapes=[pltpu.VMEM((SLOTS, 2 * D), F32)],
        out_shape=jax.ShapeDtypeStruct((SLOTS, w2.shape[1]), F32),
        compiler_params=params(),
        cost_estimate=cost(2),
        name="hidden_back",
    )(total, w2)


def slots(ref, scratch):
    scratch[...] = jnp.zeros_like(scratch)
    scratch[:PREFIX] = ref[...].astype(F32)
    return scratch[...]


def second_kernel(total_ref, hidden_ref, w2_out, b2_out, total, hidden):
    total[...] = jnp.zeros_like(total)
    total[:PREFIX] = joined(total_ref)
    units = slots(hidden_ref, hidden)
    for columns in row_tiles(2 * D, 512):
        w2_out[0, :, columns] = exact_tn(units, total[:, columns])
    b2_out[...] = jnp.sum(total[...], axis=0, keepdims=True)


def second_back(total, hidden):
    rh = hidden.shape[1]
    return pl.pallas_call(
        second_kernel,
        in_specs=[IN_VMEM] * 2,
        out_specs=[IN_VMEM] * 2,
        scratch_shapes=[pltpu.VMEM((SLOTS, 2 * D), F32), pltpu.VMEM((SLOTS, rh), F32)],
        out_shape=[
            jax.ShapeDtypeStruct((1, rh, 2 * D), F32),
            jax.ShapeDtypeStruct((1, 2 * D), F32),
        ],
        compiler_params=params(),
        cost_estimate=cost(3),
        name="second_back",
    )(total, hidden)


def last_kernel(
    spot_ref,
    own_ref,
    other_ref,
    hidden_ref,
    table_ref,
    w1_ref,
    outputs_in,
    top_ref,
    bottom_ref,
    table_out,
    w1_out,
    b1_out,
    outputs_ref,
    hidden,
    table,
    buffer,
    semaphores,
):
    del outputs_in
    half = D // 2
    pieces = [(top_ref, slice(0, half)), (bottom_ref, slice(half, D))]
    loads = [
        pltpu.make_async_copy(piece.at[0], buffer.at[rows], semaphores.at[0, index])
        for index, (piece, rows) in enumerate(pieces)
    ]
    stores = [
        pltpu.make_async_copy(buffer.at[rows], outputs_ref.at[1, rows], semaphores.at[1, index])
        for index, (_, rows) in enumerate(pieces)
    ]

    @pl.when(spot_ref[0] == 0)
    def _():
        for load in loads:
            load.start()

    units = slots(hidden_ref, hidden)
    grad_pre = (own_ref[...] + other_ref[...]) * (1.0 - units * units)
    b1_out[...] = jnp.sum(grad_pre, axis=0, keepdims=True)
    table_out[...] = exact_nt(grad_pre, w1_ref[...])[:PREFIX]

    @pl.when(spot_ref[0] == 0)
    def _():
        for load, store in zip(loads, stores):
            load.wait()
            store.start()

    w1_out[...] = exact_tn(slots(table_ref, table), grad_pre)

    @pl.when(spot_ref[0] == 0)
    def _():
        for store in stores:
            store.wait()


def last_block(spot, own, other, hidden, table, w1, outputs, pieces):
    rh = w1.shape[1]
    return pl.pallas_call(
        last_kernel,
        in_specs=[SCALARS] + [IN_VMEM] * 5 + [ANY] * 3,
        out_specs=[IN_VMEM] * 3 + [ANY],
        scratch_shapes=[
            pltpu.VMEM((SLOTS, rh), F32),
            pltpu.VMEM((SLOTS, D), F32),
            whole_scratch(BF16),
            pltpu.SemaphoreType.DMA((2, 2)),
        ],
        out_shape=[
            jax.ShapeDtypeStruct((PREFIX, D), F32),
            jax.ShapeDtypeStruct(w1.shape, F32),
            jax.ShapeDtypeStruct((1, rh), F32),
            jax.ShapeDtypeStruct(outputs.shape, outputs.dtype),
        ],
        input_output_aliases={6: 3},
        compiler_params=params(),
        cost_estimate=cost(3),
        name="last_block",
    )(spot, own, other, hidden, table, w1, outputs, *pieces)


def swap_sections(values):
    return lax.ppermute(values, "section", [(0, 1), (1, 0)])


def per_section(section_index, own):
    other = swap_sections(own)
    is_first = section_index == 0
    return jnp.where(is_first, own, other), jnp.where(is_first, other, own)


def halves(w_qkv, w_out, w_fc, w_proj):
    columns = lambda matrix: jnp.moveaxis(matrix.reshape(SHARD_ROWS, -1, D), 1, 0)
    attention = jnp.concatenate([columns(w_qkv), w_out[None]], axis=0).reshape(2, HALF, D)
    up = columns(w_fc).reshape(2, HALF, D)
    down = w_proj.reshape(2, HALF, D)
    return jnp.stack([attention, up, down], axis=1)


def gather_weights(is_first, w_qkv, w_out, w_fc, w_proj):
    if D // w_qkv.shape[1] == SHARDS:
        own = halves(w_qkv[0], w_out[0], w_fc[0], w_proj[0])
        received = swap_sections(jnp.where(is_first, own[1], own[0]))
        first = jnp.where(is_first, own[0], received)
        last = jnp.where(is_first, received, own[1])
        early = jnp.concatenate([first.reshape(3 * HALF, D), last[0]], axis=0)
        gather = lambda rows: lax.all_gather(rows, ("dp", "section"), axis=0).reshape(
            SHARDS, 2, -1, D
        )
        early, late = gather(early), gather(last[1:].reshape(2 * HALF, D))
    else:
        whole = lambda matrix: lax.all_gather(matrix[0], ("dp", "section"), axis=0)
        every = [whole(matrix) for matrix in (w_qkv, w_out, w_fc, w_proj)]
        layers = []
        for layer in range(2):
            mine = [matrix[layer::2] for matrix in every]
            shards = [matrix.reshape(SHARDS, -1, matrix.shape[-1]) for matrix in mine]
            layers.append(jax.vmap(halves)(*shards).reshape(SHARDS, 2, 3 * HALF, D))
        early = jnp.concatenate([layers[0], layers[1][:, :, :HALF]], axis=2)
        late = layers[1][:, :, HALF:]
    return (
        [(early, 0), (early, HALF), (early, 2 * HALF)],
        [(early, 3 * HALF), (late, 0), (late, HALF)],
    )


def reparam_hidden(table, w_first, b_first):
    return jnp.tanh(jnp.dot(table, w_first, precision=highest_mode) + b_first)


def reparam_out(hidden_units, w_second, b_second):
    return jnp.dot(hidden_units, w_second, precision=highest_mode) + b_second


def sum_dp(values):
    count = lax.axis_size("dp")
    moved = lambda bits: lax.ppermute(values, "dp", [(i, i ^ bits) for i in range(count)])
    step = count
    while step > 1:
        if step % 4 == 0:
            step //= 4
            values = (values + moved(step)) + (moved(2 * step) + moved(3 * step))
        else:
            step //= 2
            values = values + moved(step)
    return values


def per_device(
    tokens,
    seq_length,
    cotangent,
    ln_gain,
    ln_bias,
    w_qkv,
    w_out,
    w_fc,
    w_proj,
    prefix_table,
    reparam_w1,
    reparam_b1,
    reparam_w2,
    reparam_b2,
):
    section_index = lax.axis_index("section")
    is_first = section_index == 0
    first, last = gather_weights(is_first, w_qkv, w_out, w_fc, w_proj)
    spot = jnp.stack([section_index, jnp.zeros_like(section_index)]).astype(jnp.int32)
    seq = lax.dynamic_slice_in_dim(seq_length, section_index, 1, 0)

    table_values = prefix_table.astype(F32)
    first_weight = reparam_w1.astype(F32)
    first_bias = reparam_b1.astype(F32)
    second_weight = reparam_w2[0].astype(F32)
    second_bias = reparam_b2[0].astype(F32)
    hidden_units = reparam_hidden(table_values, first_weight, first_bias)
    prefix_kv = reparam_out(hidden_units, second_weight, second_bias).astype(BF16)
    pad = ((0, SLOTS - PREFIX), (0, 0))
    small = jnp.concatenate(
        [
            jnp.pad(prefix_kv[:, :D], pad),
            jnp.pad(prefix_kv[:, D:], pad),
            ln_gain[0],
            ln_bias[0],
            jnp.zeros((4, D), BF16),
        ],
        axis=0,
    )
    small_pair = per_section(section_index, small)
    pairs_apart = lambda rows: jnp.moveaxis(rows.reshape(SLOTS, PAIRS, PAIR_DIM), 1, 0)
    prefix_pair = [
        (pairs_apart(part[:SLOTS]), pairs_apart(part[SLOTS : 2 * SLOTS])) for part in small_pair
    ]
    norm_pair = [part[2 * SLOTS :].astype(F32) for part in small_pair]

    prefix_first, prefix_last = prefix_pair
    projected_first = project(spot, 0, tokens, norm_pair[0], first[0])
    attended_first, *probs_first = attend(seq, projected_first, *prefix_first)
    middle_first, normed = middle_block(spot, 0, attended_first, tokens, norm_pair[0], first[0])
    slope, handed = forward_block(normed, middle_first, *first[1:])
    projected = project(spot, 1, handed, norm_pair[1], last[0])
    attended, *probs = attend(seq, projected, *prefix_last)
    middle, normed = middle_block(spot, 1, attended, handed, norm_pair[1], last[0])
    final, sent, grad_middle, grad_attended = turn_block(
        spot, normed, middle, cotangent, handed, norm_pair[1], *last
    )
    received = swap_sections(sent)
    grads, prefix_grad_last = attend_back(
        seq, projected, attended, grad_attended, *prefix_last, *probs
    )
    grad_handed = unproject(spot, 1, grads, handed, grad_middle, norm_pair[1], last[0])
    received_grad = lax.ppermute(grad_handed, "section", [(0, 1)])
    activations, grad_middle, grad_attended = backward_block(
        spot, grad_handed, slope, middle_first, (handed, final, received), norm_pair[0], *first
    )
    grads, prefix_grad_first = attend_back(
        seq,
        projected_first,
        attended_first,
        grad_attended,
        *prefix_first,
        *probs_first,
    )
    input_grads, *pieces = unproject(
        spot,
        0,
        grads,
        tokens,
        grad_middle,
        norm_pair[0],
        first[0],
        (grad_handed, received_grad),
    )
    pieces = [lax.ppermute(piece, "section", [(1, 0)]) for piece in pieces]

    kept = jnp.where(is_first, prefix_grad_first, prefix_grad_last)
    sent = jnp.where(is_first, prefix_grad_last, prefix_grad_first)
    total = sum_dp(kept + swap_sections(sent))
    grad_hidden = hidden_back(total, reparam_w2)
    grad_w2, grad_b2 = second_back(total, hidden_units)
    grad_table, grad_w1, grad_b1, input_grads = last_block(
        spot,
        grad_hidden,
        swap_sections(grad_hidden),
        hidden_units,
        prefix_table,
        reparam_w1,
        input_grads,
        pieces,
    )
    return (
        activations[None],
        input_grads[None],
        grad_table,
        grad_w1,
        grad_b1[0],
        grad_w2,
        grad_b2,
    )


def solution(mesh):
    in_specs = (
        P("dp", None, None),
        P("dp"),
        P("dp", None, None),
        P("section", None, None),
        P("section", None, None),
        P("section", "dp", None),
        P("section", "dp", None),
        P("section", "dp", None),
        P("section", "dp", None),
        P(),
        P(),
        P(),
        P("section", None, None),
        P("section", None),
    )
    out_specs = (
        P("section", "dp", None, None),
        P("section", "dp", None, None),
        P(),
        P(),
        P(),
        P("section", None, None),
        P("section", None),
    )
    return jax.shard_map(
        per_device, mesh=mesh, in_specs=in_specs, out_specs=out_specs, check_vma=False
    )
```

```python
import functools

import jax
import jax.numpy as jnp
from jax import lax
from jax.experimental import pallas as pl
from jax.experimental.pallas import tpu as pltpu
from jax.sharding import PartitionSpec as P

D = 1024
HEADS = 16
HEAD_DIM = 64
FF = 4096
PREFIX = 10
SLOTS = 16
BOTH = 24
PAIRS = 8
PAIR_DIM = 128
BLOCK = 256

eps_norm = 1e-05
neg_big = -1e30
highest_mode = lax.Precision.HIGHEST
F32 = jnp.float32
BF16 = jnp.bfloat16


def dot(left, right, dims):
    return lax.dot_general(left, right, (dims, ((), ())), preferred_element_type=F32)


def dot_nn(left, right):
    return dot(left, right, ((1,), (0,)))


def dot_nt(left, right):
    return dot(left, right, ((1,), (1,)))


def dot_tn(left, right):
    return dot(left, right, ((0,), (0,)))


def normalised(values):
    centre = jnp.mean(values, axis=-1, keepdims=True)
    spread = values - centre
    variance = jnp.mean(spread * spread, axis=-1, keepdims=True)
    inverse = lax.rsqrt(variance + eps_norm)
    return spread * inverse, inverse


def layer_norm(values, gain, offset):
    return normalised(values)[0] * gain + offset


def norm_back(values, gain, upstream):
    unit, inverse = normalised(values)
    scaled = upstream * gain
    mean_scaled = jnp.mean(scaled, axis=-1, keepdims=True)
    mean_unit = jnp.mean(scaled * unit, axis=-1, keepdims=True)
    return (scaled - mean_scaled - unit * mean_unit) * inverse


SQRT_2_PI = 0.7978845608028654
CUBIC = 0.044715


def gelu_pair(values):
    cubic_part = (SQRT_2_PI * CUBIC) * (values * values)
    half_tanh = 0.5 + 0.5 * jnp.tanh(values * (SQRT_2_PI + cubic_part))
    out = values * half_tanh
    slope = half_tanh + out * ((2.0 - 2.0 * half_tanh) * (SQRT_2_PI + 3.0 * cubic_part))
    return out, slope


def params(mebibytes=62):
    return pltpu.CompilerParams(vmem_limit_bytes=mebibytes * 2**20)


def cost(micros):
    return pl.CostEstimate(flops=int(micros * 1.15e9), bytes_accessed=2**20, transcendentals=0)


SHARDS = 16
HALF = 128
SHARD_ROWS = 64
BLOCKS = FF // D


def load_across(array, half, row, target, semaphore):
    return pltpu.make_async_copy(array.at[:, half, pl.ds(row, SHARD_ROWS)], target, semaphore)


def load_qkv(array, row, part, weights, semaphores):
    half, inner = divmod(part, 2)
    return load_across(
        array, half, row + inner * SHARD_ROWS, weights.at[part], semaphores.at[part]
    )


def load_out(array, row, target, semaphore):
    return load_across(array, 1, row + SHARD_ROWS, target, semaphore)


def load_up(array, row, block, target, semaphore):
    half, inner = divmod(block, 2)
    return load_across(array, half, row + inner * SHARD_ROWS, target, semaphore)


def load_down(array, row, block, target, semaphore):
    few = SHARDS // BLOCKS
    return pltpu.make_async_copy(
        array.at[pl.ds(block * few, few), :, pl.ds(row, HALF)], target, semaphore
    )


def across_scratch(count):
    return pltpu.VMEM((count, SHARDS, SHARD_ROWS, D), BF16)


def down_scratch():
    return pltpu.VMEM((BLOCKS, SHARDS // BLOCKS, 2, HALF, D), BF16)


def matrix(ref, *index):
    return ref[index].reshape(D, D) if index else ref[...].reshape(D, D)


ANY = pl.BlockSpec(memory_space=pl.ANY)
TILE = 512
SCALARS = pl.BlockSpec(memory_space=pltpu.SMEM)
IN_VMEM = pl.BlockSpec(memory_space=pltpu.VMEM)


def whole_scratch(dtype):
    return pltpu.VMEM((D, D), dtype)


def once(shape, index):
    return pl.BlockSpec(shape, index, pipeline_mode=pl.Buffered(1))


def row_tiles(length, size):
    return [slice(start, start + size) for start in range(0, length, size)]


CHUNK = 16


def put_pairs(ref, rows, values):
    for pair in range(PAIRS):
        ref[pair, rows] = values[:, pair * PAIR_DIM : (pair + 1) * PAIR_DIM]


def get_pairs(ref, rows, *lead):
    return jnp.concatenate([ref[(*lead, pair, rows)] for pair in range(PAIRS)], axis=1)


def chunks(rows, size=CHUNK):
    return [slice(start, start + size) for start in range(rows.start, rows.stop, size)]


def shifted(rows, by):
    return slice(rows.start + by, rows.stop + by)


def qkv_kernel(row, spot_ref, hidden_ref, norm_ref, array, out_ref, normed, weights, semaphores):
    step = pl.program_id(0)
    loads = [load_qkv(array, row, part, weights, semaphores) for part in range(3)]
    length = hidden_ref.shape[1]
    tiles = row_tiles(length, 256)

    @pl.when(step == 0)
    def _():
        loads[0].start()
        gain, offset = norm_ref[0:1], norm_ref[2:3]

        def norm(tile):
            for rows in chunks(tile):
                values = hidden_ref[0, rows].astype(F32)
                normed[rows] = layer_norm(values, gain, offset).astype(BF16)

        norm(tiles[0])
        loads[0].wait()
        loads[1].start()
        loads[2].start()
        for index, rows in enumerate(tiles):
            if index + 1 < len(tiles):
                norm(tiles[index + 1])
            queries = dot_nn(normed[rows], matrix(weights, 0))
            put_pairs(out_ref, rows, (queries * HEAD_DIM**-0.5).astype(BF16))

    for part in (1, 2):

        @pl.when(step == part)
        def _(part=part):
            loads[part].wait()
            for rows in tiles:
                put_pairs(out_ref, rows, dot_nn(normed[rows], matrix(weights, part)).astype(BF16))


def project(spot, which, hidden, norms, place):
    length = hidden.shape[1]
    return pl.pallas_call(
        functools.partial(qkv_kernel, place[1]),
        grid_spec=pltpu.PrefetchScalarGridSpec(
            num_scalar_prefetch=1,
            grid=(3,),
            in_specs=[
                once((1, length, D), lambda j, s: (s[which], 0, 0)),
                once((8, D), lambda j, s: (0, 0)),
                ANY,
            ],
            out_specs=pl.BlockSpec((PAIRS, length, PAIR_DIM), lambda j, s: (j, 0, 0)),
            scratch_shapes=[
                pltpu.VMEM((length, D), BF16),
                across_scratch(3),
                pltpu.SemaphoreType.DMA((3,)),
            ],
        ),
        out_shape=jax.ShapeDtypeStruct((3 * PAIRS, length, PAIR_DIM), BF16),
        compiler_params=params(),
        cost_estimate=cost(12),
        name="norm_project",
    )(spot, hidden, norms, place[0])


def lane_halves(block):
    lanes = lax.broadcasted_iota(jnp.int32, block.shape, 1)
    zero = jnp.zeros_like(block)
    return jnp.where(lanes < HEAD_DIM, block, zero), jnp.where(lanes < HEAD_DIM, zero, block)


def key_spans(first, stop):
    if first == 0:
        return [slice(0, SLOTS + stop)]
    return [slice(0, SLOTS), slice(SLOTS + first, SLOTS + stop)]


def read_spans(ref, spans, *rest):
    parts = [ref[(span, *rest)] for span in spans]
    return parts[0] if len(parts) == 1 else jnp.concatenate(parts, axis=0)


def cut_spans(values, spans):
    start = 0
    for span in spans:
        size = span.stop - span.start
        yield span, values[start : start + size]
        start += size


def strips(length, short):
    return [
        (rows, slice(2 * rows.start, 2 * rows.stop), rows.start if short else 0)
        for rows in row_tiles(length, BLOCK)
    ]


def stacked_halves(block):
    return jnp.concatenate(lane_halves(block), axis=0)


def own_heads(product):
    return jnp.concatenate([product[:HEAD_DIM, :BLOCK], product[HEAD_DIM:, BLOCK:]], axis=0)


def either_length(length_ref, length, run):
    short = length_ref[0] < length
    pl.when(short)(lambda: run(True))
    pl.when(jnp.logical_not(short))(lambda: run(False))


def allowed(rows, first_diagonal):
    shape = (rows.stop - rows.start, 2 * BLOCK)
    keys = lax.broadcasted_iota(jnp.int32, shape, 0) + rows.start
    if rows.stop <= SLOTS:
        return keys < PREFIX
    queries = lax.broadcasted_iota(jnp.int32, shape, 1) % BLOCK
    return keys - first_diagonal <= queries


def eight_rows(values, reduce):
    return reduce(values.reshape(-1, 8, values.shape[-1]), axis=0)


def attend_kernel(
    seq_ref, q_ref, k_ref, v_ref, kp_ref, vp_ref, out_ref, probs_ref, scale_ref, keys, values_t, scores
):
    length = q_ref.shape[1]
    keys[:SLOTS], keys[SLOTS:] = kp_ref[0], k_ref[0]
    values_t[...] = v_ref[0].T
    prefix_values = vp_ref[0]

    def run(short):
        def scored(strip, slot):
            rows, _, first = strip
            count = SLOTS + rows.stop - first
            scores[slot, :count] = dot_nt(
                read_spans(keys, key_spans(first, rows.stop)), stacked_halves(q_ref[0, rows])
            )

        todo = strips(length, short)
        scored(todo[0], 0)
        for index, (rows, columns, first) in enumerate(todo):
            slot = index % 2
            if index + 1 < len(todo):
                scored(todo[index + 1], 1 - slot)
            count = SLOTS + rows.stop - first
            parts = chunks(slice(0, count))
            top = None
            for part in parts:
                values = scores[slot, part]
                if part.stop <= SLOTS or part.start >= count - BLOCK:
                    values = jnp.where(allowed(part, count - BLOCK), values, neg_big)
                    scores[slot, part] = values
                values = eight_rows(values, jnp.max)
                top = values if top is None else jnp.maximum(top, values)
            top = jnp.max(top, axis=0, keepdims=True)
            total = None
            for part in parts:
                values = jnp.exp(scores[slot, part] - top)
                place = part if part.stop <= SLOTS else shifted(part, first)
                probs_ref[0, place, columns] = values.astype(BF16)
                values = eight_rows(values, jnp.sum)
                total = values if total is None else total + values
            inverse = 1.0 / jnp.sum(total, axis=0, keepdims=True)
            both = dot_nn(
                values_t[:, first : rows.stop],
                probs_ref[0, SLOTS + first : SLOTS + rows.stop, columns],
            ) + dot_tn(prefix_values, probs_ref[0, :SLOTS, columns])
            inverse = jnp.concatenate(
                [
                    jnp.broadcast_to(inverse[:, :BLOCK], (HEAD_DIM, BLOCK)),
                    jnp.broadcast_to(inverse[:, BLOCK:], (HEAD_DIM, BLOCK)),
                ],
                axis=0,
            )
            out_ref[0, rows] = (own_heads(both) * inverse).T.astype(BF16)
            scale_ref[0, rows] = inverse.T

    either_length(seq_ref, length, run)


def pair_spec(length, part):
    return pl.BlockSpec((1, length, PAIR_DIM), lambda p, s: (part * PAIRS + p, 0, 0))


def probs_spec(length):
    return pl.BlockSpec((1, SLOTS + length, 2 * length), lambda p, s: (p, 0, 0))


def attend(seq, projected, prefix_keys, prefix_values):
    length = projected.shape[1]
    return pl.pallas_call(
        attend_kernel,
        grid_spec=pltpu.PrefetchScalarGridSpec(
            num_scalar_prefetch=1,
            grid=(PAIRS,),
            in_specs=[
                pair_spec(length, 0),
                pair_spec(length, 1),
                pair_spec(length, 2),
                pair_spec(SLOTS, 0),
                pair_spec(SLOTS, 0),
            ],
            out_specs=[pair_spec(length, 0), probs_spec(length), pair_spec(length, 0)],
            scratch_shapes=[
                pltpu.VMEM((SLOTS + length, PAIR_DIM), BF16),
                pltpu.VMEM((PAIR_DIM, length), BF16),
                pltpu.VMEM((2, SLOTS + length, 2 * BLOCK), F32),
            ],
        ),
        out_shape=[
            jax.ShapeDtypeStruct((PAIRS, length, PAIR_DIM), BF16),
            jax.ShapeDtypeStruct((PAIRS, SLOTS + length, 2 * length), BF16),
            jax.ShapeDtypeStruct((PAIRS, length, PAIR_DIM), F32),
        ],
        compiler_params=params(),
        cost_estimate=cost(30),
        name="attend",
    )(seq, projected, projected, projected, prefix_keys, prefix_values)


def attend_back_kernel(
    seq_ref,
    q_ref,
    k_ref,
    v_ref,
    out_ref,
    grad_ref,
    kp_ref,
    vp_ref,
    probs_ref,
    scale_ref,
    grads_ref,
    prefix_ref,
    values,
    keys_t,
    dk,
    dv,
    dprobs,
    ds,
):
    length = q_ref.shape[1]
    values[:SLOTS], values[SLOTS:] = vp_ref[0], v_ref[0]
    keys_t[...] = k_ref[0].T
    prefix_keys = kp_ref[0]
    dk[...] = jnp.zeros_like(dk)
    dv[...] = jnp.zeros_like(dv)

    def run(short):
        def prepared(strip, slot):
            rows, _, first = strip
            grads = (grad_ref[0, rows].astype(F32) * scale_ref[0, rows]).astype(BF16)
            halves = stacked_halves(grads)
            weighted_t = (grads.astype(F32) * out_ref[0, rows].astype(F32)).T
            centre = jnp.concatenate(
                [
                    jnp.sum(weighted_t[:HEAD_DIM], axis=0, keepdims=True),
                    jnp.sum(weighted_t[HEAD_DIM:], axis=0, keepdims=True),
                ],
                axis=1,
            )
            dprobs[slot, : SLOTS + rows.stop - first] = dot_nt(
                read_spans(values, key_spans(first, rows.stop)), halves
            )
            return halves, centre

        todo = strips(length, short)
        ahead = prepared(todo[0], 0)
        for index, (rows, columns, first) in enumerate(todo):
            slot = index % 2
            spans = key_spans(first, rows.stop)
            grad_halves, centre = ahead
            if index + 1 < len(todo):
                ahead = prepared(todo[index + 1], 1 - slot)
            count = SLOTS + rows.stop - first
            for part in chunks(slice(0, count)):
                place = part if part.stop <= SLOTS else shifted(part, first)
                probs = probs_ref[0, place, columns].astype(F32)
                ds[slot, part] = (probs * (dprobs[slot, part] - centre)).astype(BF16)
            for total, left, right in (
                (dv, read_spans(probs_ref.at[0], spans, columns), grad_halves),
                (dk, ds[slot, :count], stacked_halves(q_ref[0, rows])),
            ):
                for span, part in cut_spans(dot_nn(left, right), spans):
                    total[span] += part
            both = dot_nn(keys_t[:, first : rows.stop], ds[slot, SLOTS:count]) + dot_tn(
                prefix_keys, ds[slot, :SLOTS]
            )
            grads_ref[0, 0, rows] = (own_heads(both).T * HEAD_DIM**-0.5).astype(BF16)

    either_length(seq_ref, length, run)
    grads_ref[1, 0] = dk[SLOTS:].astype(BF16)
    grads_ref[2, 0] = dv[SLOTS:].astype(BF16)
    prefix_ref[0, :PREFIX] = dk[:PREFIX]
    prefix_ref[0, PREFIX : 2 * PREFIX] = dv[:PREFIX]
    prefix_ref[0, 2 * PREFIX :] = jnp.zeros_like(prefix_ref[0, 2 * PREFIX :])


def attend_back(seq, projected, attended, grad_attended, prefix_keys, prefix_values, probs, scale):
    length = projected.shape[1]
    ext = (SLOTS + length, PAIR_DIM)
    return pl.pallas_call(
        attend_back_kernel,
        grid_spec=pltpu.PrefetchScalarGridSpec(
            num_scalar_prefetch=1,
            grid=(PAIRS,),
            in_specs=[
                pair_spec(length, 0),
                pair_spec(length, 1),
                pair_spec(length, 2),
                pair_spec(length, 0),
                pair_spec(length, 0),
                pair_spec(SLOTS, 0),
                pair_spec(SLOTS, 0),
                probs_spec(length),
                pair_spec(length, 0),
            ],
            out_specs=[
                pl.BlockSpec((3, 1, length, PAIR_DIM), lambda p, s: (0, p, 0, 0)),
                pair_spec(BOTH, 0),
            ],
            scratch_shapes=[
                pltpu.VMEM(ext, BF16),
                pltpu.VMEM((PAIR_DIM, length), BF16),
                pltpu.VMEM(ext, F32),
                pltpu.VMEM(ext, F32),
                pltpu.VMEM((2, SLOTS + length, 2 * BLOCK), F32),
                pltpu.VMEM((2, SLOTS + length, 2 * BLOCK), BF16),
            ],
        ),
        out_shape=[
            jax.ShapeDtypeStruct((3, PAIRS, length, PAIR_DIM), BF16),
            jax.ShapeDtypeStruct((PAIRS, BOTH, PAIR_DIM), F32),
        ],
        compiler_params=params(),
        cost_estimate=cost(30),
        name="attend_back",
    )(
        seq,
        projected,
        projected,
        projected,
        attended,
        grad_attended,
        prefix_keys,
        prefix_values,
        probs,
        scale,
    )


def middle_kernel(
    row,
    which,
    spot_ref,
    norm_ref,
    attended_ref,
    hidden_ref,
    array,
    middle_ref,
    normed_ref,
    attended,
    hidden,
    middle,
    normed,
    weights,
    semaphores,
    load_semaphores,
    store_semaphores,
):
    copy = pltpu.make_async_copy
    tiles = row_tiles(D, 256)
    get_weights = load_out(array, row, weights, semaphores.at[0])
    get_attended = [
        copy(attended_ref.at[:, rows], attended.at[:, rows], load_semaphores.at[0, index])
        for index, rows in enumerate(tiles)
    ]
    get_hidden = [
        copy(hidden_ref.at[spot_ref[which], rows], hidden.at[rows], load_semaphores.at[1, index])
        for index, rows in enumerate(tiles)
    ]
    get_weights.start()
    for loads in zip(get_attended, get_hidden):
        for load in loads:
            load.start()
    gain, offset = norm_ref[1:2], norm_ref[3:4]
    stores = []

    def finish(index, rows):
        get_hidden[index].wait()
        for part in chunks(rows):
            values = hidden[part].astype(F32) + middle[part]
            middle[part] = values
            normed[part] = layer_norm(values, gain, offset).astype(BF16)
        for source, target, kind in ((middle, middle_ref, 0), (normed, normed_ref, 1)):
            stores.append(copy(source.at[rows], target.at[rows], store_semaphores.at[kind, index]))
            stores[-1].start()

    get_weights.wait()
    for index, rows in enumerate(tiles):
        get_attended[index].wait()
        middle[rows] = dot_nn(get_pairs(attended, rows), matrix(weights))
        if index:
            finish(index - 1, tiles[index - 1])
    finish(len(tiles) - 1, tiles[-1])
    for store in stores:
        store.wait()


def middle_block(spot, which, attended, hidden, norms, place):
    length = attended.shape[1]
    count = D // 256
    return pl.pallas_call(
        functools.partial(middle_kernel, place[1], which),
        in_specs=[SCALARS, IN_VMEM] + [ANY] * 3,
        out_specs=[ANY] * 2,
        scratch_shapes=[
            pltpu.VMEM((PAIRS, D, PAIR_DIM), BF16),
            whole_scratch(BF16),
            whole_scratch(F32),
            whole_scratch(BF16),
            pltpu.VMEM((SHARDS, SHARD_ROWS, D), BF16),
            pltpu.SemaphoreType.DMA((1,)),
            pltpu.SemaphoreType.DMA((2, count)),
            pltpu.SemaphoreType.DMA((2, count)),
        ],
        out_shape=[
            jax.ShapeDtypeStruct((length, D), F32),
            jax.ShapeDtypeStruct((length, D), BF16),
        ],
        compiler_params=params(),
        cost_estimate=cost(5),
        name="middle_block",
    )(spot, norms, attended, hidden, place[0])


def feed_forward_loads(up, down, rows, up_weights, down_weights, semaphores):
    return [
        (
            load_up(up, rows[0], block, up_weights.at[block], semaphores.at[0, block]),
            load_down(down, rows[1], block, down_weights.at[block], semaphores.at[1, block]),
        )
        for block in range(BLOCKS)
    ]


def start_all(loads):
    for pair in loads:
        for load in pair:
            load.start()


def wait_step(loads, step):
    for block, pair in enumerate(loads):

        @pl.when(step == block)
        def _(pair=pair):
            for load in pair:
                load.wait()


def wait_for(target, semaphore):
    pltpu.make_async_copy(target, target, semaphore).wait()


def feed_forward_scratch():
    return [across_scratch(BLOCKS), down_scratch(), pltpu.SemaphoreType.DMA((2, BLOCKS))]


def forward_kernel(
    rows_at,
    normed_ref,
    middle_ref,
    up,
    down,
    slope_ref,
    out_ref,
    total,
    inner,
    activated,
    up_weights,
    down_weights,
    semaphores,
):
    step = pl.program_id(0)
    tiles = row_tiles(middle_ref.shape[0], TILE)
    loads = feed_forward_loads(up, down, rows_at, up_weights, down_weights, semaphores)

    @pl.when(step == 0)
    def _():
        start_all(loads[:1])
        total[...] = middle_ref[...]

    wait_step(loads, step)
    for later in range(1, BLOCKS):
        pl.when(step == later - 1)(lambda later=later: start_all(loads[later : later + 1]))
    w_fc, w_proj = matrix(up_weights, step), matrix(down_weights, step)
    inner[tiles[0]] = dot_nn(normed_ref[tiles[0]], w_fc)
    for index, rows in enumerate(tiles):
        if index + 1 < len(tiles):
            inner[tiles[index + 1]] = dot_nn(normed_ref[tiles[index + 1]], w_fc)
        for part in chunks(rows):
            value, slope = gelu_pair(inner[part])
            activated[part] = value.astype(BF16)
            slope_ref[part] = slope.astype(BF16)
        total[rows] += dot_nn(activated[rows], w_proj)

    @pl.when(step == pl.num_programs(0) - 1)
    def _():
        out_ref[0] = total[...].astype(BF16)


def forward_block(normed, middle, up, down):
    length = normed.shape[0]
    whole = lambda j: (0, 0)
    return pl.pallas_call(
        functools.partial(forward_kernel, (up[1], down[1])),
        grid=(BLOCKS,),
        in_specs=[once((length, D), whole), once((length, D), whole), ANY, ANY],
        out_specs=[
            pl.BlockSpec((length, D), lambda j: (0, j)),
            once((1, length, D), lambda j: (0, 0, 0)),
        ],
        scratch_shapes=[whole_scratch(F32), whole_scratch(F32), whole_scratch(BF16)]
        + feed_forward_scratch(),
        out_shape=[
            jax.ShapeDtypeStruct((length, FF), BF16),
            jax.ShapeDtypeStruct((1, length, D), BF16),
        ],
        compiler_params=params(),
        cost_estimate=cost(25),
        name="forward_block",
    )(normed, middle, up[0], down[0])


FINISH = 256


def finish_backward(upstream, middle, grad_total, norm_ref, w_out, grad_middle, grad_attended, stores):
    gain = norm_ref[1:2]
    for index, rows in enumerate(row_tiles(D, FINISH)):
        for part in chunks(rows):
            grad = upstream[part].astype(F32) + norm_back(middle[part], gain, grad_total[part])
            grad_middle[part] = grad.astype(BF16)
        put_pairs(grad_attended, rows, dot_nt(grad_middle[rows], w_out).astype(BF16))
        for store in stores(rows, index):
            store.start()
    for index, rows in enumerate(row_tiles(D, FINISH)):
        for store in stores(rows, index):
            store.wait()


def turn_kernel(
    rows_at,
    spot_ref,
    norm_ref,
    normed_ref,
    middle_ref,
    upstream_ref,
    hidden_ref,
    attention,
    up,
    down,
    out_ref,
    sent_ref,
    grad_middle_ref,
    grad_attended_ref,
    normed,
    middle,
    upstream,
    total,
    grad_total,
    inner,
    grad_act,
    out,
    grad_middle,
    grad_attended,
    up_weights,
    down_weights,
    out_weights,
    semaphores,
    load_semaphores,
    store_semaphores,
):
    activated, grad_inner = grad_middle, out
    loads = feed_forward_loads(up, down, rows_at[1:], up_weights, down_weights, semaphores)
    copy = pltpu.make_async_copy
    get_normed = copy(normed_ref, normed, load_semaphores.at[0])
    get_upstream = copy(upstream_ref.at[spot_ref[0]], upstream, load_semaphores.at[1])
    get_middle = copy(middle_ref, middle, load_semaphores.at[2])
    get_out = load_out(attention, rows_at[0], out_weights, load_semaphores.at[3])
    get_normed.start()
    loads[0][0].start()
    total[...] = jnp.zeros_like(total)
    grad_total[...] = jnp.zeros_like(grad_total)
    get_normed.wait()
    get_upstream.start()
    loads[0][1].start()

    def step(block, carry):
        wait_for(up_weights.at[block], semaphores.at[0, block])
        tiles = row_tiles(D, TILE)
        w_fc = matrix(up_weights, block)
        inner[0] = dot_nn(normed[tiles[0]], w_fc)
        pl.when(block == 0)(get_upstream.wait)
        wait_for(down_weights.at[block], semaphores.at[1, block])
        w_proj = matrix(down_weights, block)
        for later in range(1, BLOCKS):
            pl.when(block == later - 1)(lambda later=later: start_all(loads[later : later + 1]))

        @pl.when(block == BLOCKS - 1)
        def _():
            get_middle.start()
            get_out.start()

        grad_act[0] = dot_nt(upstream[tiles[0]], w_proj)
        for index, rows in enumerate(tiles):
            slot = index % 2
            if index + 1 < len(tiles):
                inner[1 - slot] = dot_nn(normed[tiles[index + 1]], w_fc)
                grad_act[1 - slot] = dot_nt(upstream[tiles[index + 1]], w_proj)
            for part in chunks(rows):
                here = shifted(part, -rows.start)
                value, slope = gelu_pair(inner[slot, here])
                activated[part] = value.astype(BF16)
                grad_inner[part] = (grad_act[slot, here] * slope).astype(BF16)
            total[rows] += dot_nn(activated[rows], w_proj)
            grad_total[rows] += dot_nt(grad_inner[rows], w_fc)
        return carry

    lax.fori_loop(0, BLOCKS, step, 0)
    get_middle.wait()
    for part in chunks(slice(0, D)):
        out[part] = (total[part] + middle[part]).astype(BF16)
    put_out = copy(out, out_ref.at[0], store_semaphores.at[0, 0])
    put_out.start()
    put_sent = copy(out, sent_ref.at[0], store_semaphores.at[0, 1])
    get_hidden = copy(hidden_ref.at[0], normed, load_semaphores.at[4])
    put_hidden = copy(normed, sent_ref.at[0], store_semaphores.at[0, 1])
    pl.when(spot_ref[0] == 0)(put_sent.start)
    pl.when(spot_ref[0] != 0)(get_hidden.start)
    get_out.wait()

    def stores(rows, index):
        return (
            copy(grad_middle.at[rows], grad_middle_ref.at[rows], store_semaphores.at[1, index]),
            copy(grad_attended.at[:, rows], grad_attended_ref.at[:, rows], store_semaphores.at[2, index]),
        )

    finish_backward(
        upstream, middle, grad_total, norm_ref, matrix(out_weights), grad_middle, grad_attended, stores
    )
    put_out.wait()

    @pl.when(spot_ref[0] != 0)
    def _():
        get_hidden.wait()
        put_hidden.start()

    put_sent.wait()


def turn_block(spot, normed, middle, upstream, hidden, norms, attention, up, down):
    length = normed.shape[0]
    return pl.pallas_call(
        functools.partial(turn_kernel, (attention[1], up[1], down[1])),
        in_specs=[SCALARS, IN_VMEM] + [ANY] * 7,
        out_specs=[ANY] * 4,
        scratch_shapes=[
            whole_scratch(BF16),
            whole_scratch(F32),
            whole_scratch(BF16),
            whole_scratch(F32),
            whole_scratch(F32),
            pltpu.VMEM((2, TILE, D), F32),
            pltpu.VMEM((2, TILE, D), F32),
            whole_scratch(BF16),
            whole_scratch(BF16),
            pltpu.VMEM((PAIRS, D, PAIR_DIM), BF16),
            across_scratch(BLOCKS),
            down_scratch(),
            pltpu.VMEM((SHARDS, SHARD_ROWS, D), BF16),
            pltpu.SemaphoreType.DMA((2, BLOCKS)),
            pltpu.SemaphoreType.DMA((5,)),
            pltpu.SemaphoreType.DMA((3, D // FINISH)),
        ],
        out_shape=[
            jax.ShapeDtypeStruct((1, length, D), BF16),
            jax.ShapeDtypeStruct((1, length, D), BF16),
            jax.ShapeDtypeStruct((length, D), BF16),
            jax.ShapeDtypeStruct((PAIRS, length, PAIR_DIM), BF16),
        ],
        compiler_params=params(),
        cost_estimate=cost(42),
        name="turn_block",
    )(spot, norms, normed, middle, upstream, hidden, attention[0], up[0], down[0])


def backward_kernel(
    rows_at,
    spot_ref,
    norm_ref,
    slope_ref,
    middle_ref,
    upstream_ref,
    first_ref,
    last_ref,
    received_ref,
    attention,
    up,
    down,
    activations_ref,
    grad_middle_ref,
    grad_attended_ref,
    slope,
    middle,
    upstream,
    grad_total,
    grad_act,
    grad_middle,
    grad_attended,
    up_weights,
    down_weights,
    out_weights,
    semaphores,
    load_semaphores,
    store_semaphores,
    activations,
    output_semaphores,
):
    grad_inner = grad_middle
    section = spot_ref[0]
    loads = feed_forward_loads(up, down, rows_at[1:], up_weights, down_weights, semaphores)
    copy = pltpu.make_async_copy
    get_upstream = copy(upstream_ref.at[0], upstream, load_semaphores.at[BLOCKS])
    get_middle = copy(middle_ref, middle, load_semaphores.at[BLOCKS + 1])
    get_out = load_out(attention, rows_at[0], out_weights, load_semaphores.at[BLOCKS + 2])
    take = copy(received_ref.at[0], activations.at[1 - section], output_semaphores.at[0])
    keep_first = copy(first_ref.at[0], activations.at[section], output_semaphores.at[1])
    keep_last = copy(last_ref.at[0], activations.at[section], output_semaphores.at[1])
    put_activations = copy(activations, activations_ref, output_semaphores.at[2])
    get_slopes = [
        copy(slope_ref.at[:, pl.ds(block * D, D)], slope.at[block], load_semaphores.at[block])
        for block in range(BLOCKS)
    ]
    get_upstream.start()
    loads[0][1].start()
    grad_total[...] = jnp.zeros_like(grad_total)
    get_upstream.wait()
    get_slopes[0].start()
    loads[0][0].start()

    def step(block, carry):
        wait_for(down_weights.at[block], semaphores.at[1, block])
        w_proj = matrix(down_weights, block)
        tiles = row_tiles(D, TILE)
        grad_act[tiles[0]] = dot_nt(upstream[tiles[0]], w_proj)
        wait_for(slope.at[block], load_semaphores.at[block])
        wait_for(up_weights.at[block], semaphores.at[0, block])
        w_fc = matrix(up_weights, block)
        for later in range(1, BLOCKS):

            @pl.when(block == later - 1)
            def _(later=later):
                loads[later][1].start()
                get_slopes[later].start()
                loads[later][0].start()

        @pl.when(block == BLOCKS - 1)
        def _():
            get_middle.start()
            get_out.start()

        @pl.when(block == 1)
        def _():
            take.start()
            pl.when(section == 0)(keep_first.start)
            pl.when(section != 0)(keep_last.start)

        @pl.when(block == 2)
        def _():
            take.wait()
            keep_first.wait()
            put_activations.start()

        for index, rows in enumerate(tiles):
            if index + 1 < len(tiles):
                grad_act[tiles[index + 1]] = dot_nt(upstream[tiles[index + 1]], w_proj)
            for part in chunks(rows):
                grad_inner[part] = (grad_act[part] * slope[block, part].astype(F32)).astype(BF16)
            grad_total[rows] += dot_nt(grad_inner[rows], w_fc)
        return carry

    lax.fori_loop(0, BLOCKS, step, 0)
    get_middle.wait()
    get_out.wait()

    def stores(rows, index):
        return (
            copy(grad_middle.at[rows], grad_middle_ref.at[rows], store_semaphores.at[0, index]),
            copy(grad_attended.at[:, rows], grad_attended_ref.at[:, rows], store_semaphores.at[1, index]),
        )

    finish_backward(
        upstream, middle, grad_total, norm_ref, matrix(out_weights), grad_middle, grad_attended, stores
    )
    put_activations.wait()


def backward_block(spot, upstream, slope, middle, outputs, norms, attention, up, down):
    length = middle.shape[0]
    return pl.pallas_call(
        functools.partial(backward_kernel, (attention[1], up[1], down[1])),
        in_specs=[SCALARS, IN_VMEM] + [ANY] * 9,
        out_specs=[ANY] * 3,
        scratch_shapes=[
            pltpu.VMEM((BLOCKS, D, D), BF16),
            whole_scratch(F32),
            whole_scratch(BF16),
            whole_scratch(F32),
            whole_scratch(F32),
            whole_scratch(BF16),
            pltpu.VMEM((PAIRS, D, PAIR_DIM), BF16),
            across_scratch(BLOCKS),
            down_scratch(),
            pltpu.VMEM((SHARDS, SHARD_ROWS, D), BF16),
            pltpu.SemaphoreType.DMA((2, BLOCKS)),
            pltpu.SemaphoreType.DMA((BLOCKS + 3,)),
            pltpu.SemaphoreType.DMA((2, D // FINISH)),
            pltpu.VMEM((2, D, D), BF16),
            pltpu.SemaphoreType.DMA((3,)),
        ],
        out_shape=[
            jax.ShapeDtypeStruct((2, length, D), BF16),
            jax.ShapeDtypeStruct((length, D), BF16),
            jax.ShapeDtypeStruct((PAIRS, length, PAIR_DIM), BF16),
        ],
        compiler_params=params(),
        cost_estimate=cost(25),
        name="backward_block",
    )(spot, norms, slope, middle, upstream, *outputs, attention[0], up[0], down[0])


UNPROJECT = 256


def unproject_kernel(
    row,
    which,
    spot_ref,
    norm_ref,
    grads_ref,
    hidden_ref,
    grad_middle_ref,
    array,
    *refs,
):
    last = (*refs[:3], *refs[-2:]) if len(refs) > 10 else None
    out_ref, *refs = (refs[3:5], *refs[5:-2]) if last else refs
    unproject_body(
        row, which, spot_ref, norm_ref, grads_ref, hidden_ref, grad_middle_ref, array, last, out_ref, *refs
    )


def unproject_body(
    row,
    which,
    spot_ref,
    norm_ref,
    grads_ref,
    hidden_ref,
    grad_middle_ref,
    array,
    last,
    out_ref,
    grads,
    hidden,
    grad_middle,
    out,
    total,
    weights,
    semaphores,
    load_semaphores,
    store_semaphores,
):
    copy = pltpu.make_async_copy
    tiles = row_tiles(D, UNPROJECT)
    if last:
        kept_ref, received_ref, outputs_ref, rows_of_two, last_semaphores = last
        get_others = [
            copy(received_ref.at[0], rows_of_two.at[0], last_semaphores.at[0]),
            copy(kept_ref.at[0], rows_of_two.at[1], last_semaphores.at[1]),
        ]
        put_others = copy(rows_of_two, outputs_ref, last_semaphores.at[2])

    get_weights = [load_qkv(array, row, part, weights, semaphores) for part in range(3)]
    get_grads = [
        copy(grads_ref.at[part], grads.at[part], load_semaphores.at[0, part]) for part in range(3)
    ]
    get_hidden = copy(hidden_ref.at[spot_ref[which]], hidden, load_semaphores.at[1, 0])
    get_grad_middle = copy(grad_middle_ref, grad_middle, load_semaphores.at[1, 1])

    def start_part(part):
        get_weights[part].start()
        get_grads[part].start()

    start_part(0)
    stores = []
    gain = norm_ref[0:1]

    def finish(index, rows):
        for part in chunks(rows):
            back = norm_back(hidden[part].astype(F32), gain, total[part])
            out[part] = (grad_middle[part].astype(F32) + back).astype(BF16)
        if last:
            piece, start = divmod(rows.start, D // 2)
            target = out_ref[piece].at[0, start : start + UNPROJECT]
        else:
            target = out_ref.at[0, rows]
        stores.append(copy(out.at[rows], target, store_semaphores.at[index]))
        if last:
            pl.when(spot_ref[0] != 0)(stores[-1].start)
            straight = copy(out.at[rows], outputs_ref.at[0, rows], store_semaphores.at[index])
            pl.when(spot_ref[0] == 0)(straight.start)
        else:
            stores[-1].start()

    for part in range(3):
        get_weights[part].wait()
        get_grads[part].wait()
        if part < 2:
            start_part(part + 1)
        if part == 1:
            get_hidden.start()
            get_grad_middle.start()
        if part == 2:
            get_hidden.wait()
            get_grad_middle.wait()
        if part == 2 and last:

            @pl.when(spot_ref[0] != 0)
            def _():
                for other in get_others:
                    other.start()

        for index, rows in enumerate(tiles):
            term = dot_nt(get_pairs(grads, rows, part), matrix(weights, part))
            total[rows] = term if part == 0 else total[rows] + term
            if part == 2 and index:
                finish(index - 1, tiles[index - 1])
            if part == 2 and last and index == len(tiles) - 1:

                @pl.when(spot_ref[0] != 0)
                def _():
                    for other in get_others:
                        other.wait()
                    put_others.start()

    finish(len(tiles) - 1, tiles[-1])
    for store in stores:
        store.wait()
    if last:
        pl.when(spot_ref[0] != 0)(put_others.wait)


def unproject(spot, which, grads, hidden, grad_middle, norms, place, others=()):
    length = hidden.shape[1]
    count = D // UNPROJECT
    row = jax.ShapeDtypeStruct((1, length, D), BF16)
    piece = jax.ShapeDtypeStruct((1, length // 2, D), BF16)
    return pl.pallas_call(
        functools.partial(unproject_kernel, place[1], which),
        in_specs=[SCALARS, IN_VMEM] + [ANY] * (4 + len(others)),
        out_specs=[ANY] * 3 if others else ANY,
        scratch_shapes=[
            pltpu.VMEM((3, PAIRS, D, PAIR_DIM), BF16),
            whole_scratch(BF16),
            whole_scratch(BF16),
            whole_scratch(BF16),
            whole_scratch(F32),
            across_scratch(3),
            pltpu.SemaphoreType.DMA((3,)),
            pltpu.SemaphoreType.DMA((2, 3)),
            pltpu.SemaphoreType.DMA((count,)),
        ]
        + ([pltpu.VMEM((2, D, D), BF16), pltpu.SemaphoreType.DMA((3,))] if others else []),
        out_shape=[jax.ShapeDtypeStruct((2, length, D), BF16), piece, piece] if others else row,
        compiler_params=params(),
        cost_estimate=cost(11),
        name="unproject",
    )(spot, norms, grads, hidden, grad_middle, place[0], *others)


def three_terms(values):
    high = values.astype(BF16)
    rest = values - high.astype(F32)
    middle = rest.astype(BF16)
    return high, middle, (rest - middle.astype(F32)).astype(BF16)


def exact_nt(values, right):
    count = values.shape[0]
    product = dot_nt(jnp.concatenate(three_terms(values), axis=0), right)
    return (product[2 * count :] + product[count : 2 * count]) + product[:count]


def exact_tn(left, right):
    high, middle, low = three_terms(left)
    first, second, third = three_terms(right)
    return dot_tn(
        jnp.concatenate([low, middle, high, middle, high, high], axis=0),
        jnp.concatenate([first, second, third, first, second, first], axis=0),
    )


def joined(ref):
    return jnp.concatenate(
        [
            ref[pair, part * PREFIX : (part + 1) * PREFIX]
            for part in range(2)
            for pair in range(PAIRS)
        ],
        axis=1,
    )


def hidden_kernel(total_ref, w2_ref, out_ref, total):
    total[...] = jnp.zeros_like(total)
    total[:PREFIX] = joined(total_ref)
    out_ref[...] = exact_nt(total[...], w2_ref[0])


def hidden_back(total, w2):
    return pl.pallas_call(
        hidden_kernel,
        in_specs=[IN_VMEM] * 2,
        out_specs=IN_VMEM,
        scratch_shapes=[pltpu.VMEM((SLOTS, 2 * D), F32)],
        out_shape=jax.ShapeDtypeStruct((SLOTS, w2.shape[1]), F32),
        compiler_params=params(16),
        cost_estimate=cost(2),
        name="hidden_back",
    )(total, w2)


def slots(ref, scratch):
    scratch[...] = jnp.zeros_like(scratch)
    scratch[:PREFIX] = ref[...].astype(F32)
    return scratch[...]


def second_kernel(total_ref, hidden_ref, w2_out, b2_out, total, hidden):
    total[...] = jnp.zeros_like(total)
    total[:PREFIX] = joined(total_ref)
    units = slots(hidden_ref, hidden)
    for columns in row_tiles(2 * D, 512):
        w2_out[0, :, columns] = exact_tn(units, total[:, columns])
    b2_out[...] = jnp.sum(total[...], axis=0, keepdims=True)


def second_back(total, hidden):
    rh = hidden.shape[1]
    return pl.pallas_call(
        second_kernel,
        in_specs=[IN_VMEM] * 2,
        out_specs=[IN_VMEM] * 2,
        scratch_shapes=[pltpu.VMEM((SLOTS, 2 * D), F32), pltpu.VMEM((SLOTS, rh), F32)],
        out_shape=[
            jax.ShapeDtypeStruct((1, rh, 2 * D), F32),
            jax.ShapeDtypeStruct((1, 2 * D), F32),
        ],
        compiler_params=params(16),
        cost_estimate=cost(3),
        name="second_back",
    )(total, hidden)


def last_kernel(
    spot_ref,
    own_ref,
    other_ref,
    hidden_ref,
    table_ref,
    w1_ref,
    outputs_in,
    top_ref,
    bottom_ref,
    table_out,
    w1_out,
    b1_out,
    outputs_ref,
    hidden,
    table,
    buffer,
    semaphores,
):
    del outputs_in
    half = D // 2
    pieces = [(top_ref, slice(0, half)), (bottom_ref, slice(half, D))]
    loads = [
        pltpu.make_async_copy(piece.at[0], buffer.at[rows], semaphores.at[0, index])
        for index, (piece, rows) in enumerate(pieces)
    ]
    stores = [
        pltpu.make_async_copy(buffer.at[rows], outputs_ref.at[1, rows], semaphores.at[1, index])
        for index, (_, rows) in enumerate(pieces)
    ]

    @pl.when(spot_ref[0] == 0)
    def _():
        for load in loads:
            load.start()

    units = slots(hidden_ref, hidden)
    grad_pre = (own_ref[...] + other_ref[...]) * (1.0 - units * units)
    b1_out[...] = jnp.sum(grad_pre, axis=0, keepdims=True)
    table_out[...] = exact_nt(grad_pre, w1_ref[...])[:PREFIX]

    @pl.when(spot_ref[0] == 0)
    def _():
        for load, store in zip(loads, stores):
            load.wait()
            store.start()

    w1_out[...] = exact_tn(slots(table_ref, table), grad_pre)

    @pl.when(spot_ref[0] == 0)
    def _():
        for store in stores:
            store.wait()


def last_block(spot, own, other, hidden, table, w1, outputs, pieces):
    rh = w1.shape[1]
    return pl.pallas_call(
        last_kernel,
        in_specs=[SCALARS] + [IN_VMEM] * 5 + [ANY] * 3,
        out_specs=[IN_VMEM] * 3 + [ANY],
        scratch_shapes=[
            pltpu.VMEM((SLOTS, rh), F32),
            pltpu.VMEM((SLOTS, D), F32),
            whole_scratch(BF16),
            pltpu.SemaphoreType.DMA((2, 2)),
        ],
        out_shape=[
            jax.ShapeDtypeStruct((PREFIX, D), F32),
            jax.ShapeDtypeStruct(w1.shape, F32),
            jax.ShapeDtypeStruct((1, rh), F32),
            jax.ShapeDtypeStruct(outputs.shape, outputs.dtype),
        ],
        input_output_aliases={6: 3},
        compiler_params=params(16),
        cost_estimate=cost(3),
        name="last_block",
    )(spot, own, other, hidden, table, w1, outputs, *pieces)


def swap_sections(values):
    return lax.ppermute(values, "section", [(0, 1), (1, 0)])


def per_section(section_index, own):
    other = swap_sections(own)
    is_first = section_index == 0
    return jnp.where(is_first, own, other), jnp.where(is_first, other, own)


def halves(w_qkv, w_out, w_fc, w_proj):
    columns = lambda matrix: jnp.moveaxis(matrix.reshape(SHARD_ROWS, -1, D), 1, 0)
    attention = jnp.concatenate([columns(w_qkv), w_out[None]], axis=0).reshape(2, HALF, D)
    up = columns(w_fc).reshape(2, HALF, D)
    down = w_proj.reshape(2, HALF, D)
    return jnp.stack([attention, up, down], axis=1)


def gather_weights(is_first, w_qkv, w_out, w_fc, w_proj):
    if D // w_qkv.shape[1] == SHARDS:
        own = halves(w_qkv[0], w_out[0], w_fc[0], w_proj[0])
        received = swap_sections(jnp.where(is_first, own[1], own[0]))
        first = jnp.where(is_first, own[0], received)
        last = jnp.where(is_first, received, own[1])
        early = jnp.concatenate([first.reshape(3 * HALF, D), last[0]], axis=0)
        gather = lambda rows: lax.all_gather(rows, ("dp", "section"), axis=0).reshape(
            SHARDS, 2, -1, D
        )
        early, late = gather(early), gather(last[1:].reshape(2 * HALF, D))
    else:
        whole = lambda matrix: lax.all_gather(matrix[0], ("dp", "section"), axis=0)
        every = [whole(matrix) for matrix in (w_qkv, w_out, w_fc, w_proj)]
        layers = []
        for layer in range(2):
            mine = [matrix[layer::2] for matrix in every]
            shards = [matrix.reshape(SHARDS, -1, matrix.shape[-1]) for matrix in mine]
            layers.append(jax.vmap(halves)(*shards).reshape(SHARDS, 2, 3 * HALF, D))
        early = jnp.concatenate([layers[0], layers[1][:, :, :HALF]], axis=2)
        late = layers[1][:, :, HALF:]
    return (
        [(early, 0), (early, HALF), (early, 2 * HALF)],
        [(early, 3 * HALF), (late, 0), (late, HALF)],
    )


def reparam_hidden(table, w_first, b_first):
    return jnp.tanh(jnp.dot(table, w_first, precision=highest_mode) + b_first)


def reparam_out(hidden_units, w_second, b_second):
    return jnp.dot(hidden_units, w_second, precision=highest_mode) + b_second


def sum_dp(values):
    count = lax.axis_size("dp")
    moved = lambda bits: lax.ppermute(values, "dp", [(i, i ^ bits) for i in range(count)])
    step = count
    while step > 1:
        if step % 4 == 0:
            step //= 4
            values = (values + moved(step)) + (moved(2 * step) + moved(3 * step))
        else:
            step //= 2
            values = values + moved(step)
    return values


def per_device(
    tokens,
    seq_length,
    cotangent,
    ln_gain,
    ln_bias,
    w_qkv,
    w_out,
    w_fc,
    w_proj,
    prefix_table,
    reparam_w1,
    reparam_b1,
    reparam_w2,
    reparam_b2,
):
    section_index = lax.axis_index("section")
    is_first = section_index == 0
    first, last = gather_weights(is_first, w_qkv, w_out, w_fc, w_proj)
    spot = jnp.stack([section_index, jnp.zeros_like(section_index)]).astype(jnp.int32)
    seq = lax.dynamic_slice_in_dim(seq_length, section_index, 1, 0)

    table_values = prefix_table.astype(F32)
    first_weight = reparam_w1.astype(F32)
    first_bias = reparam_b1.astype(F32)
    second_weight = reparam_w2[0].astype(F32)
    second_bias = reparam_b2[0].astype(F32)
    hidden_units = reparam_hidden(table_values, first_weight, first_bias)
    prefix_kv = reparam_out(hidden_units, second_weight, second_bias).astype(BF16)
    pad = ((0, SLOTS - PREFIX), (0, 0))
    small = jnp.concatenate(
        [
            jnp.pad(prefix_kv[:, :D], pad),
            jnp.pad(prefix_kv[:, D:], pad),
            ln_gain[0],
            ln_bias[0],
            jnp.zeros((4, D), BF16),
        ],
        axis=0,
    )
    small_pair = per_section(section_index, small)
    pairs_apart = lambda rows: jnp.moveaxis(rows.reshape(SLOTS, PAIRS, PAIR_DIM), 1, 0)
    prefix_pair = [
        (pairs_apart(part[:SLOTS]), pairs_apart(part[SLOTS : 2 * SLOTS])) for part in small_pair
    ]
    norm_pair = [part[2 * SLOTS :].astype(F32) for part in small_pair]

    prefix_first, prefix_last = prefix_pair
    projected_first = project(spot, 0, tokens, norm_pair[0], first[0])
    attended_first, *probs_first = attend(seq, projected_first, *prefix_first)
    middle_first, normed = middle_block(spot, 0, attended_first, tokens, norm_pair[0], first[0])
    slope, handed = forward_block(normed, middle_first, *first[1:])
    projected = project(spot, 1, handed, norm_pair[1], last[0])
    attended, *probs = attend(seq, projected, *prefix_last)
    middle, normed = middle_block(spot, 1, attended, handed, norm_pair[1], last[0])
    final, sent, grad_middle, grad_attended = turn_block(
        spot, normed, middle, cotangent, handed, norm_pair[1], *last
    )
    received = swap_sections(sent)
    grads, prefix_grad_last = attend_back(
        seq, projected, attended, grad_attended, *prefix_last, *probs
    )
    grad_handed = unproject(spot, 1, grads, handed, grad_middle, norm_pair[1], last[0])
    received_grad = lax.ppermute(grad_handed, "section", [(0, 1)])
    activations, grad_middle, grad_attended = backward_block(
        spot, grad_handed, slope, middle_first, (handed, final, received), norm_pair[0], *first
    )
    grads, prefix_grad_first = attend_back(
        seq,
        projected_first,
        attended_first,
        grad_attended,
        *prefix_first,
        *probs_first,
    )
    input_grads, *pieces = unproject(
        spot,
        0,
        grads,
        tokens,
        grad_middle,
        norm_pair[0],
        first[0],
        (grad_handed, received_grad),
    )
    pieces = [lax.ppermute(piece, "section", [(1, 0)]) for piece in pieces]

    kept = jnp.where(is_first, prefix_grad_first, prefix_grad_last)
    sent = jnp.where(is_first, prefix_grad_last, prefix_grad_first)
    total = sum_dp(kept + swap_sections(sent))
    grad_hidden = hidden_back(total, reparam_w2)
    grad_w2, grad_b2 = second_back(total, hidden_units)
    grad_table, grad_w1, grad_b1, input_grads = last_block(
        spot,
        grad_hidden,
        swap_sections(grad_hidden),
        hidden_units,
        prefix_table,
        reparam_w1,
        input_grads,
        pieces,
    )
    return (
        activations[None],
        input_grads[None],
        grad_table,
        grad_w1,
        grad_b1[0],
        grad_w2,
        grad_b2,
    )


def solution(mesh):
    in_specs = (
        P("dp", None, None),
        P("dp"),
        P("dp", None, None),
        P("section", None, None),
        P("section", None, None),
        P("section", "dp", None),
        P("section", "dp", None),
        P("section", "dp", None),
        P("section", "dp", None),
        P(),
        P(),
        P(),
        P("section", None, None),
        P("section", None),
    )
    out_specs = (
        P("section", "dp", None, None),
        P("section", "dp", None, None),
        P(),
        P(),
        P(),
        P("section", None, None),
        P("section", None),
    )
    return jax.shard_map(
        per_device, mesh=mesh, in_specs=in_specs, out_specs=out_specs, check_vma=False
    )
```

```python
import functools

import jax
import jax.numpy as jnp
from jax import lax
from jax.experimental import pallas as pl
from jax.experimental.pallas import tpu as pltpu
from jax.sharding import PartitionSpec as P

D = 1024
HEADS = 16
HEAD_DIM = 64
FF = 4096
PREFIX = 10
SLOTS = 16
BOTH = 24
PAIRS = 8
PAIR_DIM = 128
BLOCK = 256

eps_norm = 1e-05
neg_big = -1e30
highest_mode = lax.Precision.HIGHEST
F32 = jnp.float32
BF16 = jnp.bfloat16


def dot(left, right, dims):
    return lax.dot_general(left, right, (dims, ((), ())), preferred_element_type=F32)


def dot_nn(left, right):
    return dot(left, right, ((1,), (0,)))


def dot_nt(left, right):
    return dot(left, right, ((1,), (1,)))


def dot_tn(left, right):
    return dot(left, right, ((0,), (0,)))


def normalised(values):
    centre = jnp.mean(values, axis=-1, keepdims=True)
    spread = values - centre
    variance = jnp.mean(spread * spread, axis=-1, keepdims=True)
    inverse = lax.rsqrt(variance + eps_norm)
    return spread * inverse, inverse


def layer_norm(values, gain, offset):
    return normalised(values)[0] * gain + offset


def norm_back(values, gain, upstream):
    unit, inverse = normalised(values)
    scaled = upstream * gain
    mean_scaled = jnp.mean(scaled, axis=-1, keepdims=True)
    mean_unit = jnp.mean(scaled * unit, axis=-1, keepdims=True)
    return (scaled - mean_scaled - unit * mean_unit) * inverse


SQRT_2_PI = 0.7978845608028654
CUBIC = 0.044715


def gelu_pair(values):
    cubic_part = (SQRT_2_PI * CUBIC) * (values * values)
    half_tanh = 0.5 + 0.5 * jnp.tanh(values * (SQRT_2_PI + cubic_part))
    out = values * half_tanh
    slope = half_tanh + out * ((2.0 - 2.0 * half_tanh) * (SQRT_2_PI + 3.0 * cubic_part))
    return out, slope


def params(mebibytes=62):
    return pltpu.CompilerParams(vmem_limit_bytes=mebibytes * 2**20)


def cost(micros):
    return pl.CostEstimate(flops=int(micros * 1.15e9), bytes_accessed=2**20, transcendentals=0)


SHARDS = 16
HALF = 128
SHARD_ROWS = 64
BLOCKS = FF // D


def load_across(array, half, row, target, semaphore):
    return pltpu.make_async_copy(array.at[:, half, pl.ds(row, SHARD_ROWS)], target, semaphore)


def load_qkv(array, row, part, weights, semaphores):
    half, inner = divmod(part, 2)
    return load_across(
        array, half, row + inner * SHARD_ROWS, weights.at[part], semaphores.at[part]
    )


def load_out(array, row, target, semaphore):
    return load_across(array, 1, row + SHARD_ROWS, target, semaphore)


def load_up(array, row, block, target, semaphore):
    half, inner = divmod(block, 2)
    return load_across(array, half, row + inner * SHARD_ROWS, target, semaphore)


def load_down(array, row, block, target, semaphore):
    few = SHARDS // BLOCKS
    return pltpu.make_async_copy(
        array.at[pl.ds(block * few, few), :, pl.ds(row, HALF)], target, semaphore
    )


def across_scratch(count):
    return pltpu.VMEM((count, SHARDS, SHARD_ROWS, D), BF16)


def down_scratch():
    return pltpu.VMEM((BLOCKS, SHARDS // BLOCKS, 2, HALF, D), BF16)


def matrix(ref, *index):
    return ref[index].reshape(D, D) if index else ref[...].reshape(D, D)


ANY = pl.BlockSpec(memory_space=pl.ANY)
TILE = 512
SCALARS = pl.BlockSpec(memory_space=pltpu.SMEM)
IN_VMEM = pl.BlockSpec(memory_space=pltpu.VMEM)


def whole_scratch(dtype):
    return pltpu.VMEM((D, D), dtype)


def once(shape, index):
    return pl.BlockSpec(shape, index, pipeline_mode=pl.Buffered(1))


def row_tiles(length, size):
    return [slice(start, start + size) for start in range(0, length, size)]


CHUNK = 16


def put_pairs(ref, rows, values):
    for pair in range(PAIRS):
        ref[pair, rows] = values[:, pair * PAIR_DIM : (pair + 1) * PAIR_DIM]


def get_pairs(ref, rows, *lead):
    return jnp.concatenate([ref[(*lead, pair, rows)] for pair in range(PAIRS)], axis=1)


def chunks(rows, size=CHUNK):
    return [slice(start, start + size) for start in range(rows.start, rows.stop, size)]


def shifted(rows, by):
    return slice(rows.start + by, rows.stop + by)


def qkv_kernel(row, spot_ref, hidden_ref, norm_ref, array, out_ref, normed, weights, semaphores):
    step = pl.program_id(0)
    loads = [load_qkv(array, row, part, weights, semaphores) for part in range(3)]
    length = hidden_ref.shape[1]
    tiles = row_tiles(length, 256)

    @pl.when(step == 0)
    def _():
        loads[0].start()
        gain, offset = norm_ref[0:1], norm_ref[2:3]

        def norm(tile):
            for rows in chunks(tile):
                values = hidden_ref[0, rows].astype(F32)
                normed[rows] = layer_norm(values, gain, offset).astype(BF16)

        norm(tiles[0])
        loads[0].wait()
        loads[1].start()
        loads[2].start()
        for index, rows in enumerate(tiles):
            if index + 1 < len(tiles):
                norm(tiles[index + 1])
            queries = dot_nn(normed[rows], matrix(weights, 0))
            put_pairs(out_ref, rows, (queries * HEAD_DIM**-0.5).astype(BF16))

    for part in (1, 2):

        @pl.when(step == part)
        def _(part=part):
            loads[part].wait()
            for rows in tiles:
                put_pairs(out_ref, rows, dot_nn(normed[rows], matrix(weights, part)).astype(BF16))


def project(spot, which, hidden, norms, place):
    length = hidden.shape[1]
    return pl.pallas_call(
        functools.partial(qkv_kernel, place[1]),
        grid_spec=pltpu.PrefetchScalarGridSpec(
            num_scalar_prefetch=1,
            grid=(3,),
            in_specs=[
                once((1, length, D), lambda j, s: (s[which], 0, 0)),
                once((8, D), lambda j, s: (0, 0)),
                ANY,
            ],
            out_specs=pl.BlockSpec((PAIRS, length, PAIR_DIM), lambda j, s: (j, 0, 0)),
            scratch_shapes=[
                pltpu.VMEM((length, D), BF16),
                across_scratch(3),
                pltpu.SemaphoreType.DMA((3,)),
            ],
        ),
        out_shape=jax.ShapeDtypeStruct((3 * PAIRS, length, PAIR_DIM), BF16),
        compiler_params=params(),
        cost_estimate=cost(12),
        name="norm_project",
    )(spot, hidden, norms, place[0])


def lane_halves(block):
    lanes = lax.broadcasted_iota(jnp.int32, block.shape, 1)
    zero = jnp.zeros_like(block)
    return jnp.where(lanes < HEAD_DIM, block, zero), jnp.where(lanes < HEAD_DIM, zero, block)


def key_spans(first, stop):
    if first == 0:
        return [slice(0, SLOTS + stop)]
    return [slice(0, SLOTS), slice(SLOTS + first, SLOTS + stop)]


def read_spans(ref, spans, *rest):
    parts = [ref[(span, *rest)] for span in spans]
    return parts[0] if len(parts) == 1 else jnp.concatenate(parts, axis=0)


def cut_spans(values, spans):
    start = 0
    for span in spans:
        size = span.stop - span.start
        yield span, values[start : start + size]
        start += size


def strips(length, short):
    return [
        (rows, slice(2 * rows.start, 2 * rows.stop), rows.start if short else 0)
        for rows in row_tiles(length, BLOCK)
    ]


def stacked_halves(block):
    return jnp.concatenate(lane_halves(block), axis=0)


def own_heads(product):
    return jnp.concatenate([product[:HEAD_DIM, :BLOCK], product[HEAD_DIM:, BLOCK:]], axis=0)


def either_length(length_ref, length, run):
    short = length_ref[0] < length
    pl.when(short)(lambda: run(True))
    pl.when(jnp.logical_not(short))(lambda: run(False))


def allowed(rows, first_diagonal):
    shape = (rows.stop - rows.start, 2 * BLOCK)
    keys = lax.broadcasted_iota(jnp.int32, shape, 0) + rows.start
    if rows.stop <= SLOTS:
        return keys < PREFIX
    queries = lax.broadcasted_iota(jnp.int32, shape, 1) % BLOCK
    return keys - first_diagonal <= queries


def eight_rows(values, reduce):
    return reduce(values.reshape(-1, 8, values.shape[-1]), axis=0)


def attend_kernel(
    seq_ref, q_ref, k_ref, v_ref, kp_ref, vp_ref, out_ref, probs_ref, scale_ref, keys, values_t, scores
):
    length = q_ref.shape[1]
    keys[:SLOTS], keys[SLOTS:] = kp_ref[0], k_ref[0]
    values_t[...] = v_ref[0].T
    prefix_values = vp_ref[0]

    def run(short):
        def scored(strip, slot):
            rows, _, first = strip
            count = SLOTS + rows.stop - first
            scores[slot, :count] = dot_nt(
                read_spans(keys, key_spans(first, rows.stop)), stacked_halves(q_ref[0, rows])
            )

        todo = strips(length, short)
        scored(todo[0], 0)
        for index, (rows, columns, first) in enumerate(todo):
            slot = index % 2
            if index + 1 < len(todo):
                scored(todo[index + 1], 1 - slot)
            count = SLOTS + rows.stop - first
            parts = chunks(slice(0, count))
            top = None
            for part in parts:
                values = scores[slot, part]
                if part.stop <= SLOTS or part.start >= count - BLOCK:
                    values = jnp.where(allowed(part, count - BLOCK), values, neg_big)
                    scores[slot, part] = values
                values = eight_rows(values, jnp.max)
                top = values if top is None else jnp.maximum(top, values)
            top = jnp.max(top, axis=0, keepdims=True)
            total = None
            for part in parts:
                values = jnp.exp(scores[slot, part] - top)
                place = part if part.stop <= SLOTS else shifted(part, first)
                probs_ref[0, place, columns] = values.astype(BF16)
                values = eight_rows(values, jnp.sum)
                total = values if total is None else total + values
            inverse = 1.0 / jnp.sum(total, axis=0, keepdims=True)
            both = dot_nn(
                values_t[:, first : rows.stop],
                probs_ref[0, SLOTS + first : SLOTS + rows.stop, columns],
            ) + dot_tn(prefix_values, probs_ref[0, :SLOTS, columns])
            inverse = jnp.concatenate(
                [
                    jnp.broadcast_to(inverse[:, :BLOCK], (HEAD_DIM, BLOCK)),
                    jnp.broadcast_to(inverse[:, BLOCK:], (HEAD_DIM, BLOCK)),
                ],
                axis=0,
            )
            out_ref[0, rows] = (own_heads(both) * inverse).T.astype(BF16)
            scale_ref[0, rows] = inverse.T

    either_length(seq_ref, length, run)


def pair_spec(length, part):
    return pl.BlockSpec((1, length, PAIR_DIM), lambda p, s: (part * PAIRS + p, 0, 0))


def probs_spec(length):
    return pl.BlockSpec((1, SLOTS + length, 2 * length), lambda p, s: (p, 0, 0))


def attend(seq, projected, prefix_keys, prefix_values):
    length = projected.shape[1]
    return pl.pallas_call(
        attend_kernel,
        grid_spec=pltpu.PrefetchScalarGridSpec(
            num_scalar_prefetch=1,
            grid=(PAIRS,),
            in_specs=[
                pair_spec(length, 0),
                pair_spec(length, 1),
                pair_spec(length, 2),
                pair_spec(SLOTS, 0),
                pair_spec(SLOTS, 0),
            ],
            out_specs=[pair_spec(length, 0), probs_spec(length), pair_spec(length, 0)],
            scratch_shapes=[
                pltpu.VMEM((SLOTS + length, PAIR_DIM), BF16),
                pltpu.VMEM((PAIR_DIM, length), BF16),
                pltpu.VMEM((2, SLOTS + length, 2 * BLOCK), F32),
            ],
        ),
        out_shape=[
            jax.ShapeDtypeStruct((PAIRS, length, PAIR_DIM), BF16),
            jax.ShapeDtypeStruct((PAIRS, SLOTS + length, 2 * length), BF16),
            jax.ShapeDtypeStruct((PAIRS, length, PAIR_DIM), F32),
        ],
        compiler_params=params(),
        cost_estimate=cost(30),
        name="attend",
    )(seq, projected, projected, projected, prefix_keys, prefix_values)


def attend_back_kernel(
    seq_ref,
    q_ref,
    k_ref,
    v_ref,
    out_ref,
    grad_ref,
    kp_ref,
    vp_ref,
    probs_ref,
    scale_ref,
    grads_ref,
    prefix_ref,
    values,
    keys_t,
    dk,
    dv,
    dprobs,
    ds,
):
    length = q_ref.shape[1]
    values[:SLOTS], values[SLOTS:] = vp_ref[0], v_ref[0]
    keys_t[...] = k_ref[0].T
    prefix_keys = kp_ref[0]
    dk[...] = jnp.zeros_like(dk)
    dv[...] = jnp.zeros_like(dv)

    def run(short):
        def prepared(strip, slot):
            rows, _, first = strip
            grads = (grad_ref[0, rows].astype(F32) * scale_ref[0, rows]).astype(BF16)
            halves = stacked_halves(grads)
            weighted_t = (grads.astype(F32) * out_ref[0, rows].astype(F32)).T
            centre = jnp.concatenate(
                [
                    jnp.sum(weighted_t[:HEAD_DIM], axis=0, keepdims=True),
                    jnp.sum(weighted_t[HEAD_DIM:], axis=0, keepdims=True),
                ],
                axis=1,
            )
            dprobs[slot, : SLOTS + rows.stop - first] = dot_nt(
                read_spans(values, key_spans(first, rows.stop)), halves
            )
            return halves, centre

        todo = strips(length, short)
        ahead = prepared(todo[0], 0)
        for index, (rows, columns, first) in enumerate(todo):
            slot = index % 2
            spans = key_spans(first, rows.stop)
            grad_halves, centre = ahead
            if index + 1 < len(todo):
                ahead = prepared(todo[index + 1], 1 - slot)
            count = SLOTS + rows.stop - first
            for part in chunks(slice(0, count)):
                place = part if part.stop <= SLOTS else shifted(part, first)
                probs = probs_ref[0, place, columns].astype(F32)
                ds[slot, part] = (probs * (dprobs[slot, part] - centre)).astype(BF16)
            for total, left, right in (
                (dv, read_spans(probs_ref.at[0], spans, columns), grad_halves),
                (dk, ds[slot, :count], stacked_halves(q_ref[0, rows])),
            ):
                for span, part in cut_spans(dot_nn(left, right), spans):
                    total[span] += part
            both = dot_nn(keys_t[:, first : rows.stop], ds[slot, SLOTS:count]) + dot_tn(
                prefix_keys, ds[slot, :SLOTS]
            )
            grads_ref[0, 0, rows] = (own_heads(both).T * HEAD_DIM**-0.5).astype(BF16)

    either_length(seq_ref, length, run)
    grads_ref[1, 0] = dk[SLOTS:].astype(BF16)
    grads_ref[2, 0] = dv[SLOTS:].astype(BF16)
    prefix_ref[0, :PREFIX] = dk[:PREFIX]
    prefix_ref[0, PREFIX : 2 * PREFIX] = dv[:PREFIX]
    prefix_ref[0, 2 * PREFIX :] = jnp.zeros_like(prefix_ref[0, 2 * PREFIX :])


def attend_back(seq, projected, attended, grad_attended, prefix_keys, prefix_values, probs, scale):
    length = projected.shape[1]
    ext = (SLOTS + length, PAIR_DIM)
    return pl.pallas_call(
        attend_back_kernel,
        grid_spec=pltpu.PrefetchScalarGridSpec(
            num_scalar_prefetch=1,
            grid=(PAIRS,),
            in_specs=[
                pair_spec(length, 0),
                pair_spec(length, 1),
                pair_spec(length, 2),
                pair_spec(length, 0),
                pair_spec(length, 0),
                pair_spec(SLOTS, 0),
                pair_spec(SLOTS, 0),
                probs_spec(length),
                pair_spec(length, 0),
            ],
            out_specs=[
                pl.BlockSpec((3, 1, length, PAIR_DIM), lambda p, s: (0, p, 0, 0)),
                pair_spec(BOTH, 0),
            ],
            scratch_shapes=[
                pltpu.VMEM(ext, BF16),
                pltpu.VMEM((PAIR_DIM, length), BF16),
                pltpu.VMEM(ext, F32),
                pltpu.VMEM(ext, F32),
                pltpu.VMEM((2, SLOTS + length, 2 * BLOCK), F32),
                pltpu.VMEM((2, SLOTS + length, 2 * BLOCK), BF16),
            ],
        ),
        out_shape=[
            jax.ShapeDtypeStruct((3, PAIRS, length, PAIR_DIM), BF16),
            jax.ShapeDtypeStruct((PAIRS, BOTH, PAIR_DIM), F32),
        ],
        compiler_params=params(),
        cost_estimate=cost(30),
        name="attend_back",
    )(
        seq,
        projected,
        projected,
        projected,
        attended,
        grad_attended,
        prefix_keys,
        prefix_values,
        probs,
        scale,
    )


def middle_kernel(
    row,
    which,
    spot_ref,
    norm_ref,
    attended_ref,
    hidden_ref,
    array,
    middle_ref,
    normed_ref,
    attended,
    hidden,
    middle,
    normed,
    weights,
    semaphores,
    load_semaphores,
    store_semaphores,
):
    copy = pltpu.make_async_copy
    tiles = row_tiles(D, 256)
    get_weights = load_out(array, row, weights, semaphores.at[0])
    get_attended = [
        copy(attended_ref.at[:, rows], attended.at[:, rows], load_semaphores.at[0, index])
        for index, rows in enumerate(tiles)
    ]
    get_hidden = [
        copy(hidden_ref.at[spot_ref[which], rows], hidden.at[rows], load_semaphores.at[1, index])
        for index, rows in enumerate(tiles)
    ]
    get_weights.start()
    for loads in zip(get_attended, get_hidden):
        for load in loads:
            load.start()
    gain, offset = norm_ref[1:2], norm_ref[3:4]
    stores = []

    def finish(index, rows):
        get_hidden[index].wait()
        for part in chunks(rows):
            values = hidden[part].astype(F32) + middle[part]
            middle[part] = values
            normed[part] = layer_norm(values, gain, offset).astype(BF16)
        for source, target, kind in ((middle, middle_ref, 0), (normed, normed_ref, 1)):
            stores.append(copy(source.at[rows], target.at[rows], store_semaphores.at[kind, index]))
            stores[-1].start()

    get_weights.wait()
    for index, rows in enumerate(tiles):
        get_attended[index].wait()
        middle[rows] = dot_nn(get_pairs(attended, rows), matrix(weights))
        if index:
            finish(index - 1, tiles[index - 1])
    finish(len(tiles) - 1, tiles[-1])
    for store in stores:
        store.wait()


def middle_block(spot, which, attended, hidden, norms, place):
    length = attended.shape[1]
    count = D // 256
    return pl.pallas_call(
        functools.partial(middle_kernel, place[1], which),
        in_specs=[SCALARS, IN_VMEM] + [ANY] * 3,
        out_specs=[ANY] * 2,
        scratch_shapes=[
            pltpu.VMEM((PAIRS, D, PAIR_DIM), BF16),
            whole_scratch(BF16),
            whole_scratch(F32),
            whole_scratch(BF16),
            pltpu.VMEM((SHARDS, SHARD_ROWS, D), BF16),
            pltpu.SemaphoreType.DMA((1,)),
            pltpu.SemaphoreType.DMA((2, count)),
            pltpu.SemaphoreType.DMA((2, count)),
        ],
        out_shape=[
            jax.ShapeDtypeStruct((length, D), F32),
            jax.ShapeDtypeStruct((length, D), BF16),
        ],
        compiler_params=params(),
        cost_estimate=cost(5),
        name="middle_block",
    )(spot, norms, attended, hidden, place[0])


def feed_forward_loads(up, down, rows, up_weights, down_weights, semaphores):
    return [
        (
            load_up(up, rows[0], block, up_weights.at[block], semaphores.at[0, block]),
            load_down(down, rows[1], block, down_weights.at[block], semaphores.at[1, block]),
        )
        for block in range(BLOCKS)
    ]


def start_all(loads):
    for pair in loads:
        for load in pair:
            load.start()


def wait_step(loads, step):
    for block, pair in enumerate(loads):

        @pl.when(step == block)
        def _(pair=pair):
            for load in pair:
                load.wait()


def wait_for(target, semaphore):
    pltpu.make_async_copy(target, target, semaphore).wait()


def feed_forward_scratch():
    return [across_scratch(BLOCKS), down_scratch(), pltpu.SemaphoreType.DMA((2, BLOCKS))]


def forward_kernel(
    rows_at,
    normed_ref,
    middle_ref,
    up,
    down,
    slope_ref,
    out_ref,
    total,
    inner,
    activated,
    up_weights,
    down_weights,
    semaphores,
):
    step = pl.program_id(0)
    tiles = row_tiles(middle_ref.shape[0], TILE)
    loads = feed_forward_loads(up, down, rows_at, up_weights, down_weights, semaphores)

    @pl.when(step == 0)
    def _():
        start_all(loads[:1])
        total[...] = middle_ref[...]

    wait_step(loads, step)
    for later in range(1, BLOCKS):
        pl.when(step == later - 1)(lambda later=later: start_all(loads[later : later + 1]))
    w_fc, w_proj = matrix(up_weights, step), matrix(down_weights, step)
    inner[tiles[0]] = dot_nn(normed_ref[tiles[0]], w_fc)
    for index, rows in enumerate(tiles):
        if index + 1 < len(tiles):
            inner[tiles[index + 1]] = dot_nn(normed_ref[tiles[index + 1]], w_fc)
        for part in chunks(rows):
            value, slope = gelu_pair(inner[part])
            activated[part] = value.astype(BF16)
            slope_ref[part] = slope.astype(BF16)
        total[rows] += dot_nn(activated[rows], w_proj)

    @pl.when(step == pl.num_programs(0) - 1)
    def _():
        out_ref[0] = total[...].astype(BF16)


def forward_block(normed, middle, up, down):
    length = normed.shape[0]
    whole = lambda j: (0, 0)
    return pl.pallas_call(
        functools.partial(forward_kernel, (up[1], down[1])),
        grid=(BLOCKS,),
        in_specs=[once((length, D), whole), once((length, D), whole), ANY, ANY],
        out_specs=[
            pl.BlockSpec((length, D), lambda j: (0, j)),
            once((1, length, D), lambda j: (0, 0, 0)),
        ],
        scratch_shapes=[whole_scratch(F32), whole_scratch(F32), whole_scratch(BF16)]
        + feed_forward_scratch(),
        out_shape=[
            jax.ShapeDtypeStruct((length, FF), BF16),
            jax.ShapeDtypeStruct((1, length, D), BF16),
        ],
        compiler_params=params(),
        cost_estimate=cost(25),
        name="forward_block",
    )(normed, middle, up[0], down[0])


FINISH = 256


def finish_backward(upstream, middle, grad_total, norm_ref, w_out, grad_middle, grad_attended, stores):
    gain = norm_ref[1:2]
    for index, rows in enumerate(row_tiles(D, FINISH)):
        for part in chunks(rows):
            grad = upstream[part].astype(F32) + norm_back(middle[part], gain, grad_total[part])
            grad_middle[part] = grad.astype(BF16)
        put_pairs(grad_attended, rows, dot_nt(grad_middle[rows], w_out).astype(BF16))
        for store in stores(rows, index):
            store.start()
    for index, rows in enumerate(row_tiles(D, FINISH)):
        for store in stores(rows, index):
            store.wait()


def turn_kernel(
    rows_at,
    spot_ref,
    norm_ref,
    normed_ref,
    middle_ref,
    upstream_ref,
    hidden_ref,
    attention,
    up,
    down,
    out_ref,
    sent_ref,
    grad_middle_ref,
    grad_attended_ref,
    normed,
    middle,
    upstream,
    total,
    grad_total,
    inner,
    grad_act,
    out,
    grad_middle,
    grad_attended,
    up_weights,
    down_weights,
    out_weights,
    semaphores,
    load_semaphores,
    store_semaphores,
):
    activated, grad_inner = grad_middle, out
    loads = feed_forward_loads(up, down, rows_at[1:], up_weights, down_weights, semaphores)
    copy = pltpu.make_async_copy
    get_normed = copy(normed_ref, normed, load_semaphores.at[0])
    get_upstream = copy(upstream_ref.at[spot_ref[0]], upstream, load_semaphores.at[1])
    get_middle = copy(middle_ref, middle, load_semaphores.at[2])
    get_out = load_out(attention, rows_at[0], out_weights, load_semaphores.at[3])
    get_normed.start()
    loads[0][0].start()
    total[...] = jnp.zeros_like(total)
    grad_total[...] = jnp.zeros_like(grad_total)
    get_normed.wait()
    get_upstream.start()
    loads[0][1].start()

    def step(block, carry):
        wait_for(up_weights.at[block], semaphores.at[0, block])
        tiles = row_tiles(D, TILE)
        w_fc = matrix(up_weights, block)
        inner[0] = dot_nn(normed[tiles[0]], w_fc)
        pl.when(block == 0)(get_upstream.wait)
        wait_for(down_weights.at[block], semaphores.at[1, block])
        w_proj = matrix(down_weights, block)
        for later in range(1, BLOCKS):
            pl.when(block == later - 1)(lambda later=later: start_all(loads[later : later + 1]))

        @pl.when(block == BLOCKS - 1)
        def _():
            get_middle.start()
            get_out.start()

        grad_act[0] = dot_nt(upstream[tiles[0]], w_proj)
        for index, rows in enumerate(tiles):
            slot = index % 2
            if index + 1 < len(tiles):
                inner[1 - slot] = dot_nn(normed[tiles[index + 1]], w_fc)
                grad_act[1 - slot] = dot_nt(upstream[tiles[index + 1]], w_proj)
            for part in chunks(rows):
                here = shifted(part, -rows.start)
                value, slope = gelu_pair(inner[slot, here])
                activated[part] = value.astype(BF16)
                grad_inner[part] = (grad_act[slot, here] * slope).astype(BF16)
            total[rows] += dot_nn(activated[rows], w_proj)
            grad_total[rows] += dot_nt(grad_inner[rows], w_fc)
        return carry

    lax.fori_loop(0, BLOCKS, step, 0)
    get_middle.wait()
    for part in chunks(slice(0, D)):
        out[part] = (total[part] + middle[part]).astype(BF16)
    put_out = copy(out, out_ref.at[0], store_semaphores.at[0, 0])
    put_out.start()
    put_sent = copy(out, sent_ref.at[0], store_semaphores.at[0, 1])
    get_hidden = copy(hidden_ref.at[0], normed, load_semaphores.at[4])
    put_hidden = copy(normed, sent_ref.at[0], store_semaphores.at[0, 1])
    pl.when(spot_ref[0] == 0)(put_sent.start)
    pl.when(spot_ref[0] != 0)(get_hidden.start)
    get_out.wait()

    def stores(rows, index):
        return (
            copy(grad_middle.at[rows], grad_middle_ref.at[rows], store_semaphores.at[1, index]),
            copy(grad_attended.at[:, rows], grad_attended_ref.at[:, rows], store_semaphores.at[2, index]),
        )

    finish_backward(
        upstream, middle, grad_total, norm_ref, matrix(out_weights), grad_middle, grad_attended, stores
    )
    put_out.wait()

    @pl.when(spot_ref[0] != 0)
    def _():
        get_hidden.wait()
        put_hidden.start()

    put_sent.wait()


def turn_block(spot, normed, middle, upstream, hidden, norms, attention, up, down):
    length = normed.shape[0]
    return pl.pallas_call(
        functools.partial(turn_kernel, (attention[1], up[1], down[1])),
        in_specs=[SCALARS, IN_VMEM] + [ANY] * 7,
        out_specs=[ANY] * 4,
        scratch_shapes=[
            whole_scratch(BF16),
            whole_scratch(F32),
            whole_scratch(BF16),
            whole_scratch(F32),
            whole_scratch(F32),
            pltpu.VMEM((2, TILE, D), F32),
            pltpu.VMEM((2, TILE, D), F32),
            whole_scratch(BF16),
            whole_scratch(BF16),
            pltpu.VMEM((PAIRS, D, PAIR_DIM), BF16),
            across_scratch(BLOCKS),
            down_scratch(),
            pltpu.VMEM((SHARDS, SHARD_ROWS, D), BF16),
            pltpu.SemaphoreType.DMA((2, BLOCKS)),
            pltpu.SemaphoreType.DMA((5,)),
            pltpu.SemaphoreType.DMA((3, D // FINISH)),
        ],
        out_shape=[
            jax.ShapeDtypeStruct((1, length, D), BF16),
            jax.ShapeDtypeStruct((1, length, D), BF16),
            jax.ShapeDtypeStruct((length, D), BF16),
            jax.ShapeDtypeStruct((PAIRS, length, PAIR_DIM), BF16),
        ],
        compiler_params=params(),
        cost_estimate=cost(42),
        name="turn_block",
    )(spot, norms, normed, middle, upstream, hidden, attention[0], up[0], down[0])


def backward_kernel(
    rows_at,
    spot_ref,
    norm_ref,
    slope_ref,
    middle_ref,
    upstream_ref,
    first_ref,
    last_ref,
    received_ref,
    attention,
    up,
    down,
    activations_ref,
    grad_middle_ref,
    grad_attended_ref,
    slope,
    middle,
    upstream,
    grad_total,
    grad_act,
    grad_middle,
    grad_attended,
    up_weights,
    down_weights,
    out_weights,
    semaphores,
    load_semaphores,
    store_semaphores,
    activations,
    output_semaphores,
):
    grad_inner = grad_middle
    section = spot_ref[0]
    loads = feed_forward_loads(up, down, rows_at[1:], up_weights, down_weights, semaphores)
    copy = pltpu.make_async_copy
    get_upstream = copy(upstream_ref.at[0], upstream, load_semaphores.at[BLOCKS])
    get_middle = copy(middle_ref, middle, load_semaphores.at[BLOCKS + 1])
    get_out = load_out(attention, rows_at[0], out_weights, load_semaphores.at[BLOCKS + 2])
    take = copy(received_ref.at[0], activations.at[1 - section], output_semaphores.at[0])
    keep_first = copy(first_ref.at[0], activations.at[section], output_semaphores.at[1])
    keep_last = copy(last_ref.at[0], activations.at[section], output_semaphores.at[1])
    put_activations = copy(activations, activations_ref, output_semaphores.at[2])
    get_slopes = [
        copy(slope_ref.at[:, pl.ds(block * D, D)], slope.at[block], load_semaphores.at[block])
        for block in range(BLOCKS)
    ]
    get_upstream.start()
    loads[0][1].start()
    grad_total[...] = jnp.zeros_like(grad_total)
    get_upstream.wait()
    get_slopes[0].start()
    loads[0][0].start()

    def step(block, carry):
        wait_for(down_weights.at[block], semaphores.at[1, block])
        w_proj = matrix(down_weights, block)
        tiles = row_tiles(D, TILE)
        grad_act[tiles[0]] = dot_nt(upstream[tiles[0]], w_proj)
        wait_for(slope.at[block], load_semaphores.at[block])
        wait_for(up_weights.at[block], semaphores.at[0, block])
        w_fc = matrix(up_weights, block)
        for later in range(1, BLOCKS):

            @pl.when(block == later - 1)
            def _(later=later):
                loads[later][1].start()
                get_slopes[later].start()
                loads[later][0].start()

        @pl.when(block == BLOCKS - 1)
        def _():
            get_middle.start()
            get_out.start()

        @pl.when(block == 1)
        def _():
            take.start()
            pl.when(section == 0)(keep_first.start)
            pl.when(section != 0)(keep_last.start)

        @pl.when(block == 2)
        def _():
            take.wait()
            keep_first.wait()
            put_activations.start()

        for index, rows in enumerate(tiles):
            if index + 1 < len(tiles):
                grad_act[tiles[index + 1]] = dot_nt(upstream[tiles[index + 1]], w_proj)
            for part in chunks(rows):
                grad_inner[part] = (grad_act[part] * slope[block, part].astype(F32)).astype(BF16)
            grad_total[rows] += dot_nt(grad_inner[rows], w_fc)
        return carry

    lax.fori_loop(0, BLOCKS, step, 0)
    get_middle.wait()
    get_out.wait()

    def stores(rows, index):
        return (
            copy(grad_middle.at[rows], grad_middle_ref.at[rows], store_semaphores.at[0, index]),
            copy(grad_attended.at[:, rows], grad_attended_ref.at[:, rows], store_semaphores.at[1, index]),
        )

    finish_backward(
        upstream, middle, grad_total, norm_ref, matrix(out_weights), grad_middle, grad_attended, stores
    )
    put_activations.wait()


def backward_block(spot, upstream, slope, middle, outputs, norms, attention, up, down):
    length = middle.shape[0]
    return pl.pallas_call(
        functools.partial(backward_kernel, (attention[1], up[1], down[1])),
        in_specs=[SCALARS, IN_VMEM] + [ANY] * 9,
        out_specs=[ANY] * 3,
        scratch_shapes=[
            pltpu.VMEM((BLOCKS, D, D), BF16),
            whole_scratch(F32),
            whole_scratch(BF16),
            whole_scratch(F32),
            whole_scratch(F32),
            whole_scratch(BF16),
            pltpu.VMEM((PAIRS, D, PAIR_DIM), BF16),
            across_scratch(BLOCKS),
            down_scratch(),
            pltpu.VMEM((SHARDS, SHARD_ROWS, D), BF16),
            pltpu.SemaphoreType.DMA((2, BLOCKS)),
            pltpu.SemaphoreType.DMA((BLOCKS + 3,)),
            pltpu.SemaphoreType.DMA((2, D // FINISH)),
            pltpu.VMEM((2, D, D), BF16),
            pltpu.SemaphoreType.DMA((3,)),
        ],
        out_shape=[
            jax.ShapeDtypeStruct((2, length, D), BF16),
            jax.ShapeDtypeStruct((length, D), BF16),
            jax.ShapeDtypeStruct((PAIRS, length, PAIR_DIM), BF16),
        ],
        compiler_params=params(),
        cost_estimate=cost(25),
        name="backward_block",
    )(spot, norms, slope, middle, upstream, *outputs, attention[0], up[0], down[0])


UNPROJECT = 256


def unproject_kernel(
    row,
    which,
    spot_ref,
    norm_ref,
    grads_ref,
    hidden_ref,
    grad_middle_ref,
    array,
    *refs,
):
    last = (*refs[:3], *refs[-2:]) if len(refs) > 10 else None
    out_ref, *refs = (refs[3:5], *refs[5:-2]) if last else refs
    unproject_body(
        row, which, spot_ref, norm_ref, grads_ref, hidden_ref, grad_middle_ref, array, last, out_ref, *refs
    )


def unproject_body(
    row,
    which,
    spot_ref,
    norm_ref,
    grads_ref,
    hidden_ref,
    grad_middle_ref,
    array,
    last,
    out_ref,
    grads,
    hidden,
    grad_middle,
    out,
    total,
    weights,
    semaphores,
    load_semaphores,
    store_semaphores,
):
    copy = pltpu.make_async_copy
    tiles = row_tiles(D, UNPROJECT)
    if last:
        kept_ref, received_ref, outputs_ref, rows_of_two, last_semaphores = last
        get_others = [
            copy(received_ref.at[0], rows_of_two.at[0], last_semaphores.at[0]),
            copy(kept_ref.at[0], rows_of_two.at[1], last_semaphores.at[1]),
        ]
        put_others = copy(rows_of_two, outputs_ref, last_semaphores.at[2])

    get_weights = [load_qkv(array, row, part, weights, semaphores) for part in range(3)]
    get_grads = [
        copy(grads_ref.at[part], grads.at[part], load_semaphores.at[0, part]) for part in range(3)
    ]
    get_hidden = copy(hidden_ref.at[spot_ref[which]], hidden, load_semaphores.at[1, 0])
    get_grad_middle = copy(grad_middle_ref, grad_middle, load_semaphores.at[1, 1])

    def start_part(part):
        get_weights[part].start()
        get_grads[part].start()

    start_part(0)
    stores = []
    gain = norm_ref[0:1]

    def finish(index, rows):
        for part in chunks(rows):
            back = norm_back(hidden[part].astype(F32), gain, total[part])
            out[part] = (grad_middle[part].astype(F32) + back).astype(BF16)
        if last:
            piece, start = divmod(rows.start, D // 2)
            target = out_ref[piece].at[0, start : start + UNPROJECT]
        else:
            target = out_ref.at[0, rows]
        stores.append(copy(out.at[rows], target, store_semaphores.at[index]))
        if last:
            pl.when(spot_ref[0] != 0)(stores[-1].start)
            straight = copy(out.at[rows], outputs_ref.at[0, rows], store_semaphores.at[index])
            pl.when(spot_ref[0] == 0)(straight.start)
        else:
            stores[-1].start()

    for part in range(3):
        get_weights[part].wait()
        get_grads[part].wait()
        if part < 2:
            start_part(part + 1)
        if part == 1:
            get_hidden.start()
            get_grad_middle.start()
        if part == 2:
            get_hidden.wait()
            get_grad_middle.wait()
        if part == 2 and last:

            @pl.when(spot_ref[0] != 0)
            def _():
                for other in get_others:
                    other.start()

        for index, rows in enumerate(tiles):
            term = dot_nt(get_pairs(grads, rows, part), matrix(weights, part))
            total[rows] = term if part == 0 else total[rows] + term
            if part == 2 and index:
                finish(index - 1, tiles[index - 1])
            if part == 2 and last and index == len(tiles) - 1:

                @pl.when(spot_ref[0] != 0)
                def _():
                    for other in get_others:
                        other.wait()
                    put_others.start()

    finish(len(tiles) - 1, tiles[-1])
    for store in stores:
        store.wait()
    if last:
        pl.when(spot_ref[0] != 0)(put_others.wait)


def unproject(spot, which, grads, hidden, grad_middle, norms, place, others=()):
    length = hidden.shape[1]
    count = D // UNPROJECT
    row = jax.ShapeDtypeStruct((1, length, D), BF16)
    piece = jax.ShapeDtypeStruct((1, length // 2, D), BF16)
    return pl.pallas_call(
        functools.partial(unproject_kernel, place[1], which),
        in_specs=[SCALARS, IN_VMEM] + [ANY] * (4 + len(others)),
        out_specs=[ANY] * 3 if others else ANY,
        scratch_shapes=[
            pltpu.VMEM((3, PAIRS, D, PAIR_DIM), BF16),
            whole_scratch(BF16),
            whole_scratch(BF16),
            whole_scratch(BF16),
            whole_scratch(F32),
            across_scratch(3),
            pltpu.SemaphoreType.DMA((3,)),
            pltpu.SemaphoreType.DMA((2, 3)),
            pltpu.SemaphoreType.DMA((count,)),
        ]
        + ([pltpu.VMEM((2, D, D), BF16), pltpu.SemaphoreType.DMA((3,))] if others else []),
        out_shape=[jax.ShapeDtypeStruct((2, length, D), BF16), piece, piece] if others else row,
        compiler_params=params(44),
        cost_estimate=cost(11),
        name="unproject",
    )(spot, norms, grads, hidden, grad_middle, place[0], *others)


def three_terms(values):
    high = values.astype(BF16)
    rest = values - high.astype(F32)
    middle = rest.astype(BF16)
    return high, middle, (rest - middle.astype(F32)).astype(BF16)


def exact_nt(values, right):
    count = values.shape[0]
    product = dot_nt(jnp.concatenate(three_terms(values), axis=0), right)
    return (product[2 * count :] + product[count : 2 * count]) + product[:count]


def exact_tn(left, right):
    high, middle, low = three_terms(left)
    first, second, third = three_terms(right)
    return dot_tn(
        jnp.concatenate([low, middle, high, middle, high, high], axis=0),
        jnp.concatenate([first, second, third, first, second, first], axis=0),
    )


def joined(ref):
    return jnp.concatenate(
        [
            ref[pair, part * PREFIX : (part + 1) * PREFIX]
            for part in range(2)
            for pair in range(PAIRS)
        ],
        axis=1,
    )


def hidden_kernel(total_ref, w2_ref, out_ref, total):
    total[...] = jnp.zeros_like(total)
    total[:PREFIX] = joined(total_ref)
    out_ref[...] = exact_nt(total[...], w2_ref[0])


def hidden_back(total, w2):
    return pl.pallas_call(
        hidden_kernel,
        in_specs=[IN_VMEM] * 2,
        out_specs=IN_VMEM,
        scratch_shapes=[pltpu.VMEM((SLOTS, 2 * D), F32)],
        out_shape=jax.ShapeDtypeStruct((SLOTS, w2.shape[1]), F32),
        compiler_params=params(16),
        cost_estimate=cost(2),
        name="hidden_back",
    )(total, w2)


def slots(ref, scratch):
    scratch[...] = jnp.zeros_like(scratch)
    scratch[:PREFIX] = ref[...].astype(F32)
    return scratch[...]


def second_kernel(total_ref, hidden_ref, w2_out, b2_out, total, hidden):
    total[...] = jnp.zeros_like(total)
    total[:PREFIX] = joined(total_ref)
    units = slots(hidden_ref, hidden)
    for columns in row_tiles(2 * D, 512):
        w2_out[0, :, columns] = exact_tn(units, total[:, columns])
    b2_out[...] = jnp.sum(total[...], axis=0, keepdims=True)


def second_back(total, hidden):
    rh = hidden.shape[1]
    return pl.pallas_call(
        second_kernel,
        in_specs=[IN_VMEM] * 2,
        out_specs=[IN_VMEM] * 2,
        scratch_shapes=[pltpu.VMEM((SLOTS, 2 * D), F32), pltpu.VMEM((SLOTS, rh), F32)],
        out_shape=[
            jax.ShapeDtypeStruct((1, rh, 2 * D), F32),
            jax.ShapeDtypeStruct((1, 2 * D), F32),
        ],
        compiler_params=params(16),
        cost_estimate=cost(3),
        name="second_back",
    )(total, hidden)


def last_kernel(
    spot_ref,
    own_ref,
    other_ref,
    hidden_ref,
    table_ref,
    w1_ref,
    outputs_in,
    top_ref,
    bottom_ref,
    table_out,
    w1_out,
    b1_out,
    outputs_ref,
    hidden,
    table,
    buffer,
    semaphores,
):
    del outputs_in
    half = D // 2
    pieces = [(top_ref, slice(0, half)), (bottom_ref, slice(half, D))]
    loads = [
        pltpu.make_async_copy(piece.at[0], buffer.at[rows], semaphores.at[0, index])
        for index, (piece, rows) in enumerate(pieces)
    ]
    stores = [
        pltpu.make_async_copy(buffer.at[rows], outputs_ref.at[1, rows], semaphores.at[1, index])
        for index, (_, rows) in enumerate(pieces)
    ]

    @pl.when(spot_ref[0] == 0)
    def _():
        for load in loads:
            load.start()

    units = slots(hidden_ref, hidden)
    grad_pre = (own_ref[...] + other_ref[...]) * (1.0 - units * units)
    b1_out[...] = jnp.sum(grad_pre, axis=0, keepdims=True)
    table_out[...] = exact_nt(grad_pre, w1_ref[...])[:PREFIX]

    @pl.when(spot_ref[0] == 0)
    def _():
        for load, store in zip(loads, stores):
            load.wait()
            store.start()

    w1_out[...] = exact_tn(slots(table_ref, table), grad_pre)

    @pl.when(spot_ref[0] == 0)
    def _():
        for store in stores:
            store.wait()


def last_block(spot, own, other, hidden, table, w1, outputs, pieces):
    rh = w1.shape[1]
    return pl.pallas_call(
        last_kernel,
        in_specs=[SCALARS] + [IN_VMEM] * 5 + [ANY] * 3,
        out_specs=[IN_VMEM] * 3 + [ANY],
        scratch_shapes=[
            pltpu.VMEM((SLOTS, rh), F32),
            pltpu.VMEM((SLOTS, D), F32),
            whole_scratch(BF16),
            pltpu.SemaphoreType.DMA((2, 2)),
        ],
        out_shape=[
            jax.ShapeDtypeStruct((PREFIX, D), F32),
            jax.ShapeDtypeStruct(w1.shape, F32),
            jax.ShapeDtypeStruct((1, rh), F32),
            jax.ShapeDtypeStruct(outputs.shape, outputs.dtype),
        ],
        input_output_aliases={6: 3},
        compiler_params=params(16),
        cost_estimate=cost(3),
        name="last_block",
    )(spot, own, other, hidden, table, w1, outputs, *pieces)


def swap_sections(values):
    return lax.ppermute(values, "section", [(0, 1), (1, 0)])


def per_section(section_index, own):
    other = swap_sections(own)
    is_first = section_index == 0
    return jnp.where(is_first, own, other), jnp.where(is_first, other, own)


def halves(w_qkv, w_out, w_fc, w_proj):
    columns = lambda matrix: jnp.moveaxis(matrix.reshape(SHARD_ROWS, -1, D), 1, 0)
    attention = jnp.concatenate([columns(w_qkv), w_out[None]], axis=0).reshape(2, HALF, D)
    up = columns(w_fc).reshape(2, HALF, D)
    down = w_proj.reshape(2, HALF, D)
    return jnp.stack([attention, up, down], axis=1)


def gather_weights(is_first, w_qkv, w_out, w_fc, w_proj):
    if D // w_qkv.shape[1] == SHARDS:
        own = halves(w_qkv[0], w_out[0], w_fc[0], w_proj[0])
        received = swap_sections(jnp.where(is_first, own[1], own[0]))
        first = jnp.where(is_first, own[0], received)
        last = jnp.where(is_first, received, own[1])
        early = jnp.concatenate([first.reshape(3 * HALF, D), last[0]], axis=0)
        gather = lambda rows: lax.all_gather(rows, ("dp", "section"), axis=0).reshape(
            SHARDS, 2, -1, D
        )
        early, late = gather(early), gather(last[1:].reshape(2 * HALF, D))
    else:
        whole = lambda matrix: lax.all_gather(matrix[0], ("dp", "section"), axis=0)
        every = [whole(matrix) for matrix in (w_qkv, w_out, w_fc, w_proj)]
        layers = []
        for layer in range(2):
            mine = [matrix[layer::2] for matrix in every]
            shards = [matrix.reshape(SHARDS, -1, matrix.shape[-1]) for matrix in mine]
            layers.append(jax.vmap(halves)(*shards).reshape(SHARDS, 2, 3 * HALF, D))
        early = jnp.concatenate([layers[0], layers[1][:, :, :HALF]], axis=2)
        late = layers[1][:, :, HALF:]
    return (
        [(early, 0), (early, HALF), (early, 2 * HALF)],
        [(early, 3 * HALF), (late, 0), (late, HALF)],
    )


def reparam_hidden(table, w_first, b_first):
    return jnp.tanh(jnp.dot(table, w_first, precision=highest_mode) + b_first)


def reparam_out(hidden_units, w_second, b_second):
    return jnp.dot(hidden_units, w_second, precision=highest_mode) + b_second


def sum_dp(values):
    count = lax.axis_size("dp")
    moved = lambda bits: lax.ppermute(values, "dp", [(i, i ^ bits) for i in range(count)])
    step = count
    while step > 1:
        if step % 4 == 0:
            step //= 4
            values = (values + moved(step)) + (moved(2 * step) + moved(3 * step))
        else:
            step //= 2
            values = values + moved(step)
    return values


def per_device(
    tokens,
    seq_length,
    cotangent,
    ln_gain,
    ln_bias,
    w_qkv,
    w_out,
    w_fc,
    w_proj,
    prefix_table,
    reparam_w1,
    reparam_b1,
    reparam_w2,
    reparam_b2,
):
    section_index = lax.axis_index("section")
    is_first = section_index == 0
    first, last = gather_weights(is_first, w_qkv, w_out, w_fc, w_proj)
    spot = jnp.stack([section_index, jnp.zeros_like(section_index)]).astype(jnp.int32)
    seq = lax.dynamic_slice_in_dim(seq_length, section_index, 1, 0)

    table_values = prefix_table.astype(F32)
    first_weight = reparam_w1.astype(F32)
    first_bias = reparam_b1.astype(F32)
    second_weight = reparam_w2[0].astype(F32)
    second_bias = reparam_b2[0].astype(F32)
    hidden_units = reparam_hidden(table_values, first_weight, first_bias)
    prefix_kv = reparam_out(hidden_units, second_weight, second_bias).astype(BF16)
    pad = ((0, SLOTS - PREFIX), (0, 0))
    small = jnp.concatenate(
        [
            jnp.pad(prefix_kv[:, :D], pad),
            jnp.pad(prefix_kv[:, D:], pad),
            ln_gain[0],
            ln_bias[0],
            jnp.zeros((4, D), BF16),
        ],
        axis=0,
    )
    small_pair = per_section(section_index, small)
    pairs_apart = lambda rows: jnp.moveaxis(rows.reshape(SLOTS, PAIRS, PAIR_DIM), 1, 0)
    prefix_pair = [
        (pairs_apart(part[:SLOTS]), pairs_apart(part[SLOTS : 2 * SLOTS])) for part in small_pair
    ]
    norm_pair = [part[2 * SLOTS :].astype(F32) for part in small_pair]

    prefix_first, prefix_last = prefix_pair
    projected_first = project(spot, 0, tokens, norm_pair[0], first[0])
    attended_first, *probs_first = attend(seq, projected_first, *prefix_first)
    middle_first, normed = middle_block(spot, 0, attended_first, tokens, norm_pair[0], first[0])
    slope, handed = forward_block(normed, middle_first, *first[1:])
    projected = project(spot, 1, handed, norm_pair[1], last[0])
    attended, *probs = attend(seq, projected, *prefix_last)
    middle, normed = middle_block(spot, 1, attended, handed, norm_pair[1], last[0])
    final, sent, grad_middle, grad_attended = turn_block(
        spot, normed, middle, cotangent, handed, norm_pair[1], *last
    )
    received = swap_sections(sent)
    grads, prefix_grad_last = attend_back(
        seq, projected, attended, grad_attended, *prefix_last, *probs
    )
    grad_handed = unproject(spot, 1, grads, handed, grad_middle, norm_pair[1], last[0])
    received_grad = lax.ppermute(grad_handed, "section", [(0, 1)])
    activations, grad_middle, grad_attended = backward_block(
        spot, grad_handed, slope, middle_first, (handed, final, received), norm_pair[0], *first
    )
    grads, prefix_grad_first = attend_back(
        seq,
        projected_first,
        attended_first,
        grad_attended,
        *prefix_first,
        *probs_first,
    )
    input_grads, *pieces = unproject(
        spot,
        0,
        grads,
        tokens,
        grad_middle,
        norm_pair[0],
        first[0],
        (grad_handed, received_grad),
    )
    pieces = [lax.ppermute(piece, "section", [(1, 0)]) for piece in pieces]

    kept = jnp.where(is_first, prefix_grad_first, prefix_grad_last)
    sent = jnp.where(is_first, prefix_grad_last, prefix_grad_first)
    total = sum_dp(kept + swap_sections(sent))
    grad_hidden = hidden_back(total, reparam_w2)
    grad_w2, grad_b2 = second_back(total, hidden_units)
    grad_table, grad_w1, grad_b1, input_grads = last_block(
        spot,
        grad_hidden,
        swap_sections(grad_hidden),
        hidden_units,
        prefix_table,
        reparam_w1,
        input_grads,
        pieces,
    )
    return (
        activations[None],
        input_grads[None],
        grad_table,
        grad_w1,
        grad_b1[0],
        grad_w2,
        grad_b2,
    )


def solution(mesh):
    in_specs = (
        P("dp", None, None),
        P("dp"),
        P("dp", None, None),
        P("section", None, None),
        P("section", None, None),
        P("section", "dp", None),
        P("section", "dp", None),
        P("section", "dp", None),
        P("section", "dp", None),
        P(),
        P(),
        P(),
        P("section", None, None),
        P("section", None),
    )
    out_specs = (
        P("section", "dp", None, None),
        P("section", "dp", None, None),
        P(),
        P(),
        P(),
        P("section", None, None),
        P("section", None),
    )
    return jax.shard_map(
        per_device, mesh=mesh, in_specs=in_specs, out_specs=out_specs, check_vma=False
    )
```
